32 devices in a mesh: space: 8 (over y, x, core), tm: 2 (over z_hi), op: 2 (over z_lo).
Axes of the slice: x: 2, y: 2, z: 4 (z_hi: 2, z_lo: 2; z = z_hi * 2 + z_lo), core: 2. Of those that a mesh axis runs over, the one named last changes fastest.
Arguments:
- eigvecs: bfloat16 [2, 2, 256, 3, 16, 256], P('tm', None, None, None, 'space'), may hold values from -6 to 6
- links: float32 [2, 3, 3, 3, 2, 16, 256], P('tm', None, None, None, None, 'space'), may hold values from -2.5 to 2.5
- momenta: int32 [4, 3], P('op'), may hold values from -2 to 2
- coef_num: int32 [4, 4, 3], P(None, 'op'), may hold values from -3 to 3
- coef_den: int32 [4], replicated, may hold values from 1 to 6
- peram: bfloat16 [2, 256, 4, 4, 2, 256], P('tm'), may hold values from -0.25 to 0.25
Outputs:
- quark_lines: float32 [2, 4, 4, 4, 2, 256, 256], P('tm', 'op', None, None, None, 'space')
The draws below stay inside these ranges and needn't reach their ends.
All inputs are finite; a program needn't handle non-finite values.
Results may differ from the reference program's by a relative error of at most 0.0053.
Values may be sent and summed in bfloat16 or wider, within the bound.
No kernel may reach another device: no remote copies, remote signals or barrier semaphores. Data moves between devices by JAX's collectives and lax.ppermute only.
A program may use at most 128 MiB of HBM per device.

```python
import math
import jax
import jax.numpy as jnp
from jax import lax

NV = 256
LY = 32
LZ = 8
NMOM = 4
NDIR = 3
HEL = 4
NX = 16
PLANE = 256
NT = 2


def place_ends(drawn, rng, least, largest):
    longest = drawn.shape.index(max(drawn.shape))
    spots = []
    for shift in (0, 1):
        where = [jax.random.randint(jax.random.fold_in(rng, axis), (), 0, length) for axis, length in enumerate(drawn.shape)]
        where[longest] = (where[longest] + shift) % drawn.shape[longest]
        spots.append(tuple(where))
    return drawn.at[spots[0]].set(least).at[spots[1]].set(largest)


def level_of(own_key, extent, cuts, low, top_value):
    level, own = 1.0, jax.random.fold_in(own_key, 6)
    for position, blocks in cuts:
        heights = jnp.exp(jax.random.uniform(jax.random.fold_in(own, position), (blocks,), jnp.float32, low / len(cuts), top_value / len(cuts)))
        level = level * jnp.repeat(heights, extent[position] // blocks).reshape([-1 if axis == position else 1 for axis in range(len(extent))])
    return level


def centred(stream_key, extent, spread, limit, cuts=(), kind=jnp.bfloat16):
    loudness = level_of(stream_key, extent, cuts, -0.22, 0.18) if cuts else 1.0
    array = jax.random.normal(stream_key, extent, jnp.float32) * spread * loudness
    return jnp.minimum(jnp.maximum(array, -limit), limit).astype(kind)


def setup_inputs(seed: int = 0) -> dict:
    seeds = jax.random.split(jax.random.key(seed), 7)
    return {
        "eigvecs": centred(seeds[0], (NT, 2, NV, 3, NX, PLANE), 1.0, 6.0, ((0, 2), (4, 8))),
        "links": centred(seeds[1], (NT, NDIR, 3, 3, 2, NX, PLANE), 6 ** -0.5, 2.5, ((0, 2), (5, 8)), jnp.float32),
        "momenta": place_ends(jax.random.randint(seeds[2], (NMOM, 3), -2, 3), jax.random.fold_in(seeds[2], 1), -2, 2).astype(jnp.int32),
        "coef_num": place_ends(jax.random.randint(seeds[3], (HEL, NMOM, NDIR), -3, 4), jax.random.fold_in(seeds[3], 1), -3, 3).astype(jnp.int32),
        "coef_den": place_ends(jax.random.randint(seeds[4], (HEL,), 1, 7), jax.random.fold_in(seeds[4], 1), 1, 6).astype(jnp.int32),
        "peram": centred(seeds[5], (NT, NV, 4, 4, 2, NV), (2 * NV) ** -0.5, 0.25, ((0, 2),)),
    }


def colour(link, field, dagger):
    reals = []
    imags = []
    for col in range(3):
        acc_r = None
        acc_i = None
        for col_two in range(3):
            if dagger:
                link_r = link[col_two, col, 0]
                link_i = -link[col_two, col, 1]
            else:
                link_r = link[col, col_two, 0]
                link_i = link[col, col_two, 1]
            field_r = field[0, :, col_two].astype(jnp.float32)
            field_i = field[1, :, col_two].astype(jnp.float32)
            term_r = link_r * field_r - link_i * field_i
            term_i = link_r * field_i + link_i * field_r
            acc_r = term_r if acc_r is None else acc_r + term_r
            acc_i = term_i if acc_i is None else acc_i + term_i
        reals.append(acc_r)
        imags.append(acc_i)
    return jnp.stack([jnp.stack(reals, 1), jnp.stack(imags, 1)], 0)

def roll_plane(arr, by, axis):
    shape = arr.shape
    grid = arr.reshape(shape[:-1] + (LY, LZ))
    return jnp.roll(grid, by, axis=axis).reshape(shape)

def angles(mom, coord_x, n_x):
    yy = jnp.arange(LY, dtype=jnp.int32)
    zz = jnp.arange(LZ, dtype=jnp.int32)
    part_x = (mom[0] * coord_x % n_x).astype(jnp.float32) / n_x
    part_y = (mom[1] * yy % LY).astype(jnp.float32) / LY
    part_z = (mom[2] * zz % LZ).astype(jnp.float32) / LZ
    total = part_x[:, None, None] + part_y[None, :, None] + part_z[None, None, :]
    return (2.0 * math.pi * total).reshape(coord_x.shape[0], LY * LZ)

def left_operand(vec, theta):
    cosine = jnp.cos(theta)
    sine = jnp.sin(theta)
    vec_r = vec[0].astype(jnp.float32)
    vec_i = vec[1].astype(jnp.float32)
    left_r = cosine * vec_r - sine * vec_i
    left_i = -(sine * vec_r + cosine * vec_i)
    return jnp.stack([left_r, left_i], 0).astype(jnp.bfloat16)

def contract(left, right_mat, count):
    depth = right_mat.shape[1]
    mat = left.reshape(2 * count, depth)
    prod = lax.dot_general(mat, right_mat, (((1,), (1,)), ((), ())), preferred_element_type=jnp.float32)
    prod = prod.reshape(2, count, NDIR, 2, -1)
    real = prod[0, :, :, 0] - prod[1, :, :, 1]
    imag = prod[0, :, :, 1] + prod[1, :, :, 0]
    return jnp.stack([real, imag], 2)

def quark(ops_b, tau):
    hel_n, _, rows_n, cols_n = ops_b.shape
    left = ops_b.reshape(hel_n * 2 * rows_n, cols_n)
    right = tau.reshape(cols_n, -1)
    out = jnp.dot(left, right, preferred_element_type=jnp.float32)
    out = out.reshape(hel_n, 2, rows_n, 4, 4, 2, -1)
    real = out[:, 0, :, :, :, 0] - out[:, 1, :, :, :, 1]
    imag = out[:, 0, :, :, :, 1] + out[:, 1, :, :, :, 0]
    res = jnp.stack([real, imag], 4)
    return jnp.transpose(res, (0, 2, 3, 4, 1, 5))

def reference(eigvecs, links, momenta, coef_num, coef_den, peram):
    scale = 1.0 / math.sqrt(3.0 * NX * LY * LZ)
    weights = coef_num.astype(jnp.float32) / coef_den.astype(jnp.float32)[:, None, None]
    coord_x = jnp.arange(NX, dtype=jnp.int32)
    results = []
    for tslice in range(NT):
        vec = eigvecs[tslice]
        displaced = []
        for direc in range(NDIR):
            link = links[tslice, direc]
            back = colour(link, vec, True).astype(jnp.bfloat16)
            if direc == 0:
                vec_plus = jnp.roll(vec, -1, axis=3)
                back_minus = jnp.roll(back, 1, axis=3)
            else:
                vec_plus = roll_plane(vec, -1, direc + 3)
                back_minus = roll_plane(back, 1, direc + 3)
            forward = colour(link, vec_plus, False)
            displaced.append((forward - back_minus.astype(jnp.float32)).astype(jnp.bfloat16))
        right_mat = jnp.stack(displaced, 0).reshape(NDIR * 2 * NV, -1)
        elems = []
        for mom_idx in range(NMOM):
            theta = angles(momenta[mom_idx], coord_x, NX)
            left = left_operand(vec, theta)
            elems.append(contract(left, right_mat, NV) * scale)
        phi = jnp.stack(elems, 1)
        ops = jnp.einsum('hpd,apdrb->hrab', weights, phi, precision=lax.Precision.HIGHEST)
        ops_b = ops.astype(jnp.bfloat16)
        results.append(quark(ops_b, peram[1 - tslice]))
    return jnp.stack(results, 0)
```

```python
import functools
import math

import jax
import jax.numpy as jnp
from jax import lax
from jax.experimental import pallas as pl
from jax.experimental.pallas import tpu as pltpu
from jax.sharding import PartitionSpec as P

LY = 32
LZ = 8
NDIR = 3
SPINS = 16
ROWS = 16
HALF = 128


def from_behind(value, axis, steps):
    count = lax.axis_size(axis)
    pairs = [(source, (source + steps) % count) for source in range(count)]
    return lax.ppermute(value, axis, pairs)


def dot_nt(left, right):
    return lax.dot_general(
        left, right, (((1,), (1,)), ((), ())), preferred_element_type=jnp.float32
    )


def shift_y(arr):
    return pltpu.roll(arr, arr.shape[1] - LZ, 1)


def shift_z(arr):
    width = arr.shape[1]
    lane = lax.broadcasted_iota(jnp.int32, arr.shape, 1)
    near = pltpu.roll(arr, width - 1, 1)
    far = pltpu.roll(arr, LZ - 1, 1)
    return jnp.where((lane & (LZ - 1)) == LZ - 1, far, near)


def weighted_links(u_ref, phi_ref, shifted, dirs, plane, n_h, store):
    width = u_ref.shape[-1]
    for half in range(width // HALF):
        lanes = pl.ds(half * HALF, HALF)
        for col in range(3):
            acc = {}
            for slot, direc in enumerate(dirs):
                f_r = None
                f_i = None
                for col_two in range(3):
                    u_r = u_ref[direc, col, col_two, 0, pl.ds(plane, 1), lanes]
                    u_i = u_ref[direc, col, col_two, 1, pl.ds(plane, 1), lanes]
                    v_r = shifted[slot, 0, col_two, :, lanes]
                    v_i = shifted[slot, 1, col_two, :, lanes]
                    term_r = u_r * v_r - u_i * v_i
                    term_i = u_r * v_i + u_i * v_r
                    f_r = term_r if f_r is None else f_r + term_r
                    f_i = term_i if f_i is None else f_i + term_i
                for kind in range(2):
                    for hel in range(n_h):
                        p_r = phi_ref[kind, hel, direc, 0, pl.ds(plane, 1), lanes]
                        p_i = phi_ref[kind, hel, direc, 1, pl.ds(plane, 1), lanes]
                        g_r = p_r * f_r - p_i * f_i
                        g_i = p_r * f_i + p_i * f_r
                        if (kind, hel) in acc:
                            old_r, old_i = acc[kind, hel]
                            g_r, g_i = old_r + g_r, old_i + g_i
                        acc[kind, hel] = (g_r, g_i)
            for (kind, hel), both in acc.items():
                for part in range(2):
                    store(kind, hel, part, col, half, both[part].astype(jnp.bfloat16))


def products(mat, g_ref, h_ref, hel):
    n_b = mat.shape[0] // 2
    one = dot_nt(mat, g_ref[hel])
    two = dot_nt(h_ref[hel], mat)
    real = (one[:n_b, :n_b] + one[n_b:, n_b:]) - (two[:n_b, :n_b] + two[n_b:, n_b:])
    imag = (one[:n_b, n_b:] - one[n_b:, :n_b]) - (two[:n_b, n_b:] - two[n_b:, :n_b])
    return real, imag


def local_kernel(planes, v_ref, u_ref, phi_ref, out_ref, g_ref, h_ref, sh_ref):
    n_h, _, n_b, _ = out_ref.shape
    width = u_ref.shape[-1]
    kinds = (g_ref, h_ref)

    def block(step, carry):
        row = pl.multiple_of(step * ROWS, ROWS)
        rows = pl.ds(row, ROWS)
        for plane in range(planes):
            dirs = (1, 2, 0) if plane + 1 < planes else (1, 2)
            for part in range(2):
                for col in range(3):
                    start = (col * planes + plane) * width
                    here = pl.ds(pl.multiple_of(part * n_b + row, ROWS), ROWS)
                    field = v_ref[here, pl.ds(start, width)].astype(jnp.float32)
                    sh_ref[0, part, col] = shift_y(field)
                    sh_ref[1, part, col] = shift_z(field)
                    if plane + 1 < planes:
                        sh_ref[2, part, col] = v_ref[here, pl.ds(start + width, width)].astype(jnp.float32)

            def store(kind, hel, part, col, half, value, plane=plane):
                start = (col * planes + plane) * width + half * HALF
                there = pl.ds(pl.multiple_of(part * n_b + row, ROWS), ROWS)
                kinds[kind][hel, there, pl.ds(start, HALF)] = value

            weighted_links(u_ref, phi_ref, sh_ref, dirs, plane, n_h, store)
        return carry

    lax.fori_loop(0, n_b // ROWS, block, 0)

    def multiply(hel, carry):
        real, imag = products(v_ref[...], g_ref, h_ref, hel)
        out_ref[hel, 0] = real
        out_ref[hel, 1] = imag
        return carry

    lax.fori_loop(0, n_h, multiply, 0)


def halo_kernel(planes, v_ref, up_ref, u_ref, phi_ref, part_ref, out_ref, g_ref, h_ref, sh_ref):
    n_h, _, n_b, _ = part_ref.shape
    n_dev = out_ref.shape[0]
    own = n_b // n_dev
    width = u_ref.shape[-1]
    plane = planes - 1
    kinds = (g_ref, h_ref)

    def block(step, carry):
        row = pl.multiple_of(step * ROWS, ROWS)
        rows = pl.ds(row, ROWS)
        for part in range(2):
            for col in range(3):
                sh_ref[0, part, col] = up_ref[part, col, rows, :].astype(jnp.float32)

        def store(kind, hel, part, col, half, value):
            there = pl.ds(pl.multiple_of(part * n_b + row, ROWS), ROWS)
            kinds[kind][hel, there, pl.ds(col * width + half * HALF, HALF)] = value

        weighted_links(u_ref, phi_ref, sh_ref, (0,), plane, n_h, store)
        return carry

    lax.fori_loop(0, n_b // ROWS, block, 0)

    def multiply(hel, carry):
        mat = jnp.concatenate(
            [v_ref[:, pl.ds((col * planes + plane) * width, width)] for col in range(3)], 1
        )
        both = products(mat, g_ref, h_ref, hel)
        for part in range(2):
            total = (both[part] + part_ref[hel, part]).astype(jnp.bfloat16)
            out_ref[:, hel, part] = total.reshape(n_dev, own, n_b)
        return carry

    lax.fori_loop(0, n_h, multiply, 0)


def quark_kernel(got_ref, tau_ref, out_ref, left_ref):
    n_dev, n_h, _, own, n_b = got_ref.shape

    @pl.when(pl.program_id(0) == 0)
    def _():
        row = lax.broadcasted_iota(jnp.int32, (n_b, 2 * n_b), 0)
        col = lax.broadcasted_iota(jnp.int32, (n_b, 2 * n_b), 1)
        even = (col == 2 * row).astype(jnp.bfloat16)
        odd = (col == 2 * row + 1).astype(jnp.bfloat16)
        for hel in range(n_h):
            ops = []
            for part in range(2):
                total = got_ref[0, hel, part].astype(jnp.float32)
                for dev in range(1, n_dev):
                    total = total + got_ref[dev, hel, part].astype(jnp.float32)
                ops.append(total.astype(jnp.bfloat16))
            first = jnp.concatenate(ops, 0)
            second = jnp.concatenate([-ops[1], ops[0]], 0)
            left = jnp.dot(first, even, preferred_element_type=jnp.float32) + jnp.dot(
                second, odd, preferred_element_type=jnp.float32
            )
            left_ref[pl.ds(hel * 2 * own, 2 * own), :] = left.astype(jnp.bfloat16)

    res = jnp.dot(left_ref[...], tau_ref[0], preferred_element_type=jnp.float32)
    for hel in range(n_h):
        for part in range(2):
            start = (hel * 2 + part) * own
            out_ref[hel, 0, part] = res[start : start + own]


def phases(momenta, weights, coord_x, n_x):
    site = jnp.arange(LY * LZ, dtype=jnp.int32)
    yy = site // LZ
    zz = site % LZ
    step = jnp.concatenate([jnp.zeros((1, 3), jnp.int32), jnp.eye(3, dtype=jnp.int32)], 0)
    pos_x = coord_x[None, :, None] + step[:, 0, None, None]
    pos_y = yy[None, None, :] + step[:, 1, None, None]
    pos_z = zz[None, None, :] + step[:, 2, None, None]
    mom = momenta[:, :, None, None, None]
    part_x = (mom[:, 0] * pos_x % n_x).astype(jnp.float32) / n_x
    part_y = (mom[:, 1] * pos_y % LY).astype(jnp.float32) / LY
    part_z = (mom[:, 2] * pos_z % LZ).astype(jnp.float32) / LZ
    theta = 2.0 * math.pi * (part_x + part_y + part_z)
    wave = jnp.stack([jnp.cos(theta), -jnp.sin(theta)], 1)
    wts = weights[:, :, :, None, None, None]
    here = 0.0
    ahead = 0.0
    sign = jnp.array([1.0, -1.0], jnp.float32)[None, None, :, None, None]
    for k in range(momenta.shape[0]):
        here = here + wts[:, k] * wave[k, :, 0][None, None]
        ahead = ahead + wts[:, k] * jnp.swapaxes(wave[k, :, 1:], 0, 1)[None]
    return jnp.stack([here, ahead * sign], 0)


def shards(eigvecs, links, momenta, coef_num, coef_den, peram):
    n_space = lax.axis_size("space")
    n_op = lax.axis_size("op")
    n_tm = lax.axis_size("tm")
    _, _, n_b, _, planes, width = eigvecs.shape
    n_x = planes * n_space
    own = n_b // n_space
    n_h = coef_num.shape[0] // n_op
    my_op = lax.axis_index("op")
    my_space = lax.axis_index("space")

    group = n_space * n_op
    pairs = max(1, SPINS // group)
    depth = min(n_b, n_b * SPINS // group)
    first = (my_space * n_op + my_op) * (pairs * depth)
    piece = lax.dynamic_slice(
        peram.reshape(n_b, SPINS, 2, n_b),
        (first % n_b, first // n_b, 0, 0),
        (depth, pairs, 2, n_b),
    )
    piece = jnp.swapaxes(piece, 0, 1).reshape(pairs * depth * 2, n_b)
    piece = from_behind(piece, "tm", n_tm - 1)
    tau = lax.all_gather(piece, ("space", "op"), axis=0, tiled=True).reshape(SPINS, 2 * n_b, n_b)

    upper = jnp.transpose(eigvecs[0, :, :, :, 0, :], (0, 2, 1, 3))
    upper = from_behind(upper, "space", -1)

    small = jnp.concatenate([momenta.reshape(-1), coef_num.reshape(-1)])
    parts = [small] + [from_behind(small, "op", shift) for shift in range(1, n_op)]
    n_mom = momenta.shape[0]
    moms = jnp.concatenate([part[: n_mom * 3].reshape(n_mom, 3) for part in parts], 0)
    nums = jnp.concatenate(
        [part[n_mom * 3 :].reshape(coef_num.shape) for part in parts], 1
    )
    weights = nums.astype(jnp.float32) / coef_den.astype(jnp.float32)[:, None, None]
    scale = 1.0 / math.sqrt(3.0 * n_x * LY * LZ)
    weights = lax.dynamic_slice_in_dim(weights, my_op * n_h, n_h, 0) * scale
    coord_x = planes * my_space + jnp.arange(planes, dtype=jnp.int32)
    phi = phases(moms, weights, coord_x, n_x)

    mat = eigvecs.reshape(2 * n_b, 3 * planes * width)
    link = links[0]
    params = pltpu.CompilerParams(vmem_limit_bytes=48 * 2**20)
    depth_k = 3 * planes * width
    partial = pl.pallas_call(
        functools.partial(local_kernel, planes),
        out_shape=jax.ShapeDtypeStruct((n_h, 2, n_b, n_b), jnp.float32),
        scratch_shapes=[
            pltpu.VMEM((n_h, 2 * n_b, depth_k), jnp.bfloat16),
            pltpu.VMEM((n_h, 2 * n_b, depth_k), jnp.bfloat16),
            pltpu.VMEM((3, 2, 3, ROWS, width), jnp.float32),
        ],
        compiler_params=params,
        cost_estimate=pl.CostEstimate(
            flops=16 * n_h * n_b * n_b * depth_k, bytes_accessed=2**22, transcendentals=0
        ),
        name="local_sites",
    )(mat, link, phi)
    sums = pl.pallas_call(
        functools.partial(halo_kernel, planes),
        out_shape=jax.ShapeDtypeStruct((n_space, n_h, 2, own, n_b), jnp.bfloat16),
        scratch_shapes=[
            pltpu.VMEM((n_h, 2 * n_b, 3 * width), jnp.bfloat16),
            pltpu.VMEM((n_h, 2 * n_b, 3 * width), jnp.bfloat16),
            pltpu.VMEM((1, 2, 3, ROWS, width), jnp.float32),
        ],
        compiler_params=params,
        cost_estimate=pl.CostEstimate(
            flops=16 * n_h * n_b * n_b * 3 * width, bytes_accessed=2**22, transcendentals=0
        ),
        name="halo_plane",
    )(mat, upper, link, phi, partial)
    got = lax.all_to_all(sums, "space", 0, 0, tiled=True)

    lines = pl.pallas_call(
        quark_kernel,
        grid=(SPINS,),
        in_specs=[
            pl.BlockSpec((n_space, n_h, 2, own, n_b), lambda s: (0, 0, 0, 0, 0)),
            pl.BlockSpec((1, 2 * n_b, n_b), lambda s: (s, 0, 0)),
        ],
        out_specs=pl.BlockSpec((n_h, 1, 2, own, n_b), lambda s: (0, s, 0, 0, 0)),
        out_shape=jax.ShapeDtypeStruct((n_h, SPINS, 2, own, n_b), jnp.float32),
        scratch_shapes=[pltpu.VMEM((n_h * 2 * own, 2 * n_b), jnp.bfloat16)],
        compiler_params=params,
        cost_estimate=pl.CostEstimate(
            flops=2 * SPINS * n_h * 2 * own * 2 * n_b * n_b, bytes_accessed=7 * 2**20, transcendentals=0
        ),
        name="quark_products",
    )(got, tau)
    return lines.reshape(1, n_h, 4, 4, 2, own, n_b)


def solution(mesh):
    return jax.shard_map(
        shards,
        mesh=mesh,
        in_specs=(
            P("tm", None, None, None, "space", None),
            P("tm", None, None, None, None, "space", None),
            P("op", None),
            P(None, "op", None),
            P(),
            P("tm", None, None, None, None, None),
        ),
        out_specs=P("tm", "op", None, None, None, "space", None),
        check_vma=False,
    )
```

```python
import functools
import math

import jax
import jax.numpy as jnp
from jax import lax
from jax.experimental import pallas as pl
from jax.experimental.pallas import tpu as pltpu
from jax.sharding import PartitionSpec as P

LY = 32
LZ = 8
NDIR = 3
SPINS = 16
ROWS = 16
HALF = 128


def from_behind(value, axis, steps):
    count = lax.axis_size(axis)
    pairs = [(source, (source + steps) % count) for source in range(count)]
    return lax.ppermute(value, axis, pairs)


def across(value, axis, mask):
    pairs = [(source, source ^ mask) for source in range(lax.axis_size(axis))]
    return lax.ppermute(value, axis, pairs)


def dot_nt(left, right):
    return lax.dot_general(
        left, right, (((1,), (1,)), ((), ())), preferred_element_type=jnp.float32
    )


def shift_y(arr):
    return pltpu.roll(arr, arr.shape[1] - LZ, 1)


def shift_z(arr):
    width = arr.shape[1]
    lane = lax.broadcasted_iota(jnp.int32, arr.shape, 1)
    near = pltpu.roll(arr, width - 1, 1)
    far = pltpu.roll(arr, LZ - 1, 1)
    return jnp.where((lane & (LZ - 1)) == LZ - 1, far, near)


def weighted_links(u_ref, phi_ref, shifted, dirs, plane, n_h, store):
    width = u_ref.shape[-1]
    for half in range(width // HALF):
        lanes = pl.ds(half * HALF, HALF)
        for col in range(3):
            acc = {}
            for slot, direc in enumerate(dirs):
                f_r = None
                f_i = None
                for col_two in range(3):
                    u_r = u_ref[direc, col, col_two, 0, pl.ds(plane, 1), lanes]
                    u_i = u_ref[direc, col, col_two, 1, pl.ds(plane, 1), lanes]
                    v_r = shifted[slot, 0, col_two, :, lanes]
                    v_i = shifted[slot, 1, col_two, :, lanes]
                    term_r = u_r * v_r - u_i * v_i
                    term_i = u_r * v_i + u_i * v_r
                    f_r = term_r if f_r is None else f_r + term_r
                    f_i = term_i if f_i is None else f_i + term_i
                for kind in range(2):
                    for hel in range(n_h):
                        p_r = phi_ref[kind, hel, direc, 0, pl.ds(plane, 1), lanes]
                        p_i = phi_ref[kind, hel, direc, 1, pl.ds(plane, 1), lanes]
                        g_r = p_r * f_r - p_i * f_i
                        g_i = p_r * f_i + p_i * f_r
                        if (kind, hel) in acc:
                            old_r, old_i = acc[kind, hel]
                            g_r, g_i = old_r + g_r, old_i + g_i
                        acc[kind, hel] = (g_r, g_i)
            for (kind, hel), both in acc.items():
                for part in range(2):
                    store(kind, hel, part, col, half, both[part].astype(jnp.bfloat16))


def products(mat, g_ref, h_ref, hel):
    n_b = mat.shape[0] // 2
    one = dot_nt(mat, g_ref[hel])
    two = dot_nt(h_ref[hel], mat)
    real = (one[:n_b, :n_b] + one[n_b:, n_b:]) - (two[:n_b, :n_b] + two[n_b:, n_b:])
    imag = (one[:n_b, n_b:] - one[n_b:, :n_b]) - (two[:n_b, n_b:] - two[n_b:, :n_b])
    return real, imag


def plane_kernel(plane, dirs, has_part, n_out, *refs):
    refs = list(refs)
    v_ref = refs.pop(0)
    next_ref = refs.pop(0) if 0 in dirs else None
    u_ref, phi_ref = refs.pop(0), refs.pop(0)
    part_ref = refs.pop(0) if has_part else None
    where_ref = refs.pop(0) if n_out else None
    out_refs = [refs.pop(0) for _ in range(n_out or 1)]
    g_ref, h_ref, sh_ref = refs[:3]
    n_h = phi_ref.shape[1]
    _, _, n_b, width = v_ref.shape
    kinds = (g_ref, h_ref)

    def block(step, carry):
        row = pl.multiple_of(step * ROWS, ROWS)
        rows = pl.ds(row, ROWS)
        for slot, direc in enumerate(dirs):
            for part in range(2):
                for col in range(3):
                    if direc == 0:
                        sh_ref[slot, part, col] = next_ref[part, col, rows, :].astype(jnp.float32)
                    else:
                        field = v_ref[part, col, rows, :].astype(jnp.float32)
                        sh_ref[slot, part, col] = shift_y(field) if direc == 1 else shift_z(field)

        def store(kind, hel, part, col, half, value):
            there = pl.ds(pl.multiple_of(part * n_b + row, ROWS), ROWS)
            kinds[kind][hel, there, pl.ds(col * width + half * HALF, HALF)] = value

        weighted_links(u_ref, phi_ref, sh_ref, dirs, plane, n_h, store)
        return carry

    lax.fori_loop(0, n_b // ROWS, block, 0)

    def multiply(hel, carry):
        mat = jnp.concatenate([v_ref[:, col].reshape(2 * n_b, width) for col in range(3)], 1)
        both = products(mat, g_ref, h_ref, hel)
        for part in range(2):
            total = both[part] + part_ref[hel, part] if has_part else both[part]
            if n_out:
                refs[3][hel * 2 + part] = total
            else:
                out_refs[0][hel, part] = total
        return carry

    lax.fori_loop(0, n_h, multiply, 0)
    if n_out:
        own = n_b // n_out
        for mask in range(n_out):
            rows = pl.ds(pl.multiple_of((where_ref[0] ^ mask) * own, own), own)
            pieces = [refs[3][which, rows, :] for which in range(2 * n_h)]
            out_refs[mask][...] = jnp.concatenate(pieces, 0).astype(jnp.bfloat16)


def plane_call(plane, dirs, vec, ahead, link, phi, part=None, where=None, n_out=0):
    n_h = phi.shape[1]
    _, _, n_b, width = vec.shape
    vmem = pl.BlockSpec(memory_space=pltpu.VMEM)
    args = [vec] + ([ahead] if 0 in dirs else []) + [link, phi]
    args += [part] if part is not None else []
    specs = [vmem] * len(args)
    scratch = [
        pltpu.VMEM((n_h, 2 * n_b, 3 * width), jnp.bfloat16),
        pltpu.VMEM((n_h, 2 * n_b, 3 * width), jnp.bfloat16),
        pltpu.VMEM((len(dirs), 2, 3, ROWS, width), jnp.float32),
    ]
    if n_out:
        args.append(where)
        specs.append(pl.BlockSpec(memory_space=pltpu.SMEM))
        scratch.append(pltpu.VMEM((2 * n_h, n_b, n_b), jnp.float32))
        shape = jax.ShapeDtypeStruct((2 * n_h * (n_b // n_out), n_b), jnp.bfloat16)
        out_shape = [shape] * n_out
        out_specs = [vmem] * n_out
    else:
        out_shape = jax.ShapeDtypeStruct((n_h, 2, n_b, n_b), jnp.float32)
        out_specs = vmem
    return pl.pallas_call(
        functools.partial(plane_kernel, plane, dirs, part is not None, n_out),
        in_specs=specs,
        out_specs=out_specs,
        out_shape=out_shape,
        scratch_shapes=scratch,
        compiler_params=pltpu.CompilerParams(vmem_limit_bytes=40 * 2**20),
        cost_estimate=pl.CostEstimate(
            flops=(16 + 8 * len(dirs)) * n_h * n_b * n_b * 3 * width,
            bytes_accessed=2**22,
            transcendentals=0,
        ),
        name="plane%d_%s" % (plane, "".join(str(direc) for direc in dirs)),
    )(*args)


def quark_kernel(n_got, n_tau, where_ref, *refs):
    got_refs = refs[:n_got]
    tau_refs = refs[n_got : n_got + n_tau]
    out_ref, left_ref = refs[n_got + n_tau :]
    n_h, n_pair, _, own, n_b = out_ref.shape
    row = lax.broadcasted_iota(jnp.int32, (n_b, 2 * n_b), 0)
    col = lax.broadcasted_iota(jnp.int32, (n_b, 2 * n_b), 1)
    even = (col == 2 * row).astype(jnp.bfloat16)
    odd = (col == 2 * row + 1).astype(jnp.bfloat16)
    total = got_refs[0][...].astype(jnp.float32)
    for ref in got_refs[1:]:
        total = total + ref[...].astype(jnp.float32)
    swap = []
    for hel in range(n_h):
        start = hel * 2 * own
        swap += [-total[start + own : start + 2 * own], total[start : start + own]]
    left = jnp.dot(total.astype(jnp.bfloat16), even, preferred_element_type=jnp.float32)
    left += jnp.dot(
        jnp.concatenate(swap, 0).astype(jnp.bfloat16), odd, preferred_element_type=jnp.float32
    )
    left_ref[...] = left.astype(jnp.bfloat16)
    depth = tau_refs[0].shape[0]
    whole = depth == 2 * n_b
    if not whole:
        out_ref[...] = jnp.zeros_like(out_ref)
    for which in range(n_tau):
        first = where_ref[which] * depth
        pair = first // (2 * n_b)
        if whole:
            lhs = left_ref[...]
        else:
            lhs = left_ref[:, pl.ds(pl.multiple_of(first - pair * 2 * n_b, depth), depth)]
        res = jnp.dot(lhs, tau_refs[which][...], preferred_element_type=jnp.float32)
        for hel in range(n_h):
            for part in range(2):
                start = (hel * 2 + part) * own
                if whole:
                    out_ref[hel, pair, part] = res[start : start + own]
                else:
                    out_ref[hel, pair, part] += res[start : start + own]


def phases(momenta, weights, coord_x, n_x):
    site = jnp.arange(LY * LZ, dtype=jnp.int32)
    yy = site // LZ
    zz = site % LZ
    step = jnp.concatenate([jnp.zeros((1, 3), jnp.int32), jnp.eye(3, dtype=jnp.int32)], 0)
    pos_x = coord_x[None, :, None] + step[:, 0, None, None]
    pos_y = yy[None, None, :] + step[:, 1, None, None]
    pos_z = zz[None, None, :] + step[:, 2, None, None]
    mom = momenta[:, :, None, None, None]
    part_x = (mom[:, 0] * pos_x % n_x).astype(jnp.float32) / n_x
    part_y = (mom[:, 1] * pos_y % LY).astype(jnp.float32) / LY
    part_z = (mom[:, 2] * pos_z % LZ).astype(jnp.float32) / LZ
    theta = 2.0 * math.pi * (part_x + part_y + part_z)
    wave = jnp.stack([jnp.cos(theta), -jnp.sin(theta)], 1)
    wts = weights[:, :, :, None, None, None]
    here = 0.0
    ahead = 0.0
    sign = jnp.array([1.0, -1.0], jnp.float32)[None, None, :, None, None]
    for k in range(momenta.shape[0]):
        here = here + wts[:, k] * wave[k, :, 0][None, None]
        ahead = ahead + wts[:, k] * jnp.swapaxes(wave[k, :, 1:], 0, 1)[None]
    return jnp.stack([here, ahead * sign], 0)


def shards(eigvecs, links, momenta, coef_num, coef_den, peram):
    n_space = lax.axis_size("space")
    n_op = lax.axis_size("op")
    n_tm = lax.axis_size("tm")
    _, _, n_b, _, planes, width = eigvecs.shape
    n_x = planes * n_space
    own = n_b // n_space
    n_h = coef_num.shape[0] // n_op
    my_op = lax.axis_index("op")
    my_space = lax.axis_index("space")

    group = n_space * n_op
    depth = n_b * SPINS // group
    first = (my_space * n_op + my_op) * depth
    piece = lax.dynamic_slice(
        peram.reshape(n_b, SPINS, 2, n_b), (first % n_b, first // n_b, 0, 0), (depth, 1, 2, n_b)
    ).reshape(depth * 2, n_b)
    piece = from_behind(piece, "tm", n_tm - 1)

    vecs = [jnp.transpose(eigvecs[0, :, :, :, plane, :], (0, 2, 1, 3)) for plane in range(planes)]
    upper = from_behind(vecs[0], "space", -1)

    held = [(piece, my_space, my_op)]
    for mask in range(2, n_space, 2):
        held.append((across(piece, "space", mask), my_space ^ mask, my_op))
    for mask in range(1, n_op):
        held += [(across(arr, "op", mask), place, oper ^ mask) for arr, place, oper in held[: n_space // 2]]
    held += [(across(arr, "space", 1), place ^ 1, oper) for arr, place, oper in held]
    tau = [arr for arr, _, _ in held]
    tau_place = jnp.stack([place * n_op + oper for _, place, oper in held]).astype(jnp.int32)

    small = jnp.concatenate([momenta.reshape(-1), coef_num.reshape(-1)])
    parts = [small] + [from_behind(small, "op", shift) for shift in range(1, n_op)]
    n_mom = momenta.shape[0]
    moms = jnp.concatenate([part[: n_mom * 3].reshape(n_mom, 3) for part in parts], 0)
    nums = jnp.concatenate(
        [part[n_mom * 3 :].reshape(coef_num.shape) for part in parts], 1
    )
    weights = nums.astype(jnp.float32) / coef_den.astype(jnp.float32)[:, None, None]
    scale = 1.0 / math.sqrt(3.0 * n_x * LY * LZ)
    weights = lax.dynamic_slice_in_dim(weights, my_op * n_h, n_h, 0) * scale
    coord_x = planes * my_space + jnp.arange(planes, dtype=jnp.int32)
    phi = phases(moms, weights, coord_x, n_x)

    link = links[0]
    last = planes - 1
    partial = plane_call(last, (1, 2), vecs[last], None, link, phi)
    for plane in range(last):
        partial = plane_call(plane, (1, 2, 0), vecs[plane], vecs[plane + 1], link, phi, partial)
    where = my_space.astype(jnp.int32).reshape(1)
    sums = plane_call(last, (0,), vecs[last], upper, link, phi, partial, where, n_space)
    got = [sums[0]] + [across(sums[mask], "space", mask) for mask in range(1, n_space)]

    vmem = pl.BlockSpec(memory_space=pltpu.VMEM)
    lines = pl.pallas_call(
        functools.partial(quark_kernel, len(got), len(tau)),
        in_specs=[pl.BlockSpec(memory_space=pltpu.SMEM)] + [vmem] * (len(got) + len(tau)),
        out_specs=vmem,
        out_shape=jax.ShapeDtypeStruct((n_h, SPINS, 2, own, n_b), jnp.float32),
        scratch_shapes=[pltpu.VMEM((n_h * 2 * own, 2 * n_b), jnp.bfloat16)],
        compiler_params=pltpu.CompilerParams(vmem_limit_bytes=40 * 2**20),
        cost_estimate=pl.CostEstimate(
            flops=2 * SPINS * n_h * 2 * own * 2 * n_b * n_b, bytes_accessed=7 * 2**20, transcendentals=0
        ),
        name="quark_products",
    )(tau_place, *got, *tau)
    return lines.reshape(1, n_h, 4, 4, 2, own, n_b)


def solution(mesh):
    return jax.shard_map(
        shards,
        mesh=mesh,
        in_specs=(
            P("tm", None, None, None, "space", None),
            P("tm", None, None, None, None, "space", None),
            P("op", None),
            P(None, "op", None),
            P(),
            P("tm", None, None, None, None, None),
        ),
        out_specs=P("tm", "op", None, None, None, "space", None),
        check_vma=False,
    )
```

```python
import functools
import math

import jax
import jax.numpy as jnp
from jax import lax
from jax.experimental import pallas as pl
from jax.experimental.pallas import tpu as pltpu
from jax.sharding import PartitionSpec as P

LY = 32
LZ = 8
NDIR = 3
SPINS = 16
ROWS = 16
HALF = 128
VMEM_BYTES = 20 * 2**20


def from_behind(value, axis, steps):
    count = lax.axis_size(axis)
    pairs = [(source, (source + steps) % count) for source in range(count)]
    return lax.ppermute(value, axis, pairs)


def across(value, axis, mask):
    pairs = [(source, source ^ mask) for source in range(lax.axis_size(axis))]
    return lax.ppermute(value, axis, pairs)


def dot_nt(left, right):
    return lax.dot_general(
        left, right, (((1,), (1,)), ((), ())), preferred_element_type=jnp.float32
    )


def shift_y(arr):
    return pltpu.roll(arr, arr.shape[1] - LZ, 1)


def shift_z(arr):
    width = arr.shape[1]
    lane = lax.broadcasted_iota(jnp.int32, arr.shape, 1)
    near = pltpu.roll(arr, width - 1, 1)
    far = pltpu.roll(arr, LZ - 1, 1)
    return jnp.where((lane & (LZ - 1)) == LZ - 1, far, near)


def weighted_links(u_ref, phi_ref, shifted, dirs, plane, n_h, store):
    width = u_ref.shape[-1]
    for half in range(width // HALF):
        lanes = pl.ds(half * HALF, HALF)
        for col in range(3):
            acc = {}
            for slot, direc in enumerate(dirs):
                f_r = None
                f_i = None
                for col_two in range(3):
                    u_r = u_ref[direc, col, col_two, 0, pl.ds(plane, 1), lanes]
                    u_i = u_ref[direc, col, col_two, 1, pl.ds(plane, 1), lanes]
                    v_r = shifted[slot, 0, col_two, :, lanes]
                    v_i = shifted[slot, 1, col_two, :, lanes]
                    term_r = u_r * v_r - u_i * v_i
                    term_i = u_r * v_i + u_i * v_r
                    f_r = term_r if f_r is None else f_r + term_r
                    f_i = term_i if f_i is None else f_i + term_i
                for kind in range(2):
                    for hel in range(n_h):
                        p_r = phi_ref[kind, hel, direc, 0, pl.ds(plane, 1), lanes]
                        p_i = phi_ref[kind, hel, direc, 1, pl.ds(plane, 1), lanes]
                        g_r = p_r * f_r - p_i * f_i
                        g_i = p_r * f_i + p_i * f_r
                        if (kind, hel) in acc:
                            old_r, old_i = acc[kind, hel]
                            g_r, g_i = old_r + g_r, old_i + g_i
                        acc[kind, hel] = (g_r, g_i)
            for (kind, hel), both in acc.items():
                for part in range(2):
                    store(kind, hel, part, col, half, both[part].astype(jnp.bfloat16))


def products(mat, g_ref, h_ref, hel):
    n_b = mat.shape[0] // 2
    one = dot_nt(mat, g_ref[hel])
    two = dot_nt(h_ref[hel], mat)
    real = (one[:n_b, :n_b] + one[n_b:, n_b:]) - (two[:n_b, :n_b] + two[n_b:, n_b:])
    imag = (one[:n_b, n_b:] - one[n_b:, :n_b]) - (two[:n_b, n_b:] - two[n_b:, :n_b])
    return real, imag


def plane_kernel(plane, dirs, has_part, n_out, *refs):
    refs = list(refs)
    v_ref = refs.pop(0)
    next_ref = refs.pop(0) if 0 in dirs else None
    u_ref, phi_ref = refs.pop(0), refs.pop(0)
    part_ref = refs.pop(0) if has_part else None
    out_ref = refs.pop(0)
    g_ref, h_ref, sh_ref = refs[:3]
    n_h = phi_ref.shape[1]
    _, _, n_b, width = v_ref.shape
    kinds = (g_ref, h_ref)

    def block(step, carry):
        row = pl.multiple_of(step * ROWS, ROWS)
        rows = pl.ds(row, ROWS)
        for slot, direc in enumerate(dirs):
            for part in range(2):
                for col in range(3):
                    if direc == 0:
                        sh_ref[slot, part, col] = next_ref[part, col, rows, :].astype(jnp.float32)
                    else:
                        field = v_ref[part, col, rows, :].astype(jnp.float32)
                        sh_ref[slot, part, col] = shift_y(field) if direc == 1 else shift_z(field)

        def store(kind, hel, part, col, half, value):
            there = pl.ds(pl.multiple_of(part * n_b + row, ROWS), ROWS)
            kinds[kind][hel, there, pl.ds(col * width + half * HALF, HALF)] = value

        weighted_links(u_ref, phi_ref, sh_ref, dirs, plane, n_h, store)
        return carry

    lax.fori_loop(0, n_b // ROWS, block, 0)

    def multiply(hel, carry):
        mat = jnp.concatenate([v_ref[:, col].reshape(2 * n_b, width) for col in range(3)], 1)
        both = products(mat, g_ref, h_ref, hel)
        for part in range(2):
            total = both[part] + part_ref[hel, part] if has_part else both[part]
            if n_out:
                refs[3][hel * 2 + part] = total
            else:
                out_ref[hel, part] = total
        return carry

    lax.fori_loop(0, n_h, multiply, 0)
    if n_out:
        own = n_b // n_out
        for dev in range(n_out):
            rows = pl.ds(dev * own, own)
            pieces = [refs[3][which, rows, :] for which in range(2 * n_h)]
            out_ref[dev] = jnp.concatenate(pieces, 0).astype(jnp.bfloat16)


def plane_call(plane, dirs, vec, ahead, link, phi, part=None, n_out=0):
    n_h = phi.shape[1]
    _, _, n_b, width = vec.shape
    vmem = pl.BlockSpec(memory_space=pltpu.VMEM)
    args = [vec] + ([ahead] if 0 in dirs else []) + [link, phi]
    args += [part] if part is not None else []
    specs = [vmem] * len(args)
    scratch = [
        pltpu.VMEM((n_h, 2 * n_b, 3 * width), jnp.bfloat16),
        pltpu.VMEM((n_h, 2 * n_b, 3 * width), jnp.bfloat16),
        pltpu.VMEM((len(dirs), 2, 3, ROWS, width), jnp.float32),
    ]
    if n_out:
        scratch.append(pltpu.VMEM((2 * n_h, n_b, n_b), jnp.float32))
        out_shape = jax.ShapeDtypeStruct((n_out, 2 * n_h * (n_b // n_out), n_b), jnp.bfloat16)
    else:
        out_shape = jax.ShapeDtypeStruct((n_h, 2, n_b, n_b), jnp.float32)
    return pl.pallas_call(
        functools.partial(plane_kernel, plane, dirs, part is not None, n_out),
        in_specs=specs,
        out_specs=vmem,
        out_shape=out_shape,
        scratch_shapes=scratch,
        compiler_params=pltpu.CompilerParams(vmem_limit_bytes=VMEM_BYTES),
        cost_estimate=pl.CostEstimate(
            flops=(16 + 8 * len(dirs)) * n_h * n_b * n_b * 3 * width,
            bytes_accessed=2**22,
            transcendentals=0,
        ),
        name="plane%d_%s" % (plane, "".join(str(direc) for direc in dirs)),
    )(*args)


def quark_kernel(n_tau, where_ref, got_ref, *refs):
    tau_refs = refs[:n_tau]
    out_ref, left_ref = refs[n_tau:]
    n_h, n_pair, _, own, n_b = out_ref.shape
    row = lax.broadcasted_iota(jnp.int32, (n_b, 2 * n_b), 0)
    col = lax.broadcasted_iota(jnp.int32, (n_b, 2 * n_b), 1)
    even = (col == 2 * row).astype(jnp.bfloat16)
    odd = (col == 2 * row + 1).astype(jnp.bfloat16)
    total = got_ref[0].astype(jnp.float32)
    for dev in range(1, got_ref.shape[0]):
        total = total + got_ref[dev].astype(jnp.float32)
    swap = []
    for hel in range(n_h):
        start = hel * 2 * own
        swap += [-total[start + own : start + 2 * own], total[start : start + own]]
    left = jnp.dot(total.astype(jnp.bfloat16), even, preferred_element_type=jnp.float32)
    left += jnp.dot(
        jnp.concatenate(swap, 0).astype(jnp.bfloat16), odd, preferred_element_type=jnp.float32
    )
    left_ref[...] = left.astype(jnp.bfloat16)
    depth = tau_refs[0].shape[0]
    whole = depth == 2 * n_b
    if not whole:
        out_ref[...] = jnp.zeros_like(out_ref)
    for which in range(n_tau):
        first = where_ref[which] * depth
        pair = first // (2 * n_b)
        if whole:
            lhs = left_ref[...]
        else:
            lhs = left_ref[:, pl.ds(pl.multiple_of(first - pair * 2 * n_b, depth), depth)]
        res = jnp.dot(lhs, tau_refs[which][...], preferred_element_type=jnp.float32)
        for hel in range(n_h):
            for part in range(2):
                start = (hel * 2 + part) * own
                if whole:
                    out_ref[hel, pair, part] = res[start : start + own]
                else:
                    out_ref[hel, pair, part] += res[start : start + own]


def phase_kernel(n_op, n_x, planes, *refs):
    mom_refs = refs[:n_op]
    num_refs = refs[n_op : 2 * n_op]
    den_ref, where_ref, out_ref = refs[2 * n_op :]
    _, n_h, _, _, _, width = out_ref.shape
    n_mom = mom_refs[0].shape[0]
    moms = [(op, k) for op in range(n_op) for k in range(n_mom)]
    scale = 1.0 / math.sqrt(3.0 * n_x * LY * LZ)
    shape = (planes * len(moms), width)
    row = lax.broadcasted_iota(jnp.int32, shape, 0)
    lane = lax.broadcasted_iota(jnp.int32, shape, 1)
    yy = lane // LZ
    zz = lane & (LZ - 1)

    def spread(values):
        res = jnp.full(shape, values[0], jnp.int32)
        for which in range(1, len(values)):
            res = jnp.where(row == which, values[which], res)
        return res

    comps = [[mom_refs[op][k, axis] for _ in range(planes) for op, k in moms] for axis in range(3)]
    mom_x, mom_y, mom_z = [spread(comp) for comp in comps]
    pos_x = where_ref[0] * planes + row // len(moms)
    steps = ((0, 0, 0), (1, 0, 0), (0, 1, 0), (0, 0, 1))
    waves = []
    for step_x, step_y, step_z in steps:
        turn_x = lax.rem(mom_x * (pos_x + step_x), n_x).astype(jnp.float32) * (1.0 / n_x)
        turn_y = ((mom_y * (yy + step_y)) & (LY - 1)).astype(jnp.float32) * (1.0 / LY)
        turn_z = ((mom_z * (zz + step_z)) & (LZ - 1)).astype(jnp.float32) * (1.0 / LZ)
        turn = turn_x + turn_y + turn_z
        theta = (2.0 * math.pi) * (turn - jnp.floor(turn))
        waves.append((jnp.cos(theta), jnp.sin(theta)))
    for hel in range(n_h):
        which_h = where_ref[1] * n_h + hel
        den = jnp.full((1, width), den_ref[which_h], jnp.int32).astype(jnp.float32)
        for direc in range(NDIR):
            wts = []
            for op, k in moms:
                num = num_refs[op][direc, k, which_h]
                wts.append(jnp.full((1, width), num, jnp.int32).astype(jnp.float32) / den * scale)
            for kind, wave in ((0, waves[0]), (1, waves[1 + direc])):
                for plane in range(planes):
                    start = plane * len(moms)
                    real = sum(wt * wave[0][start + at : start + at + 1] for at, wt in enumerate(wts))
                    imag = sum(wt * wave[1][start + at : start + at + 1] for at, wt in enumerate(wts))
                    out_ref[kind, hel, direc, 0, plane : plane + 1, :] = real
                    out_ref[kind, hel, direc, 1, plane : plane + 1, :] = -imag if kind == 0 else imag


def shards(eigvecs, links, momenta, coef_num, coef_den, peram):
    n_space = lax.axis_size("space")
    n_op = lax.axis_size("op")
    n_tm = lax.axis_size("tm")
    _, _, n_b, _, planes, width = eigvecs.shape
    n_x = planes * n_space
    own = n_b // n_space
    n_h = coef_num.shape[0] // n_op
    my_op = lax.axis_index("op")
    my_space = lax.axis_index("space")

    group = n_space * n_op
    depth = n_b * SPINS // group
    first = (my_space * n_op + my_op) * depth
    piece = lax.dynamic_slice(
        peram.reshape(n_b, SPINS, 2, n_b), (first % n_b, first // n_b, 0, 0), (depth, 1, 2, n_b)
    ).reshape(depth * 2, n_b)
    own_piece = from_behind(piece, "tm", n_tm - 1)

    eigvecs, piece = lax.optimization_barrier((eigvecs, piece))
    vecs = [jnp.transpose(eigvecs[0, :, :, :, 0, :], (0, 2, 1, 3))]
    upper = from_behind(vecs[0], "space", -1)
    for plane in range(1, planes):
        vecs.append(jnp.transpose(eigvecs[0, :, :, :, plane, :], (0, 2, 1, 3)))

    nums = jnp.transpose(coef_num, (2, 1, 0))
    both = [(momenta, nums)]
    both += [(across(momenta, "op", mask), across(nums, "op", mask)) for mask in range(1, n_op)]
    where = jnp.stack([my_space, my_op]).astype(jnp.int32)
    smem = pl.BlockSpec(memory_space=pltpu.SMEM)
    vmem = pl.BlockSpec(memory_space=pltpu.VMEM)
    phi = pl.pallas_call(
        functools.partial(phase_kernel, n_op, n_x, planes),
        in_specs=[smem] * (2 * n_op + 2),
        out_specs=vmem,
        out_shape=jax.ShapeDtypeStruct((2, n_h, NDIR, 2, planes, width), jnp.float32),
        name="phases",
    )(*[mom for mom, _ in both], *[num for _, num in both], coef_den, where)

    link = links[0]
    last = planes - 1
    partial = plane_call(last, (1, 2), vecs[last], None, link, phi)
    own_piece, partial = lax.optimization_barrier((own_piece, partial))
    held = [(own_piece, my_space, my_op)]
    for mask in range(2, n_space, 2):
        held.append((across(own_piece, "space", mask), my_space ^ mask, my_op))
    beyond = [across(own_piece, "op", mask) for mask in range(1, n_op)]
    for plane in range(last):
        partial = plane_call(plane, (1, 2, 0), vecs[plane], vecs[plane + 1], link, phi, partial)
    arrs = [arr for arr, _, _ in held]
    near = arrs[:3]
    *near, partial = lax.optimization_barrier((*near, partial))
    arrs = near + arrs[3:]
    tau = list(zip(arrs, [place for _, place, _ in held]))
    forward = []
    for at, (arr, place) in enumerate(tau[:3]):
        for mask in range(1, n_op):
            forward.append((beyond[mask - 1] if at == 0 else across(arr, "op", mask), place, my_op ^ mask))
    sums = plane_call(last, (0,), vecs[last], upper, link, phi, partial, n_space)
    rest = [arr for arr, _ in tau[3:]]
    *rest, sums = lax.optimization_barrier((*rest, sums))
    tau = tau[:3] + [(arr, place) for arr, (_, place) in zip(rest, tau[3:])]
    for arr, place in tau[3:]:
        for mask in range(1, n_op):
            forward.append((across(arr, "op", mask), place, my_op ^ mask))
    pieces = [(arr, place, my_op) for arr, place in tau]
    pieces += [(across(arr, "space", 1), place ^ 1, my_op) for arr, place in tau]
    got = lax.all_to_all(sums, "space", 0, 0, tiled=True)
    far = [arr for arr, _, _ in forward]
    *far, got = lax.optimization_barrier((*far, got))
    for arr, (_, place, oper) in zip(far, forward):
        pieces += [(arr, place, oper), (across(arr, "space", 1), place ^ 1, oper)]
    tau_place = jnp.stack([place * n_op + oper for _, place, oper in pieces]).astype(jnp.int32)
    tau = [arr for arr, _, _ in pieces]

    lines = pl.pallas_call(
        functools.partial(quark_kernel, len(tau)),
        in_specs=[smem, vmem] + [vmem] * len(tau),
        out_specs=vmem,
        out_shape=jax.ShapeDtypeStruct((n_h, SPINS, 2, own, n_b), jnp.float32),
        scratch_shapes=[pltpu.VMEM((n_h * 2 * own, 2 * n_b), jnp.bfloat16)],
        compiler_params=pltpu.CompilerParams(vmem_limit_bytes=VMEM_BYTES),
        cost_estimate=pl.CostEstimate(
            flops=2 * SPINS * n_h * 2 * own * 2 * n_b * n_b, bytes_accessed=7 * 2**20, transcendentals=0
        ),
        name="quark_products",
    )(tau_place, got, *tau)
    return lines.reshape(1, n_h, 4, 4, 2, own, n_b)


def solution(mesh):
    return jax.shard_map(
        shards,
        mesh=mesh,
        in_specs=(
            P("tm", None, None, None, "space", None),
            P("tm", None, None, None, None, "space", None),
            P("op", None),
            P(None, "op", None),
            P(),
            P("tm", None, None, None, None, None),
        ),
        out_specs=P("tm", "op", None, None, None, "space", None),
        check_vma=False,
    )
```

```python
import functools
import itertools
import math

import jax
import jax.numpy as jnp
from jax import lax
from jax.experimental import pallas as pl
from jax.experimental.pallas import tpu as pltpu
from jax.sharding import PartitionSpec as P

LY = 32
LZ = 8
NDIR = 3
SPINS = 16
ROWS = 16
HALF = 128
VMEM_BYTES = 20 * 2**20


def from_behind(value, axis, steps):
    count = lax.axis_size(axis)
    pairs = [(source, (source + steps) % count) for source in range(count)]
    return lax.ppermute(value, axis, pairs)


def across(value, axis, mask):
    pairs = [(source, source ^ mask) for source in range(lax.axis_size(axis))]
    return lax.ppermute(value, axis, pairs)


def dot_nt(left, right):
    return lax.dot_general(
        left, right, (((1,), (1,)), ((), ())), preferred_element_type=jnp.float32
    )


def shift_y(arr):
    return pltpu.roll(arr, arr.shape[1] - LZ, 1)


def shift_z(arr):
    width = arr.shape[1]
    lane = lax.broadcasted_iota(jnp.int32, arr.shape, 1)
    near = pltpu.roll(arr, width - 1, 1)
    far = pltpu.roll(arr, LZ - 1, 1)
    return jnp.where((lane & (LZ - 1)) == LZ - 1, far, near)


def weighted_links(u_ref, phi_ref, shifted, dirs, plane, n_h, store):
    width = u_ref.shape[-1]
    for half in range(width // HALF):
        lanes = pl.ds(half * HALF, HALF)
        for col in range(3):
            acc = {}
            for slot, direc in enumerate(dirs):
                f_r = None
                f_i = None
                for col_two in range(3):
                    u_r = u_ref[direc, col, col_two, 0, pl.ds(plane, 1), lanes]
                    u_i = u_ref[direc, col, col_two, 1, pl.ds(plane, 1), lanes]
                    v_r = shifted[slot, 0, col_two, :, lanes]
                    v_i = shifted[slot, 1, col_two, :, lanes]
                    term_r = u_r * v_r - u_i * v_i
                    term_i = u_r * v_i + u_i * v_r
                    f_r = term_r if f_r is None else f_r + term_r
                    f_i = term_i if f_i is None else f_i + term_i
                for kind in range(2):
                    for hel in range(n_h):
                        p_r = phi_ref[kind, hel, direc, 0, pl.ds(plane, 1), lanes]
                        p_i = phi_ref[kind, hel, direc, 1, pl.ds(plane, 1), lanes]
                        g_r = p_r * f_r - p_i * f_i
                        g_i = p_r * f_i + p_i * f_r
                        if (kind, hel) in acc:
                            old_r, old_i = acc[kind, hel]
                            g_r, g_i = old_r + g_r, old_i + g_i
                        acc[kind, hel] = (g_r, g_i)
            for (kind, hel), (g_r, g_i) in acc.items():
                store(kind, hel, col, half, g_r, g_i)


def plane_kernel(plane, dirs, has_part, n_out, *refs):
    refs = list(refs)
    v_ref = refs.pop(0)
    next_ref = refs.pop(0) if 0 in dirs else None
    u_ref, phi_ref = refs.pop(0), refs.pop(0)
    part_ref = refs.pop(0) if has_part else None
    out_ref, mat_ref, g_ref, h_ref, sh_ref = refs
    n_h = phi_ref.shape[1]
    _, _, n_b, width = v_ref.shape
    inner = 3 * width
    kinds = (g_ref, h_ref)

    def block(step, carry):
        rows = pl.ds(pl.multiple_of(step * ROWS, ROWS), ROWS)
        for part in range(2):
            for col in range(3):
                field = v_ref[part, col, rows, :]
                mat_ref[rows, pl.ds(part * inner + col * width, width)] = field
                field = field.astype(jnp.float32)
                for slot, direc in enumerate(dirs):
                    if direc == 0:
                        sh_ref[slot, part, col] = next_ref[part, col, rows, :].astype(jnp.float32)
                    else:
                        sh_ref[slot, part, col] = shift_y(field) if direc == 1 else shift_z(field)

        def store(kind, hel, col, half, real, imag):
            at = col * width + half * HALF
            low, high = pl.ds(at, HALF), pl.ds(inner + at, HALF)
            real_b, imag_b = real.astype(jnp.bfloat16), imag.astype(jnp.bfloat16)
            kinds[kind][hel, 0, rows, low] = real_b
            kinds[kind][hel, 0, rows, high] = imag_b
            kinds[kind][hel, 1, rows, low] = -imag_b if kind else imag_b
            kinds[kind][hel, 1, rows, high] = real_b if kind else -real_b

        weighted_links(u_ref, phi_ref, sh_ref, dirs, plane, n_h, store)
        return carry

    lax.fori_loop(0, n_b // ROWS, block, 0)

    def multiply(hel, carry):
        mat = mat_ref[...]
        one = dot_nt(mat, g_ref[hel].reshape(2 * n_b, 2 * inner))
        two = dot_nt(h_ref[hel].reshape(2 * n_b, 2 * inner), mat)
        for part in range(2):
            total = one[:, part * n_b : (part + 1) * n_b] + two[part * n_b : (part + 1) * n_b]
            if has_part:
                total = total + part_ref[hel, part]
            if n_out:
                out_ref[:, hel, part] = total.reshape(n_out, n_b // n_out, n_b).astype(jnp.bfloat16)
            else:
                out_ref[hel, part] = total
        return carry

    lax.fori_loop(0, n_h, multiply, 0)


def plane_call(plane, dirs, vec, ahead, link, phi, part=None, n_out=0):
    n_h = phi.shape[1]
    _, _, n_b, width = vec.shape
    vmem = pl.BlockSpec(memory_space=pltpu.VMEM)
    args = [vec] + ([ahead] if 0 in dirs else []) + [link, phi]
    args += [part] if part is not None else []
    specs = [vmem] * len(args)
    scratch = [
        pltpu.VMEM((n_b, 6 * width), jnp.bfloat16),
        pltpu.VMEM((n_h, 2, n_b, 6 * width), jnp.bfloat16),
        pltpu.VMEM((n_h, 2, n_b, 6 * width), jnp.bfloat16),
        pltpu.VMEM((len(dirs), 2, 3, ROWS, width), jnp.float32),
    ]
    if n_out:
        out_shape = jax.ShapeDtypeStruct((n_out, n_h, 2, n_b // n_out, n_b), jnp.bfloat16)
    else:
        out_shape = jax.ShapeDtypeStruct((n_h, 2, n_b, n_b), jnp.float32)
    return pl.pallas_call(
        functools.partial(plane_kernel, plane, dirs, part is not None, n_out),
        in_specs=specs,
        out_specs=vmem,
        out_shape=out_shape,
        scratch_shapes=scratch,
        compiler_params=pltpu.CompilerParams(vmem_limit_bytes=VMEM_BYTES),
        cost_estimate=pl.CostEstimate(
            flops=(16 + 8 * len(dirs)) * n_h * n_b * n_b * 3 * width,
            bytes_accessed=2**22,
            transcendentals=0,
        ),
        name="plane%d_%s" % (plane, "".join(str(direc) for direc in dirs)),
    )(*args)


def quark_kernel(masks, n_op, got_ref, *refs):
    n_tau = len(masks)
    tau_refs = refs[:n_tau]
    out_ref, left_ref = refs[n_tau:]
    my_space, my_op = lax.axis_index("space"), lax.axis_index("op")
    n_h, n_pair, _, own, n_b = out_ref.shape
    row = lax.broadcasted_iota(jnp.int32, (n_b, 2 * n_b), 0)
    col = lax.broadcasted_iota(jnp.int32, (n_b, 2 * n_b), 1)
    even = (col == 2 * row).astype(jnp.bfloat16)
    odd = (col == 2 * row + 1).astype(jnp.bfloat16)
    total = got_ref[0].astype(jnp.float32)
    for dev in range(1, got_ref.shape[0]):
        total = total + got_ref[dev].astype(jnp.float32)
    total = total.reshape(n_h * 2 * own, n_b)
    swap = []
    for hel in range(n_h):
        start = hel * 2 * own
        swap += [-total[start + own : start + 2 * own], total[start : start + own]]
    left = jnp.dot(total.astype(jnp.bfloat16), even, preferred_element_type=jnp.float32)
    left += jnp.dot(
        jnp.concatenate(swap, 0).astype(jnp.bfloat16), odd, preferred_element_type=jnp.float32
    )
    left_ref[...] = left.astype(jnp.bfloat16)
    depth = tau_refs[0].shape[0]
    whole = depth == 2 * n_b
    if not whole:
        out_ref[...] = jnp.zeros_like(out_ref)
    for which, (mask, mask_op) in enumerate(masks):
        first = ((my_space ^ mask) * n_op + (my_op ^ mask_op)) * depth
        pair = first // (2 * n_b)
        if whole:
            lhs = left_ref[...]
        else:
            lhs = left_ref[:, pl.ds(pl.multiple_of(first - pair * 2 * n_b, depth), depth)]
        res = jnp.dot(lhs, tau_refs[which][...], preferred_element_type=jnp.float32)
        for hel in range(n_h):
            for part in range(2):
                start = (hel * 2 + part) * own
                if whole:
                    out_ref[hel, pair, part] = res[start : start + own]
                else:
                    out_ref[hel, pair, part] += res[start : start + own]


def phase_kernel(n_op, n_x, planes, *refs):
    mom_refs = refs[:n_op]
    num_refs = refs[n_op : 2 * n_op]
    den_ref, out_ref = refs[2 * n_op :]
    my_space, my_op = lax.axis_index("space"), lax.axis_index("op")
    _, n_h, _, _, _, width = out_ref.shape
    n_mom = mom_refs[0].shape[0]
    moms = [(op, k) for op in range(n_op) for k in range(n_mom)]
    scale = 1.0 / math.sqrt(3.0 * n_x * LY * LZ)
    shape = (planes * len(moms), width)
    row = lax.broadcasted_iota(jnp.int32, shape, 0)
    lane = lax.broadcasted_iota(jnp.int32, shape, 1)
    yy = lane // LZ
    zz = lane & (LZ - 1)

    def spread(values):
        res = jnp.full(shape, values[0], jnp.int32)
        for which in range(1, len(values)):
            res = jnp.where(row == which, values[which], res)
        return res

    comps = [[mom_refs[op][k, axis] for _ in range(planes) for op, k in moms] for axis in range(3)]
    mom_x, mom_y, mom_z = [spread(comp) for comp in comps]
    pos_x = my_space * planes + row // len(moms)
    steps = ((0, 0, 0), (1, 0, 0), (0, 1, 0), (0, 0, 1))
    waves = []
    for step_x, step_y, step_z in steps:
        turn_x = lax.rem(mom_x * (pos_x + step_x), n_x).astype(jnp.float32) * (1.0 / n_x)
        turn_y = ((mom_y * (yy + step_y)) & (LY - 1)).astype(jnp.float32) * (1.0 / LY)
        turn_z = ((mom_z * (zz + step_z)) & (LZ - 1)).astype(jnp.float32) * (1.0 / LZ)
        turn = turn_x + turn_y + turn_z
        theta = (2.0 * math.pi) * (turn - jnp.floor(turn))
        waves.append((jnp.cos(theta), jnp.sin(theta)))
    for hel in range(n_h):
        which_h = my_op * n_h + hel
        den = jnp.full((1, width), den_ref[which_h], jnp.int32).astype(jnp.float32)
        for direc in range(NDIR):
            wts = []
            for op, k in moms:
                num = num_refs[op][direc, k, which_h]
                wts.append(jnp.full((1, width), num, jnp.int32).astype(jnp.float32) / den * scale)
            for kind, wave in ((0, waves[0]), (1, waves[1 + direc])):
                for plane in range(planes):
                    start = plane * len(moms)
                    real = sum(wt * wave[0][start + at : start + at + 1] for at, wt in enumerate(wts))
                    imag = sum(wt * wave[1][start + at : start + at + 1] for at, wt in enumerate(wts))
                    out_ref[kind, hel, direc, 0, plane : plane + 1, :] = -real if kind else real
                    out_ref[kind, hel, direc, 1, plane : plane + 1, :] = -imag


def shards(eigvecs, links, momenta, coef_num, coef_den, peram):
    n_space = lax.axis_size("space")
    n_op = lax.axis_size("op")
    n_tm = lax.axis_size("tm")
    _, _, n_b, _, planes, width = eigvecs.shape
    n_x = planes * n_space
    own = n_b // n_space
    n_h = coef_num.shape[0] // n_op
    my_op = lax.axis_index("op")
    my_space = lax.axis_index("space")

    group = n_space * n_op
    depth = n_b * SPINS // group
    first = (my_space * n_op + my_op) * depth
    piece = lax.dynamic_slice(
        peram.reshape(n_b, SPINS, 2, n_b), (first % n_b, first // n_b, 0, 0), (depth, 1, 2, n_b)
    ).reshape(depth * 2, n_b)
    own_piece = from_behind(piece, "tm", n_tm - 1)

    eigvecs, momenta, coef_num, piece = lax.optimization_barrier((eigvecs, momenta, coef_num, piece))
    vecs = [jnp.transpose(eigvecs[0, :, :, :, plane, :], (0, 2, 1, 3)) for plane in range(planes)]
    upper = from_behind(vecs[0], "space", -1)

    nums = jnp.transpose(coef_num, (2, 1, 0))
    both = [(momenta, nums)]
    both += [(across(momenta, "op", mask), across(nums, "op", mask)) for mask in range(1, n_op)]
    smem = pl.BlockSpec(memory_space=pltpu.SMEM)
    vmem = pl.BlockSpec(memory_space=pltpu.VMEM)
    phi = pl.pallas_call(
        functools.partial(phase_kernel, n_op, n_x, planes),
        in_specs=[smem] * (2 * n_op + 1),
        out_specs=vmem,
        out_shape=jax.ShapeDtypeStruct((2, n_h, NDIR, 2, planes, width), jnp.float32),
        name="phases",
    )(*[mom for mom, _ in both], *[num for _, num in both], coef_den)

    dims = [("op", 1 << bit) for bit in range(n_op.bit_length() - 1)]
    dims += [("space", 1 << bit) for bit in range(1, n_space.bit_length() - 1)]
    load = [0] * len(dims)

    def stage(held, size):
        for group_dims in itertools.combinations(range(len(dims)), size):
            dim = min(group_dims, key=lambda at: load[at])
            load[dim] += 1
            before = held[tuple(at for at in group_dims if at != dim)]
            held[group_dims] = across(before, *dims[dim])

    def hold(held, other):
        arrs, other = lax.optimization_barrier((list(held.values()), other))
        return dict(zip(held.keys(), arrs)), other

    link = links[0]
    last = planes - 1
    partial = plane_call(last, (1, 2), vecs[last], None, link, phi)
    held, partial = hold({(): own_piece}, partial)
    stage(held, 1)
    for plane in range(last):
        partial = plane_call(plane, (1, 2, 0), vecs[plane], vecs[plane + 1], link, phi, partial)
    held, partial = hold(held, partial)
    stage(held, 2)
    sums = plane_call(last, (0,), vecs[last], upper, link, phi, partial, n_space)
    held, sums = hold(held, sums)
    got = lax.all_to_all(sums, "space", 0, 0, tiled=True)
    for size in range(3, len(dims) + 1):
        stage(held, size)
    tau, masks = [], []
    for flip in range(2):
        for group_dims, arr in held.items():
            mask = {"space": flip, "op": 0}
            for at in group_dims:
                mask[dims[at][0]] ^= dims[at][1]
            tau.append(across(arr, "space", 1) if flip else arr)
            masks.append((mask["space"], mask["op"]))

    lines = pl.pallas_call(
        functools.partial(quark_kernel, masks, n_op),
        in_specs=[vmem] * (1 + len(tau)),
        out_specs=vmem,
        out_shape=jax.ShapeDtypeStruct((n_h, SPINS, 2, own, n_b), jnp.float32),
        scratch_shapes=[pltpu.VMEM((n_h * 2 * own, 2 * n_b), jnp.bfloat16)],
        compiler_params=pltpu.CompilerParams(vmem_limit_bytes=VMEM_BYTES),
        cost_estimate=pl.CostEstimate(
            flops=2 * SPINS * n_h * 2 * own * 2 * n_b * n_b, bytes_accessed=7 * 2**20, transcendentals=0
        ),
        name="quark_products",
    )(got, *tau)
    return lines.reshape(1, n_h, 4, 4, 2, own, n_b)


def solution(mesh):
    return jax.shard_map(
        shards,
        mesh=mesh,
        in_specs=(
            P("tm", None, None, None, "space", None),
            P("tm", None, None, None, None, "space", None),
            P("op", None),
            P(None, "op", None),
            P(),
            P("tm", None, None, None, None, None),
        ),
        out_specs=P("tm", "op", None, None, None, "space", None),
        check_vma=False,
    )
```

```python
import functools
import itertools
import math

import jax
import jax.numpy as jnp
from jax import lax
from jax.experimental import pallas as pl
from jax.experimental.pallas import tpu as pltpu
from jax.sharding import PartitionSpec as P

LY = 32
LZ = 8
NDIR = 3
SPINS = 16
ROWS = 16
HALF = 128
VMEM_BYTES = 20 * 2**20


def from_behind(value, axis, steps):
    count = lax.axis_size(axis)
    pairs = [(source, (source + steps) % count) for source in range(count)]
    return lax.ppermute(value, axis, pairs)


def across(value, axis, mask):
    pairs = [(source, source ^ mask) for source in range(lax.axis_size(axis))]
    return lax.ppermute(value, axis, pairs)


def dot_nt(left, right):
    return lax.dot_general(
        left, right, (((1,), (1,)), ((), ())), preferred_element_type=jnp.float32
    )


def shift_y(arr):
    return pltpu.roll(arr, arr.shape[1] - LZ, 1)


def shift_z(arr):
    width = arr.shape[1]
    lane = lax.broadcasted_iota(jnp.int32, arr.shape, 1)
    near = pltpu.roll(arr, width - 1, 1)
    far = pltpu.roll(arr, LZ - 1, 1)
    return jnp.where((lane & (LZ - 1)) == LZ - 1, far, near)


def weighted_links(u_ref, phi_ref, shifted, dirs, plane, n_h, store):
    width = u_ref.shape[-1]
    for half in range(width // HALF):
        lanes = pl.ds(half * HALF, HALF)
        for col in range(3):
            acc = {}
            for slot, direc in enumerate(dirs):
                f_r = None
                f_i = None
                for col_two in range(3):
                    u_r = u_ref[direc, col, col_two, 0, pl.ds(plane, 1), lanes]
                    u_i = u_ref[direc, col, col_two, 1, pl.ds(plane, 1), lanes]
                    v_r = shifted[slot, 0, col_two, :, lanes]
                    v_i = shifted[slot, 1, col_two, :, lanes]
                    term_r = u_r * v_r - u_i * v_i
                    term_i = u_r * v_i + u_i * v_r
                    f_r = term_r if f_r is None else f_r + term_r
                    f_i = term_i if f_i is None else f_i + term_i
                for kind in range(2):
                    for hel in range(n_h):
                        p_r = phi_ref[kind, hel, direc, 0, pl.ds(plane, 1), lanes]
                        p_i = phi_ref[kind, hel, direc, 1, pl.ds(plane, 1), lanes]
                        g_r = p_r * f_r - p_i * f_i
                        g_i = p_r * f_i + p_i * f_r
                        if (kind, hel) in acc:
                            old_r, old_i = acc[kind, hel]
                            g_r, g_i = old_r + g_r, old_i + g_i
                        acc[kind, hel] = (g_r, g_i)
            for (kind, hel), (g_r, g_i) in acc.items():
                store(kind, hel, col, half, (g_r, g_i))


def plane_kernel(plane, dirs, has_part, n_out, *refs):
    refs = list(refs)
    v_ref = refs.pop(0)
    next_ref = refs.pop(0) if 0 in dirs else None
    u_ref, phi_ref = refs.pop(0), refs.pop(0)
    part_ref = refs.pop(0) if has_part else None
    out_ref, g_ref, h_ref, sh_ref = refs
    n_h = phi_ref.shape[1]
    _, _, n_b, width = v_ref.shape
    kinds = (g_ref, h_ref)

    def block(step, carry):
        row = pl.multiple_of(step * ROWS, ROWS)
        rows = pl.ds(row, ROWS)
        for slot, direc in enumerate(dirs):
            for part in range(2):
                for col in range(3):
                    source = next_ref if direc == 0 else v_ref
                    field = source[part, col, rows, :].astype(jnp.float32)
                    if direc == 1:
                        field = shift_y(field)
                    elif direc == 2:
                        field = shift_z(field)
                    sh_ref[slot, part, col] = field

        def store(kind, hel, col, half, both):
            for part in range(2):
                there = pl.ds(pl.multiple_of(part * n_b + row, ROWS), ROWS)
                lanes = pl.ds(col * width + half * HALF, HALF)
                kinds[kind][hel, there, lanes] = both[part].astype(jnp.bfloat16)

        weighted_links(u_ref, phi_ref, sh_ref, dirs, plane, n_h, store)
        return carry

    lax.fori_loop(0, n_b // ROWS, block, 0)

    def multiply(hel, carry):
        mat = jnp.concatenate([v_ref[:, col].reshape(2 * n_b, width) for col in range(3)], 1)
        one = dot_nt(mat, g_ref[hel])
        two = dot_nt(h_ref[hel], mat)
        real = one[:n_b, :n_b] + one[n_b:, n_b:] + two[:n_b, :n_b] + two[n_b:, n_b:]
        imag = one[:n_b, n_b:] - one[n_b:, :n_b] + two[:n_b, n_b:] - two[n_b:, :n_b]
        for part, total in enumerate((real, imag)):
            if has_part:
                total = total + part_ref[hel, part]
            if n_out:
                out_ref[:, hel, part] = total.reshape(n_out, n_b // n_out, n_b).astype(jnp.bfloat16)
            else:
                out_ref[hel, part] = total
        return carry

    lax.fori_loop(0, n_h, multiply, 0)


def plane_call(plane, dirs, vec, ahead, link, phi, part=None, n_out=0):
    n_h = phi.shape[1]
    _, _, n_b, width = vec.shape
    vmem = pl.BlockSpec(memory_space=pltpu.VMEM)
    args = [vec] + ([ahead] if 0 in dirs else []) + [link, phi]
    args += [part] if part is not None else []
    specs = [vmem] * len(args)
    scratch = [
        pltpu.VMEM((n_h, 2 * n_b, 3 * width), jnp.bfloat16),
        pltpu.VMEM((n_h, 2 * n_b, 3 * width), jnp.bfloat16),
        pltpu.VMEM((len(dirs), 2, 3, ROWS, width), jnp.float32),
    ]
    if n_out:
        out_shape = jax.ShapeDtypeStruct((n_out, n_h, 2, n_b // n_out, n_b), jnp.bfloat16)
    else:
        out_shape = jax.ShapeDtypeStruct((n_h, 2, n_b, n_b), jnp.float32)
    return pl.pallas_call(
        functools.partial(plane_kernel, plane, dirs, part is not None, n_out),
        in_specs=specs,
        out_specs=vmem,
        out_shape=out_shape,
        scratch_shapes=scratch,
        compiler_params=pltpu.CompilerParams(vmem_limit_bytes=VMEM_BYTES),
        cost_estimate=pl.CostEstimate(
            flops=(16 + 8 * len(dirs)) * n_h * n_b * n_b * 3 * width,
            bytes_accessed=2**22,
            transcendentals=0,
        ),
        name="plane%d_%s" % (plane, "".join(str(direc) for direc in dirs)),
    )(*args)


def quark_kernel(masks, n_op, got_ref, *refs):
    n_tau = len(masks)
    sources = refs[:n_tau]
    out_ref, left_ref, tau_ref, sems = refs[n_tau:]
    my_space, my_op = lax.axis_index("space"), lax.axis_index("op")
    n_h, n_pair, _, own, n_b = out_ref.shape
    copies = [
        pltpu.make_async_copy(source, tau_ref.at[which], sems.at[which])
        for which, source in enumerate(sources)
    ]
    for copy in copies:
        copy.start()
    row = lax.broadcasted_iota(jnp.int32, (n_b, 2 * n_b), 0)
    col = lax.broadcasted_iota(jnp.int32, (n_b, 2 * n_b), 1)
    even = (col == 2 * row).astype(jnp.bfloat16)
    odd = (col == 2 * row + 1).astype(jnp.bfloat16)
    total = got_ref[0].astype(jnp.float32)
    for dev in range(1, got_ref.shape[0]):
        total = total + got_ref[dev].astype(jnp.float32)
    total = total.reshape(n_h * 2 * own, n_b)
    swap = []
    for hel in range(n_h):
        start = hel * 2 * own
        swap += [-total[start + own : start + 2 * own], total[start : start + own]]
    left = jnp.dot(total.astype(jnp.bfloat16), even, preferred_element_type=jnp.float32)
    left += jnp.dot(
        jnp.concatenate(swap, 0).astype(jnp.bfloat16), odd, preferred_element_type=jnp.float32
    )
    left_ref[...] = left.astype(jnp.bfloat16)
    depth = tau_ref.shape[1]
    whole = depth == 2 * n_b
    if not whole:
        out_ref[...] = jnp.zeros_like(out_ref)
    for which, (mask, mask_op) in enumerate(masks):
        copies[which].wait()
        first = ((my_space ^ mask) * n_op + (my_op ^ mask_op)) * depth
        pair = first // (2 * n_b)
        if whole:
            lhs = left_ref[...]
        else:
            lhs = left_ref[:, pl.ds(pl.multiple_of(first - pair * 2 * n_b, depth), depth)]
        res = jnp.dot(lhs, tau_ref[which], preferred_element_type=jnp.float32)
        for hel in range(n_h):
            for part in range(2):
                start = (hel * 2 + part) * own
                if whole:
                    out_ref[hel, pair, part] = res[start : start + own]
                else:
                    out_ref[hel, pair, part] += res[start : start + own]


def phase_kernel(n_op, n_x, planes, *refs):
    mom_refs = refs[:n_op]
    num_refs = refs[n_op : 2 * n_op]
    den_ref, out_ref = refs[2 * n_op :]
    my_space, my_op = lax.axis_index("space"), lax.axis_index("op")
    _, n_h, _, _, _, width = out_ref.shape
    n_mom = mom_refs[0].shape[0]
    moms = [(op, k) for op in range(n_op) for k in range(n_mom)]
    scale = 1.0 / math.sqrt(3.0 * n_x * LY * LZ)
    shape = (planes * len(moms), width)
    row = lax.broadcasted_iota(jnp.int32, shape, 0)
    lane = lax.broadcasted_iota(jnp.int32, shape, 1)
    yy = lane // LZ
    zz = lane & (LZ - 1)

    def spread(values):
        res = jnp.full(shape, values[0], jnp.int32)
        for which in range(1, len(values)):
            res = jnp.where(row == which, values[which], res)
        return res

    comps = [[mom_refs[op][k, axis] for _ in range(planes) for op, k in moms] for axis in range(3)]
    mom_x, mom_y, mom_z = [spread(comp) for comp in comps]
    pos_x = my_space * planes + row // len(moms)
    steps = ((0, 0, 0), (1, 0, 0), (0, 1, 0), (0, 0, 1))
    waves = []
    for step_x, step_y, step_z in steps:
        turn_x = lax.rem(mom_x * (pos_x + step_x), n_x).astype(jnp.float32) * (1.0 / n_x)
        turn_y = ((mom_y * (yy + step_y)) & (LY - 1)).astype(jnp.float32) * (1.0 / LY)
        turn_z = ((mom_z * (zz + step_z)) & (LZ - 1)).astype(jnp.float32) * (1.0 / LZ)
        turn = turn_x + turn_y + turn_z
        theta = (2.0 * math.pi) * (turn - jnp.floor(turn))
        waves.append((jnp.cos(theta), jnp.sin(theta)))
    for hel in range(n_h):
        which_h = my_op * n_h + hel
        den = jnp.full((1, width), den_ref[which_h], jnp.int32).astype(jnp.float32)
        for direc in range(NDIR):
            wts = []
            for op, k in moms:
                num = num_refs[op][direc, k, which_h]
                wts.append(jnp.full((1, width), num, jnp.int32).astype(jnp.float32) / den * scale)
            for kind, wave in ((0, waves[0]), (1, waves[1 + direc])):
                for plane in range(planes):
                    start = plane * len(moms)
                    real = sum(wt * wave[0][start + at : start + at + 1] for at, wt in enumerate(wts))
                    imag = sum(wt * wave[1][start + at : start + at + 1] for at, wt in enumerate(wts))
                    out_ref[kind, hel, direc, 0, plane : plane + 1, :] = -real if kind else real
                    out_ref[kind, hel, direc, 1, plane : plane + 1, :] = -imag


def shards(eigvecs, links, momenta, coef_num, coef_den, peram):
    n_space = lax.axis_size("space")
    n_op = lax.axis_size("op")
    n_tm = lax.axis_size("tm")
    _, _, n_b, _, planes, width = eigvecs.shape
    n_x = planes * n_space
    own = n_b // n_space
    n_h = coef_num.shape[0] // n_op
    my_op = lax.axis_index("op")
    my_space = lax.axis_index("space")

    group = n_space * n_op
    depth = n_b * SPINS // group
    first = (my_space * n_op + my_op) * depth
    piece = lax.dynamic_slice(
        peram.reshape(n_b, SPINS, 2, n_b), (first % n_b, first // n_b, 0, 0), (depth, 1, 2, n_b)
    ).reshape(depth * 2, n_b)
    own_piece = from_behind(piece, "tm", n_tm - 1)

    eigvecs, piece = lax.optimization_barrier((eigvecs, piece))
    vecs = [jnp.transpose(eigvecs[0, :, :, :, plane, :], (0, 2, 1, 3)) for plane in range(planes)]
    upper = from_behind(vecs[0], "space", -1)

    nums = jnp.transpose(coef_num, (2, 1, 0))
    both = [(momenta, nums)]
    both += [(across(momenta, "op", mask), across(nums, "op", mask)) for mask in range(1, n_op)]
    smem = pl.BlockSpec(memory_space=pltpu.SMEM)
    vmem = pl.BlockSpec(memory_space=pltpu.VMEM)
    phi = pl.pallas_call(
        functools.partial(phase_kernel, n_op, n_x, planes),
        in_specs=[smem] * (2 * n_op + 1),
        out_specs=vmem,
        out_shape=jax.ShapeDtypeStruct((2, n_h, NDIR, 2, planes, width), jnp.float32),
        compiler_params=pltpu.CompilerParams(vmem_limit_bytes=4 * 2**20),
        name="phases",
    )(*[mom for mom, _ in both], *[num for _, num in both], coef_den)

    dims = [("op", 1 << bit) for bit in range(n_op.bit_length() - 1)]
    dims += [("space", 1 << bit) for bit in range(1, n_space.bit_length() - 1)]
    load = [0] * len(dims)

    def stage(held, size):
        for group_dims in itertools.combinations(range(len(dims)), size):
            dim = min(group_dims, key=lambda at: load[at])
            load[dim] += 1
            before = held[tuple(at for at in group_dims if at != dim)]
            held[group_dims] = across(before, *dims[dim])

    def hold(held, other):
        arrs, other = lax.optimization_barrier((list(held.values()), other))
        return dict(zip(held.keys(), arrs)), other

    link = links[0]
    last = planes - 1
    partial = plane_call(last, (1, 2), vecs[last], None, link, phi)
    held, partial = hold({(): own_piece}, partial)
    stage(held, 1)
    for plane in range(last):
        partial = plane_call(plane, (1, 2, 0), vecs[plane], vecs[plane + 1], link, phi, partial)
    held, partial = hold(held, partial)
    stage(held, 2)
    sums = plane_call(last, (0,), vecs[last], upper, link, phi, partial, n_space)
    held, sums = hold(held, sums)
    got = lax.all_to_all(sums, "space", 0, 0, tiled=True)
    for size in range(3, len(dims) + 1):
        stage(held, size)
    tau, masks = [], []
    for flip in range(2):
        for group_dims, arr in held.items():
            mask = {"space": flip, "op": 0}
            for at in group_dims:
                mask[dims[at][0]] ^= dims[at][1]
            tau.append(across(arr, "space", 1) if flip else arr)
            masks.append((mask["space"], mask["op"]))

    lines = pl.pallas_call(
        functools.partial(quark_kernel, masks, n_op),
        in_specs=[vmem] + [pl.BlockSpec(memory_space=pltpu.HBM)] * len(tau),
        out_specs=vmem,
        out_shape=jax.ShapeDtypeStruct((n_h, SPINS, 2, own, n_b), jnp.float32),
        scratch_shapes=[
            pltpu.VMEM((n_h * 2 * own, 2 * n_b), jnp.bfloat16),
            pltpu.VMEM((len(tau),) + tau[0].shape, jnp.bfloat16),
            pltpu.SemaphoreType.DMA((len(tau),)),
        ],
        compiler_params=pltpu.CompilerParams(vmem_limit_bytes=VMEM_BYTES),
        cost_estimate=pl.CostEstimate(
            flops=2 * SPINS * n_h * 2 * own * 2 * n_b * n_b, bytes_accessed=7 * 2**20, transcendentals=0
        ),
        name="quark_products",
    )(got, *tau)
    return lines.reshape(1, n_h, 4, 4, 2, own, n_b)


def solution(mesh):
    return jax.shard_map(
        shards,
        mesh=mesh,
        in_specs=(
            P("tm", None, None, None, "space", None),
            P("tm", None, None, None, None, "space", None),
            P("op", None),
            P(None, "op", None),
            P(),
            P("tm", None, None, None, None, None),
        ),
        out_specs=P("tm", "op", None, None, None, "space", None),
        check_vma=False,
    )
```

```python
import functools
import itertools
import math

import jax
import jax.numpy as jnp
from jax import lax
from jax.experimental import pallas as pl
from jax.experimental.pallas import tpu as pltpu
from jax.sharding import PartitionSpec as P

LY = 32
LZ = 8
NDIR = 3
SPINS = 16
ROWS = 16
HALF = 128
VMEM_BYTES = 20 * 2**20


def from_behind(value, axis, steps):
    count = lax.axis_size(axis)
    pairs = [(source, (source + steps) % count) for source in range(count)]
    return lax.ppermute(value, axis, pairs)


def across(value, axis, mask):
    pairs = [(source, source ^ mask) for source in range(lax.axis_size(axis))]
    return lax.ppermute(value, axis, pairs)


def dot_nt(left, right):
    return lax.dot_general(
        left, right, (((1,), (1,)), ((), ())), preferred_element_type=jnp.float32
    )


def shift_y(arr):
    return pltpu.roll(arr, arr.shape[1] - LZ, 1)


def shift_z(arr):
    width = arr.shape[1]
    lane = lax.broadcasted_iota(jnp.int32, arr.shape, 1)
    near = pltpu.roll(arr, width - 1, 1)
    far = pltpu.roll(arr, LZ - 1, 1)
    return jnp.where((lane & (LZ - 1)) == LZ - 1, far, near)


def weighted_links(u_ref, phi_ref, shifted, dirs, plane, n_h, store):
    width = u_ref.shape[-1]
    for half in range(width // HALF):
        lanes = pl.ds(half * HALF, HALF)
        for col in range(3):
            acc = {}
            for slot, direc in enumerate(dirs):
                f_r = None
                f_i = None
                for col_two in range(3):
                    u_r = u_ref[direc, col, col_two, 0, pl.ds(plane, 1), lanes]
                    u_i = u_ref[direc, col, col_two, 1, pl.ds(plane, 1), lanes]
                    v_r = shifted[slot, 0, col_two, :, lanes]
                    v_i = shifted[slot, 1, col_two, :, lanes]
                    term_r = u_r * v_r - u_i * v_i
                    term_i = u_r * v_i + u_i * v_r
                    f_r = term_r if f_r is None else f_r + term_r
                    f_i = term_i if f_i is None else f_i + term_i
                for kind in range(2):
                    for hel in range(n_h):
                        p_r = phi_ref[kind, hel, direc, 0, pl.ds(plane, 1), lanes]
                        p_i = phi_ref[kind, hel, direc, 1, pl.ds(plane, 1), lanes]
                        g_r = p_r * f_r - p_i * f_i
                        g_i = p_r * f_i + p_i * f_r
                        if (kind, hel) in acc:
                            old_r, old_i = acc[kind, hel]
                            g_r, g_i = old_r + g_r, old_i + g_i
                        acc[kind, hel] = (g_r, g_i)
            for (kind, hel), (g_r, g_i) in acc.items():
                store(kind, hel, col, half, (g_r, g_i))


def plane_kernel(plane, dirs, has_part, n_out, *refs):
    refs = list(refs)
    v_ref = refs.pop(0)
    next_ref = refs.pop(0) if 0 in dirs else None
    u_ref, phi_ref = refs.pop(0), refs.pop(0)
    part_ref = refs.pop(0) if has_part else None
    out_ref = refs.pop(0)
    give_ref = refs.pop(0) if n_out else None
    g_ref, h_ref, sh_ref = refs
    n_h = phi_ref.shape[1]
    _, _, n_b, width = v_ref.shape
    kinds = (g_ref, h_ref)

    def block(step, carry):
        row = pl.multiple_of(step * ROWS, ROWS)
        rows = pl.ds(row, ROWS)
        for slot, direc in enumerate(dirs):
            for part in range(2):
                for col in range(3):
                    source = next_ref if direc == 0 else v_ref
                    field = source[part, col, rows, :].astype(jnp.float32)
                    if direc == 1:
                        field = shift_y(field)
                    elif direc == 2:
                        field = shift_z(field)
                    sh_ref[slot, part, col] = field

        def store(kind, hel, col, half, both):
            for part in range(2):
                there = pl.ds(pl.multiple_of(part * n_b + row, ROWS), ROWS)
                lanes = pl.ds(col * width + half * HALF, HALF)
                kinds[kind][hel, there, lanes] = both[part].astype(jnp.bfloat16)

        weighted_links(u_ref, phi_ref, sh_ref, dirs, plane, n_h, store)
        return carry

    lax.fori_loop(0, n_b // ROWS, block, 0)

    def multiply(hel, carry):
        mat = jnp.concatenate([v_ref[:, col].reshape(2 * n_b, width) for col in range(3)], 1)
        one = dot_nt(mat, g_ref[hel])
        two = dot_nt(h_ref[hel], mat)
        real = one[:n_b, :n_b] + one[n_b:, n_b:] + two[:n_b, :n_b] + two[n_b:, n_b:]
        imag = one[:n_b, n_b:] - one[n_b:, :n_b] + two[:n_b, n_b:] - two[n_b:, :n_b]
        for part, total in enumerate((real, imag)):
            if has_part:
                total = total + part_ref[hel, part]
            if n_out:
                core = lax.axis_index("space") & 1
                halves = total.reshape(n_out // 2, 2, n_b // n_out, n_b)
                out_ref[:, hel, part] = jnp.where(core == 0, halves[:, 0], halves[:, 1])
                give_ref[:, hel, part] = jnp.where(core == 0, halves[:, 1], halves[:, 0]).astype(jnp.bfloat16)
            else:
                out_ref[hel, part] = total
        return carry

    lax.fori_loop(0, n_h, multiply, 0)


def plane_call(plane, dirs, vec, ahead, link, phi, part=None, n_out=0):
    n_h = phi.shape[1]
    _, _, n_b, width = vec.shape
    vmem = pl.BlockSpec(memory_space=pltpu.VMEM)
    args = [vec] + ([ahead] if 0 in dirs else []) + [link, phi]
    args += [part] if part is not None else []
    specs = [vmem] * len(args)
    scratch = [
        pltpu.VMEM((n_h, 2 * n_b, 3 * width), jnp.bfloat16),
        pltpu.VMEM((n_h, 2 * n_b, 3 * width), jnp.bfloat16),
        pltpu.VMEM((len(dirs), 2, 3, ROWS, width), jnp.float32),
    ]
    if n_out:
        blocks = (n_out // 2, n_h, 2, n_b // n_out, n_b)
        out_shape = [
            jax.ShapeDtypeStruct(blocks, jnp.float32),
            jax.ShapeDtypeStruct(blocks, jnp.bfloat16),
        ]
        out_specs = [vmem, vmem]
    else:
        out_shape = jax.ShapeDtypeStruct((n_h, 2, n_b, n_b), jnp.float32)
        out_specs = vmem
    return pl.pallas_call(
        functools.partial(plane_kernel, plane, dirs, part is not None, n_out),
        in_specs=specs,
        out_specs=out_specs,
        out_shape=out_shape,
        scratch_shapes=scratch,
        compiler_params=pltpu.CompilerParams(vmem_limit_bytes=VMEM_BYTES),
        cost_estimate=pl.CostEstimate(
            flops=(16 + 8 * len(dirs)) * n_h * n_b * n_b * 3 * width,
            bytes_accessed=2**22,
            transcendentals=0,
        ),
        name="plane%d_%s" % (plane, "".join(str(direc) for direc in dirs)),
    )(*args)


def merge_kernel(keep_ref, got_ref, own_ref, *out_refs):
    chip = lax.axis_index("space") >> 1
    shape = own_ref.shape
    own_ref[...] = (keep_ref[chip] + got_ref[chip].astype(jnp.float32)).reshape(shape)
    for mask, out_ref in enumerate(out_refs, 1):
        total = keep_ref[chip ^ mask] + got_ref[chip ^ mask].astype(jnp.float32)
        out_ref[...] = total.reshape(shape).astype(jnp.bfloat16)


def merge_call(keep, got):
    chips, n_h, _, own, n_b = keep.shape
    shape = (n_h * 2 * own, n_b)
    vmem = pl.BlockSpec(memory_space=pltpu.VMEM)
    return pl.pallas_call(
        merge_kernel,
        in_specs=[vmem, vmem],
        out_specs=[vmem] * chips,
        out_shape=[jax.ShapeDtypeStruct(shape, jnp.float32)]
        + [jax.ShapeDtypeStruct(shape, jnp.bfloat16)] * (chips - 1),
        compiler_params=pltpu.CompilerParams(vmem_limit_bytes=8 * 2**20),
        name="merge_cores",
    )(keep, got)


def quark_kernel(masks, n_op, n_got, n_h, *refs):
    n_tau = len(masks)
    got_refs = refs[:n_got]
    tau_refs = refs[n_got : n_got + n_tau]
    out_ref, left_ref = refs[n_got + n_tau :]
    my_space, my_op = lax.axis_index("space"), lax.axis_index("op")
    _, n_pair, _, own, n_b = out_ref.shape
    row = lax.broadcasted_iota(jnp.int32, (n_b, 2 * n_b), 0)
    col = lax.broadcasted_iota(jnp.int32, (n_b, 2 * n_b), 1)
    even = (col == 2 * row).astype(jnp.bfloat16)
    odd = (col == 2 * row + 1).astype(jnp.bfloat16)
    total = got_refs[0][...]
    for ref in got_refs[1:]:
        total = total + ref[...].astype(jnp.float32)
    swap = []
    for hel in range(n_h):
        start = hel * 2 * own
        swap += [-total[start + own : start + 2 * own], total[start : start + own]]
    left = jnp.dot(total.astype(jnp.bfloat16), even, preferred_element_type=jnp.float32)
    left += jnp.dot(
        jnp.concatenate(swap, 0).astype(jnp.bfloat16), odd, preferred_element_type=jnp.float32
    )
    left_ref[...] = left.astype(jnp.bfloat16)
    depth = tau_refs[0].shape[0]
    whole = depth == 2 * n_b
    if not whole:
        out_ref[...] = jnp.zeros_like(out_ref)
    for which, (mask, mask_op) in enumerate(masks):
        first = ((my_space ^ mask) * n_op + (my_op ^ mask_op)) * depth
        pair = first // (2 * n_b)
        if whole:
            lhs = left_ref[...]
        else:
            lhs = left_ref[:, pl.ds(pl.multiple_of(first - pair * 2 * n_b, depth), depth)]
        res = jnp.dot(lhs, tau_refs[which][...], preferred_element_type=jnp.float32)
        for hel in range(n_h):
            for part in range(2):
                start = (hel * 2 + part) * own
                if whole:
                    out_ref[hel, pair, part] = res[start : start + own]
                else:
                    out_ref[hel, pair, part] += res[start : start + own]


def phase_kernel(n_op, n_x, planes, *refs):
    mom_refs = refs[:n_op]
    num_refs = refs[n_op : 2 * n_op]
    den_ref, out_ref = refs[2 * n_op :]
    my_space, my_op = lax.axis_index("space"), lax.axis_index("op")
    _, n_h, _, _, _, width = out_ref.shape
    n_mom = mom_refs[0].shape[0]
    moms = [(op, k) for op in range(n_op) for k in range(n_mom)]
    scale = 1.0 / math.sqrt(3.0 * n_x * LY * LZ)
    shape = (planes * len(moms), width)
    row = lax.broadcasted_iota(jnp.int32, shape, 0)
    lane = lax.broadcasted_iota(jnp.int32, shape, 1)
    yy = lane // LZ
    zz = lane & (LZ - 1)

    def spread(values):
        res = jnp.full(shape, values[0], jnp.int32)
        for which in range(1, len(values)):
            res = jnp.where(row == which, values[which], res)
        return res

    comps = [[mom_refs[op][k, axis] for _ in range(planes) for op, k in moms] for axis in range(3)]
    mom_x, mom_y, mom_z = [spread(comp) for comp in comps]
    pos_x = my_space * planes + row // len(moms)
    steps = ((0, 0, 0), (1, 0, 0), (0, 1, 0), (0, 0, 1))
    waves = []
    for step_x, step_y, step_z in steps:
        turn_x = lax.rem(mom_x * (pos_x + step_x), n_x).astype(jnp.float32) * (1.0 / n_x)
        turn_y = ((mom_y * (yy + step_y)) & (LY - 1)).astype(jnp.float32) * (1.0 / LY)
        turn_z = ((mom_z * (zz + step_z)) & (LZ - 1)).astype(jnp.float32) * (1.0 / LZ)
        turn = turn_x + turn_y + turn_z
        theta = (2.0 * math.pi) * (turn - jnp.floor(turn))
        waves.append((jnp.cos(theta), jnp.sin(theta)))
    for hel in range(n_h):
        which_h = my_op * n_h + hel
        den = jnp.full((1, width), den_ref[which_h], jnp.int32).astype(jnp.float32)
        for direc in range(NDIR):
            wts = []
            for op, k in moms:
                num = num_refs[op][direc, k, which_h]
                wts.append(jnp.full((1, width), num, jnp.int32).astype(jnp.float32) / den * scale)
            for kind, wave in ((0, waves[0]), (1, waves[1 + direc])):
                for plane in range(planes):
                    start = plane * len(moms)
                    real = sum(wt * wave[0][start + at : start + at + 1] for at, wt in enumerate(wts))
                    imag = sum(wt * wave[1][start + at : start + at + 1] for at, wt in enumerate(wts))
                    out_ref[kind, hel, direc, 0, plane : plane + 1, :] = -real if kind else real
                    out_ref[kind, hel, direc, 1, plane : plane + 1, :] = -imag


def shards(eigvecs, links, momenta, coef_num, coef_den, peram):
    n_space = lax.axis_size("space")
    n_op = lax.axis_size("op")
    n_tm = lax.axis_size("tm")
    _, _, n_b, _, planes, width = eigvecs.shape
    n_x = planes * n_space
    own = n_b // n_space
    n_h = coef_num.shape[0] // n_op
    my_op = lax.axis_index("op")
    my_space = lax.axis_index("space")

    nums = jnp.transpose(coef_num, (2, 1, 0))
    both = [(momenta, nums)]
    both += [(across(momenta, "op", mask), across(nums, "op", mask)) for mask in range(1, n_op)]

    group = n_space * n_op
    depth = n_b * SPINS // group
    first = (my_space * n_op + my_op) * depth
    piece = lax.dynamic_slice(
        peram.reshape(n_b, SPINS, 2, n_b), (first % n_b, first // n_b, 0, 0), (depth, 1, 2, n_b)
    ).reshape(depth * 2, n_b)
    eigvecs, piece, both = lax.optimization_barrier((eigvecs, piece, both))
    own_piece = from_behind(piece, "tm", n_tm - 1)

    vecs = [jnp.transpose(eigvecs[0, :, :, :, plane, :], (0, 2, 1, 3)) for plane in range(planes)]
    upper = from_behind(vecs[0], "space", -1)

    smem = pl.BlockSpec(memory_space=pltpu.SMEM)
    vmem = pl.BlockSpec(memory_space=pltpu.VMEM)
    phi = pl.pallas_call(
        functools.partial(phase_kernel, n_op, n_x, planes),
        in_specs=[smem] * (2 * n_op + 1),
        out_specs=vmem,
        out_shape=jax.ShapeDtypeStruct((2, n_h, NDIR, 2, planes, width), jnp.float32),
        compiler_params=pltpu.CompilerParams(vmem_limit_bytes=4 * 2**20),
        name="phases",
    )(*[mom for mom, _ in both], *[num for _, num in both], coef_den)

    dims = [("op", 1 << bit) for bit in range(n_op.bit_length() - 1)]
    dims += [("space", 1 << bit) for bit in range(1, n_space.bit_length() - 1)]
    load = [0] * len(dims)

    def stage(held, size):
        for group_dims in itertools.combinations(range(len(dims)), size):
            dim = min(group_dims, key=lambda at: load[at])
            load[dim] += 1
            before = held[tuple(at for at in group_dims if at != dim)]
            held[group_dims] = across(before, *dims[dim])

    def hold(held, other):
        arrs, other = lax.optimization_barrier((list(held.values()), other))
        return dict(zip(held.keys(), arrs)), other

    link = links[0]
    last = planes - 1
    partial = plane_call(last, (1, 2), vecs[last], None, link, phi)
    held, partial = hold({(): own_piece}, partial)
    stage(held, 1)
    for plane in range(last):
        partial = plane_call(plane, (1, 2, 0), vecs[plane], vecs[plane + 1], link, phi, partial)
    held, partial = hold(held, partial)
    ready = dict(held)
    stage(held, 2)
    keep, give = plane_call(last, (0,), vecs[last], upper, link, phi, partial, n_space)
    swapped = across(give, "space", 1)
    held, keep = hold(held, keep)
    for size in range(3, len(dims) + 1):
        stage(held, size)
    merged = merge_call(keep, swapped)
    got = [merged[0]] + [across(arr, "space", 2 * mask) for mask, arr in enumerate(merged[1:], 1)]
    tau, masks = [], []
    for flip in range(2):
        for group_dims, arr in held.items():
            mask = {"space": flip, "op": 0}
            for at in group_dims:
                mask[dims[at][0]] ^= dims[at][1]
            tau.append(across(ready.get(group_dims, arr), "space", 1) if flip else arr)
            masks.append((mask["space"], mask["op"]))

    lines = pl.pallas_call(
        functools.partial(quark_kernel, masks, n_op, len(got), n_h),
        in_specs=[vmem] * (len(got) + len(tau)),
        out_specs=vmem,
        out_shape=jax.ShapeDtypeStruct((n_h, SPINS, 2, own, n_b), jnp.float32),
        scratch_shapes=[
            pltpu.VMEM((n_h * 2 * own, 2 * n_b), jnp.bfloat16),
        ],
        compiler_params=pltpu.CompilerParams(vmem_limit_bytes=VMEM_BYTES),
        cost_estimate=pl.CostEstimate(
            flops=2 * SPINS * n_h * 2 * own * 2 * n_b * n_b, bytes_accessed=7 * 2**20, transcendentals=0
        ),
        name="quark_products",
    )(*got, *tau)
    return lines.reshape(1, n_h, 4, 4, 2, own, n_b)


def solution(mesh):
    return jax.shard_map(
        shards,
        mesh=mesh,
        in_specs=(
            P("tm", None, None, None, "space", None),
            P("tm", None, None, None, None, "space", None),
            P("op", None),
            P(None, "op", None),
            P(),
            P("tm", None, None, None, None, None),
        ),
        out_specs=P("tm", "op", None, None, None, "space", None),
        check_vma=False,
    )
```

```python
import functools
import itertools
import math

import jax
import jax.numpy as jnp
from jax import lax
from jax.experimental import pallas as pl
from jax.experimental.pallas import tpu as pltpu
from jax.sharding import PartitionSpec as P

LY = 32
LZ = 8
NDIR = 3
SPINS = 16
ROWS = 16
HALF = 128
VMEM_BYTES = 20 * 2**20


def from_behind(value, axis, steps):
    count = lax.axis_size(axis)
    pairs = [(source, (source + steps) % count) for source in range(count)]
    return lax.ppermute(value, axis, pairs)


def across(value, axis, mask):
    pairs = [(source, source ^ mask) for source in range(lax.axis_size(axis))]
    return lax.ppermute(value, axis, pairs)


def dot_nt(left, right):
    return lax.dot_general(
        left, right, (((1,), (1,)), ((), ())), preferred_element_type=jnp.float32
    )


def shift_y(arr):
    return pltpu.roll(arr, arr.shape[1] - LZ, 1)


def shift_z(arr):
    width = arr.shape[1]
    lane = lax.broadcasted_iota(jnp.int32, arr.shape, 1)
    near = pltpu.roll(arr, width - 1, 1)
    far = pltpu.roll(arr, LZ - 1, 1)
    return jnp.where((lane & (LZ - 1)) == LZ - 1, far, near)


def weighted_links(u_ref, phi_ref, shifted, dirs, plane, n_h, store):
    width = u_ref.shape[-1]
    for half in range(width // HALF):
        lanes = pl.ds(half * HALF, HALF)
        for col in range(3):
            acc = {}
            for slot, direc in enumerate(dirs):
                f_r = None
                f_i = None
                for col_two in range(3):
                    u_r = u_ref[direc, col, col_two, 0, pl.ds(plane, 1), lanes]
                    u_i = u_ref[direc, col, col_two, 1, pl.ds(plane, 1), lanes]
                    v_r = shifted[slot, 0, col_two, :, lanes]
                    v_i = shifted[slot, 1, col_two, :, lanes]
                    term_r = u_r * v_r - u_i * v_i
                    term_i = u_r * v_i + u_i * v_r
                    f_r = term_r if f_r is None else f_r + term_r
                    f_i = term_i if f_i is None else f_i + term_i
                for kind in range(2):
                    for hel in range(n_h):
                        p_r = phi_ref[kind, hel, direc, 0, pl.ds(plane, 1), lanes]
                        p_i = phi_ref[kind, hel, direc, 1, pl.ds(plane, 1), lanes]
                        g_r = p_r * f_r - p_i * f_i
                        g_i = p_r * f_i + p_i * f_r
                        if (kind, hel) in acc:
                            old_r, old_i = acc[kind, hel]
                            g_r, g_i = old_r + g_r, old_i + g_i
                        acc[kind, hel] = (g_r, g_i)
            for (kind, hel), (g_r, g_i) in acc.items():
                store(kind, hel, col, half, (g_r, g_i))


def plane_kernel(plane, dirs, has_part, n_out, *refs):
    refs = list(refs)
    v_ref = refs.pop(0)
    next_ref = refs.pop(0) if 0 in dirs else None
    u_ref, phi_ref = refs.pop(0), refs.pop(0)
    part_ref = refs.pop(0) if has_part else None
    out_ref = refs.pop(0)
    give_ref = refs.pop(0) if n_out else None
    g_ref, h_ref, sh_ref = refs
    n_h = phi_ref.shape[1]
    _, _, n_b, width = v_ref.shape
    kinds = (g_ref, h_ref)

    def block(step, carry):
        row = pl.multiple_of(step * ROWS, ROWS)
        rows = pl.ds(row, ROWS)
        for slot, direc in enumerate(dirs):
            for part in range(2):
                for col in range(3):
                    source = next_ref if direc == 0 else v_ref
                    field = source[part, col, rows, :].astype(jnp.float32)
                    if direc == 1:
                        field = shift_y(field)
                    elif direc == 2:
                        field = shift_z(field)
                    sh_ref[slot, part, col] = field

        def store(kind, hel, col, half, both):
            for part in range(2):
                there = pl.ds(pl.multiple_of(part * n_b + row, ROWS), ROWS)
                lanes = pl.ds(col * width + half * HALF, HALF)
                kinds[kind][hel, there, lanes] = both[part].astype(jnp.bfloat16)

        weighted_links(u_ref, phi_ref, sh_ref, dirs, plane, n_h, store)
        return carry

    lax.fori_loop(0, n_b // ROWS, block, 0)

    def multiply(hel, carry):
        mat = jnp.concatenate([v_ref[:, col].reshape(2 * n_b, width) for col in range(3)], 1)
        one = dot_nt(mat, g_ref[hel])
        two = dot_nt(h_ref[hel], mat)
        real = one[:n_b, :n_b] + one[n_b:, n_b:] + two[:n_b, :n_b] + two[n_b:, n_b:]
        imag = one[:n_b, n_b:] - one[n_b:, :n_b] + two[:n_b, n_b:] - two[n_b:, :n_b]
        for part, total in enumerate((real, imag)):
            if has_part:
                total = total + part_ref[hel, part]
            if n_out:
                core = lax.axis_index("space") & 1
                halves = total.reshape(n_out // 2, 2, n_b // n_out, n_b)
                out_ref[:, hel, part] = jnp.where(core == 0, halves[:, 0], halves[:, 1])
                give_ref[:, hel, part] = jnp.where(core == 0, halves[:, 1], halves[:, 0]).astype(jnp.bfloat16)
            else:
                out_ref[hel, part] = total
        return carry

    lax.fori_loop(0, n_h, multiply, 0)


def plane_call(plane, dirs, vec, ahead, link, phi, part=None, n_out=0):
    n_h = phi.shape[1]
    _, _, n_b, width = vec.shape
    vmem = pl.BlockSpec(memory_space=pltpu.VMEM)
    args = [vec] + ([ahead] if 0 in dirs else []) + [link, phi]
    args += [part] if part is not None else []
    specs = [vmem] * len(args)
    scratch = [
        pltpu.VMEM((n_h, 2 * n_b, 3 * width), jnp.bfloat16),
        pltpu.VMEM((n_h, 2 * n_b, 3 * width), jnp.bfloat16),
        pltpu.VMEM((len(dirs), 2, 3, ROWS, width), jnp.float32),
    ]
    if n_out:
        blocks = (n_out // 2, n_h, 2, n_b // n_out, n_b)
        out_shape = [
            jax.ShapeDtypeStruct(blocks, jnp.float32),
            jax.ShapeDtypeStruct(blocks, jnp.bfloat16),
        ]
        out_specs = [vmem, vmem]
    else:
        out_shape = jax.ShapeDtypeStruct((n_h, 2, n_b, n_b), jnp.float32)
        out_specs = vmem
    return pl.pallas_call(
        functools.partial(plane_kernel, plane, dirs, part is not None, n_out),
        in_specs=specs,
        out_specs=out_specs,
        out_shape=out_shape,
        scratch_shapes=scratch,
        compiler_params=pltpu.CompilerParams(vmem_limit_bytes=VMEM_BYTES),
        cost_estimate=pl.CostEstimate(
            flops=(16 + 8 * len(dirs)) * n_h * n_b * n_b * 3 * width,
            bytes_accessed=2**22,
            transcendentals=0,
        ),
        name="plane%d_%s" % (plane, "".join(str(direc) for direc in dirs)),
    )(*args)


def merge_kernel(n_early, keep_ref, got_ref, *refs):
    early_refs = refs[:n_early]
    pack_ref, own_ref = refs[n_early : n_early + 2]
    chip = lax.axis_index("space") >> 1
    shape = own_ref.shape
    own_ref[...] = (keep_ref[chip] + got_ref[chip].astype(jnp.float32)).reshape(shape)
    for mask, out_ref in enumerate(refs[n_early + 2 :], 1):
        total = keep_ref[chip ^ mask] + got_ref[chip ^ mask].astype(jnp.float32)
        out_ref[...] = total.reshape(shape).astype(jnp.bfloat16)
    for which, ref in enumerate(early_refs):
        pack_ref[which] = ref[...]


def merge_call(keep, got, early):
    chips, n_h, _, own, n_b = keep.shape
    shape = (n_h * 2 * own, n_b)
    vmem = pl.BlockSpec(memory_space=pltpu.VMEM)
    out = pl.pallas_call(
        functools.partial(merge_kernel, len(early)),
        in_specs=[vmem] * (2 + len(early)),
        out_specs=[vmem] * (1 + chips),
        out_shape=[
            jax.ShapeDtypeStruct((len(early),) + early[0].shape, jnp.bfloat16),
            jax.ShapeDtypeStruct(shape, jnp.float32),
        ]
        + [jax.ShapeDtypeStruct(shape, jnp.bfloat16)] * (chips - 1),
        compiler_params=pltpu.CompilerParams(vmem_limit_bytes=8 * 2**20),
        cost_estimate=pl.CostEstimate(flops=2**16, bytes_accessed=2**12, transcendentals=0),
        name="merge_cores",
    )(keep, got, *early)
    return out[0], out[1:]


def quark_kernel(masks, n_op, n_got, n_tau, n_h, *refs):
    got_refs = refs[:n_got]
    tau_refs = refs[n_got : n_got + n_tau]
    out_ref, left_ref = refs[n_got + n_tau :]
    my_space, my_op = lax.axis_index("space"), lax.axis_index("op")
    _, n_pair, _, own, n_b = out_ref.shape
    row = lax.broadcasted_iota(jnp.int32, (n_b, 2 * n_b), 0)
    col = lax.broadcasted_iota(jnp.int32, (n_b, 2 * n_b), 1)
    even = (col == 2 * row).astype(jnp.bfloat16)
    odd = (col == 2 * row + 1).astype(jnp.bfloat16)
    total = got_refs[0][...]
    for ref in got_refs[1:]:
        total = total + ref[...].astype(jnp.float32)
    swap = []
    for hel in range(n_h):
        start = hel * 2 * own
        swap += [-total[start + own : start + 2 * own], total[start : start + own]]
    left = jnp.dot(total.astype(jnp.bfloat16), even, preferred_element_type=jnp.float32)
    left += jnp.dot(
        jnp.concatenate(swap, 0).astype(jnp.bfloat16), odd, preferred_element_type=jnp.float32
    )
    left_ref[...] = left.astype(jnp.bfloat16)
    tau = []
    for ref in tau_refs:
        tau += [ref.at[which] for which in range(ref.shape[0])] if len(ref.shape) == 3 else [ref]
    depth = tau[0].shape[0]
    whole = depth == 2 * n_b
    if not whole:
        out_ref[...] = jnp.zeros_like(out_ref)
    for which, (mask, mask_op) in enumerate(masks):
        first = ((my_space ^ mask) * n_op + (my_op ^ mask_op)) * depth
        pair = first // (2 * n_b)
        if whole:
            lhs = left_ref[...]
        else:
            lhs = left_ref[:, pl.ds(pl.multiple_of(first - pair * 2 * n_b, depth), depth)]
        res = jnp.dot(lhs, tau[which][...], preferred_element_type=jnp.float32)
        for hel in range(n_h):
            for part in range(2):
                start = (hel * 2 + part) * own
                if whole:
                    out_ref[hel, pair, part] = res[start : start + own]
                else:
                    out_ref[hel, pair, part] += res[start : start + own]


def phase_kernel(n_op, n_x, planes, *refs):
    mom_refs = refs[:n_op]
    num_refs = refs[n_op : 2 * n_op]
    den_ref, out_ref = refs[2 * n_op :]
    my_space, my_op = lax.axis_index("space"), lax.axis_index("op")
    _, n_h, _, _, _, width = out_ref.shape
    n_mom = mom_refs[0].shape[0]
    moms = [(op, k) for op in range(n_op) for k in range(n_mom)]
    scale = 1.0 / math.sqrt(3.0 * n_x * LY * LZ)
    shape = (planes * len(moms), width)
    row = lax.broadcasted_iota(jnp.int32, shape, 0)
    lane = lax.broadcasted_iota(jnp.int32, shape, 1)
    yy = lane // LZ
    zz = lane & (LZ - 1)

    def spread(values):
        res = jnp.full(shape, values[0], jnp.int32)
        for which in range(1, len(values)):
            res = jnp.where(row == which, values[which], res)
        return res

    comps = [[mom_refs[op][k, axis] for _ in range(planes) for op, k in moms] for axis in range(3)]
    mom_x, mom_y, mom_z = [spread(comp) for comp in comps]
    pos_x = my_space * planes + row // len(moms)
    steps = ((0, 0, 0), (1, 0, 0), (0, 1, 0), (0, 0, 1))
    waves = []
    for step_x, step_y, step_z in steps:
        turn_x = lax.rem(mom_x * (pos_x + step_x), n_x).astype(jnp.float32) * (1.0 / n_x)
        turn_y = ((mom_y * (yy + step_y)) & (LY - 1)).astype(jnp.float32) * (1.0 / LY)
        turn_z = ((mom_z * (zz + step_z)) & (LZ - 1)).astype(jnp.float32) * (1.0 / LZ)
        turn = turn_x + turn_y + turn_z
        theta = (2.0 * math.pi) * (turn - jnp.floor(turn))
        waves.append((jnp.cos(theta), jnp.sin(theta)))
    for hel in range(n_h):
        which_h = my_op * n_h + hel
        den = jnp.full((1, width), den_ref[which_h], jnp.int32).astype(jnp.float32)
        for direc in range(NDIR):
            wts = []
            for op, k in moms:
                num = num_refs[op][direc, k, which_h]
                wts.append(jnp.full((1, width), num, jnp.int32).astype(jnp.float32) / den * scale)
            for kind, wave in ((0, waves[0]), (1, waves[1 + direc])):
                for plane in range(planes):
                    start = plane * len(moms)
                    real = sum(wt * wave[0][start + at : start + at + 1] for at, wt in enumerate(wts))
                    imag = sum(wt * wave[1][start + at : start + at + 1] for at, wt in enumerate(wts))
                    out_ref[kind, hel, direc, 0, plane : plane + 1, :] = -real if kind else real
                    out_ref[kind, hel, direc, 1, plane : plane + 1, :] = -imag


def shards(eigvecs, links, momenta, coef_num, coef_den, peram):
    n_space = lax.axis_size("space")
    n_op = lax.axis_size("op")
    n_tm = lax.axis_size("tm")
    _, _, n_b, _, planes, width = eigvecs.shape
    n_x = planes * n_space
    own = n_b // n_space
    n_h = coef_num.shape[0] // n_op
    my_op = lax.axis_index("op")
    my_space = lax.axis_index("space")

    nums = jnp.transpose(coef_num, (2, 1, 0))
    both = [(momenta, nums)]
    both += [(across(momenta, "op", mask), across(nums, "op", mask)) for mask in range(1, n_op)]

    group = n_space * n_op
    depth = n_b * SPINS // group
    first = (my_space * n_op + my_op) * depth
    piece = lax.dynamic_slice(
        peram.reshape(n_b, SPINS, 2, n_b), (first % n_b, first // n_b, 0, 0), (depth, 1, 2, n_b)
    ).reshape(depth * 2, n_b)

    moved = lax.optimization_barrier(jnp.transpose(eigvecs[0], (3, 0, 2, 1, 4)))
    moved, piece, both = lax.optimization_barrier((moved, piece, both))
    own_piece = from_behind(piece, "tm", n_tm - 1)
    vecs = [moved[plane] for plane in range(planes)]
    upper = from_behind(vecs[0], "space", -1)

    smem = pl.BlockSpec(memory_space=pltpu.SMEM)
    vmem = pl.BlockSpec(memory_space=pltpu.VMEM)
    phi = pl.pallas_call(
        functools.partial(phase_kernel, n_op, n_x, planes),
        in_specs=[smem] * (2 * n_op + 1),
        out_specs=vmem,
        out_shape=jax.ShapeDtypeStruct((2, n_h, NDIR, 2, planes, width), jnp.float32),
        compiler_params=pltpu.CompilerParams(vmem_limit_bytes=4 * 2**20),
        name="phases",
    )(*[mom for mom, _ in both], *[num for _, num in both], coef_den)

    dims = [("op", 1 << bit) for bit in range(n_op.bit_length() - 1)]
    dims += [("space", 1 << bit) for bit in range(1, n_space.bit_length() - 1)]
    load = [0] * len(dims)

    def stage(held, size):
        for group_dims in itertools.combinations(range(len(dims)), size):
            dim = min(group_dims, key=lambda at: load[at])
            load[dim] += 1
            before = held[tuple(at for at in group_dims if at != dim)]
            held[group_dims] = across(before, *dims[dim])

    def hold(held, other):
        arrs, other = lax.optimization_barrier((list(held.values()), other))
        return dict(zip(held.keys(), arrs)), other

    link = links[0]
    last = planes - 1
    partial = plane_call(last, (1, 2), vecs[last], None, link, phi)
    held, partial = hold({(): own_piece}, partial)
    stage(held, 1)
    for plane in range(last):
        partial = plane_call(plane, (1, 2, 0), vecs[plane], vecs[plane + 1], link, phi, partial)
    held, partial = hold(held, partial)
    stage(held, 2)
    keep, give = plane_call(last, (0,), vecs[last], upper, link, phi, partial, n_space)
    swapped = across(give, "space", 1)
    held, keep = hold(held, keep)
    for size in range(3, len(dims) + 1):
        stage(held, size)
    early = [key for key in held if len(key) < 3]
    late = [key for key in held if len(key) >= 3]
    packed, merged = merge_call(keep, swapped, [held[key] for key in early])
    got = [merged[0]] + [across(arr, "space", 2 * mask) for mask, arr in enumerate(merged[1:], 1)]
    last_held, got = hold({key: held[key] for key in late}, got)
    held.update(last_held)
    tau = [held[key] for key in early + late]
    tau += [across(packed, "space", 1)] + [across(held[key], "space", 1) for key in late]
    masks = []
    for flip in range(2):
        for group_dims in early + late:
            mask = {"space": flip, "op": 0}
            for at in group_dims:
                mask[dims[at][0]] ^= dims[at][1]
            masks.append((mask["space"], mask["op"]))

    lines = pl.pallas_call(
        functools.partial(quark_kernel, masks, n_op, len(got), len(tau), n_h),
        in_specs=[vmem] * (len(got) + len(tau)),
        out_specs=vmem,
        out_shape=jax.ShapeDtypeStruct((n_h, SPINS, 2, own, n_b), jnp.float32),
        scratch_shapes=[
            pltpu.VMEM((n_h * 2 * own, 2 * n_b), jnp.bfloat16),
        ],
        compiler_params=pltpu.CompilerParams(vmem_limit_bytes=VMEM_BYTES),
        cost_estimate=pl.CostEstimate(
            flops=2 * SPINS * n_h * 2 * own * 2 * n_b * n_b, bytes_accessed=7 * 2**20, transcendentals=0
        ),
        name="quark_products",
    )(*got, *tau)
    return lines.reshape(1, n_h, 4, 4, 2, own, n_b)


def solution(mesh):
    return jax.shard_map(
        shards,
        mesh=mesh,
        in_specs=(
            P("tm", None, None, None, "space", None),
            P("tm", None, None, None, None, "space", None),
            P("op", None),
            P(None, "op", None),
            P(),
            P("tm", None, None, None, None, None),
        ),
        out_specs=P("tm", "op", None, None, None, "space", None),
        check_vma=False,
    )
```

```python
import functools
import itertools
import math

import jax
import jax.numpy as jnp
from jax import lax
from jax.experimental import pallas as pl
from jax.experimental.pallas import tpu as pltpu
from jax.sharding import PartitionSpec as P

LY = 32
LZ = 8
NDIR = 3
SPINS = 16
ROWS = 16
HALF = 128
VMEM_BYTES = 20 * 2**20


def from_behind(value, axis, steps):
    count = lax.axis_size(axis)
    pairs = [(source, (source + steps) % count) for source in range(count)]
    return lax.ppermute(value, axis, pairs)


def across(value, axis, mask):
    pairs = [(source, source ^ mask) for source in range(lax.axis_size(axis))]
    return lax.ppermute(value, axis, pairs)


def dot_nt(left, right):
    return lax.dot_general(
        left, right, (((1,), (1,)), ((), ())), preferred_element_type=jnp.float32
    )


def shift_y(arr):
    return pltpu.roll(arr, arr.shape[1] - LZ, 1)


def shift_z(arr):
    width = arr.shape[1]
    lane = lax.broadcasted_iota(jnp.int32, arr.shape, 1)
    near = pltpu.roll(arr, width - 1, 1)
    far = pltpu.roll(arr, LZ - 1, 1)
    return jnp.where((lane & (LZ - 1)) == LZ - 1, far, near)


def weighted_links(u_ref, phi_ref, shifted, dirs, plane, n_h, store):
    width = u_ref.shape[-1]
    for half in range(width // HALF):
        lanes = pl.ds(half * HALF, HALF)
        for col in range(3):
            acc = {}
            for slot, direc in enumerate(dirs):
                f_r = None
                f_i = None
                for col_two in range(3):
                    u_r = u_ref[direc, col, col_two, 0, pl.ds(plane, 1), lanes]
                    u_i = u_ref[direc, col, col_two, 1, pl.ds(plane, 1), lanes]
                    v_r = shifted[slot, 0, col_two, :, lanes]
                    v_i = shifted[slot, 1, col_two, :, lanes]
                    term_r = u_r * v_r - u_i * v_i
                    term_i = u_r * v_i + u_i * v_r
                    f_r = term_r if f_r is None else f_r + term_r
                    f_i = term_i if f_i is None else f_i + term_i
                for kind in range(2):
                    for hel in range(n_h):
                        p_r = phi_ref[kind, hel, direc, 0, pl.ds(plane, 1), lanes]
                        p_i = phi_ref[kind, hel, direc, 1, pl.ds(plane, 1), lanes]
                        g_r = p_r * f_r - p_i * f_i
                        g_i = p_r * f_i + p_i * f_r
                        if (kind, hel) in acc:
                            old_r, old_i = acc[kind, hel]
                            g_r, g_i = old_r + g_r, old_i + g_i
                        acc[kind, hel] = (g_r, g_i)
            for (kind, hel), (g_r, g_i) in acc.items():
                store(kind, hel, col, half, (g_r, g_i))


def plane_kernel(plane, dirs, has_part, n_out, *refs):
    refs = list(refs)
    v_ref = refs.pop(0)
    next_ref = refs.pop(0) if 0 in dirs else None
    u_ref, phi_ref = refs.pop(0), refs.pop(0)
    part_ref = refs.pop(0) if has_part else None
    out_ref = refs.pop(0)
    give_ref = refs.pop(0) if n_out else None
    g_ref, h_ref, sh_ref = refs
    n_h = phi_ref.shape[1]
    _, _, n_b, width = v_ref.shape
    kinds = (g_ref, h_ref)

    def block(step, carry):
        row = pl.multiple_of(step * ROWS, ROWS)
        rows = pl.ds(row, ROWS)
        for slot, direc in enumerate(dirs):
            for part in range(2):
                for col in range(3):
                    source = next_ref if direc == 0 else v_ref
                    field = source[part, col, rows, :].astype(jnp.float32)
                    if direc == 1:
                        field = shift_y(field)
                    elif direc == 2:
                        field = shift_z(field)
                    sh_ref[slot, part, col] = field

        def store(kind, hel, col, half, both):
            for part in range(2):
                there = pl.ds(pl.multiple_of(part * n_b + row, ROWS), ROWS)
                lanes = pl.ds(col * width + half * HALF, HALF)
                kinds[kind][hel, there, lanes] = both[part].astype(jnp.bfloat16)

        weighted_links(u_ref, phi_ref, sh_ref, dirs, plane, n_h, store)
        return carry

    lax.fori_loop(0, n_b // ROWS, block, 0)

    def multiply(hel, carry):
        mat = jnp.concatenate([v_ref[:, col].reshape(2 * n_b, width) for col in range(3)], 1)
        one = dot_nt(mat, g_ref[hel])
        two = dot_nt(h_ref[hel], mat)
        real = one[:n_b, :n_b] + one[n_b:, n_b:] + two[:n_b, :n_b] + two[n_b:, n_b:]
        imag = one[:n_b, n_b:] - one[n_b:, :n_b] + two[:n_b, n_b:] - two[n_b:, :n_b]
        for part, total in enumerate((real, imag)):
            if has_part:
                total = total + part_ref[hel, part]
            if n_out:
                core = lax.axis_index("space") & 1
                halves = total.reshape(n_out // 2, 2, n_b // n_out, n_b)
                out_ref[:, hel, part] = jnp.where(core == 0, halves[:, 0], halves[:, 1])
                give_ref[:, hel, part] = jnp.where(core == 0, halves[:, 1], halves[:, 0]).astype(jnp.bfloat16)
            else:
                out_ref[hel, part] = total
        return carry

    lax.fori_loop(0, n_h, multiply, 0)


def plane_call(plane, dirs, vec, ahead, link, phi, part=None, n_out=0):
    n_h = phi.shape[1]
    _, _, n_b, width = vec.shape
    vmem = pl.BlockSpec(memory_space=pltpu.VMEM)
    args = [vec] + ([ahead] if 0 in dirs else []) + [link, phi]
    args += [part] if part is not None else []
    specs = [vmem] * len(args)
    scratch = [
        pltpu.VMEM((n_h, 2 * n_b, 3 * width), jnp.bfloat16),
        pltpu.VMEM((n_h, 2 * n_b, 3 * width), jnp.bfloat16),
        pltpu.VMEM((len(dirs), 2, 3, ROWS, width), jnp.float32),
    ]
    if n_out:
        blocks = (n_out // 2, n_h, 2, n_b // n_out, n_b)
        out_shape = [
            jax.ShapeDtypeStruct(blocks, jnp.float32),
            jax.ShapeDtypeStruct(blocks, jnp.bfloat16),
        ]
        out_specs = [vmem, vmem]
    else:
        out_shape = jax.ShapeDtypeStruct((n_h, 2, n_b, n_b), jnp.float32)
        out_specs = vmem
    return pl.pallas_call(
        functools.partial(plane_kernel, plane, dirs, part is not None, n_out),
        in_specs=specs,
        out_specs=out_specs,
        out_shape=out_shape,
        scratch_shapes=scratch,
        compiler_params=pltpu.CompilerParams(vmem_limit_bytes=VMEM_BYTES),
        cost_estimate=pl.CostEstimate(
            flops=(16 + 8 * len(dirs)) * n_h * n_b * n_b * 3 * width,
            bytes_accessed=2**22,
            transcendentals=0,
        ),
        name="plane%d_%s" % (plane, "".join(str(direc) for direc in dirs)),
    )(*args)


def merge_kernel(keep_ref, got_ref, own_ref, *out_refs):
    chip = lax.axis_index("space") >> 1
    shape = own_ref.shape
    own_ref[...] = (keep_ref[chip] + got_ref[chip].astype(jnp.float32)).reshape(shape)
    for mask, out_ref in enumerate(out_refs, 1):
        total = keep_ref[chip ^ mask] + got_ref[chip ^ mask].astype(jnp.float32)
        out_ref[...] = total.reshape(shape).astype(jnp.bfloat16)


def merge_call(keep, got):
    chips, n_h, _, own, n_b = keep.shape
    shape = (n_h * 2 * own, n_b)
    vmem = pl.BlockSpec(memory_space=pltpu.VMEM)
    return pl.pallas_call(
        merge_kernel,
        in_specs=[vmem, vmem],
        out_specs=[vmem] * chips,
        out_shape=[jax.ShapeDtypeStruct(shape, jnp.float32)]
        + [jax.ShapeDtypeStruct(shape, jnp.bfloat16)] * (chips - 1),
        compiler_params=pltpu.CompilerParams(vmem_limit_bytes=8 * 2**20),
        cost_estimate=pl.CostEstimate(flops=2**16, bytes_accessed=2**12, transcendentals=0),
        name="merge_cores",
    )(keep, got)


def pack_kernel(*refs):
    for which, ref in enumerate(refs[:-1]):
        refs[-1][which] = ref[...]


def pack_call(arrs):
    vmem = pl.BlockSpec(memory_space=pltpu.VMEM)
    return pl.pallas_call(
        pack_kernel,
        in_specs=[vmem] * len(arrs),
        out_specs=vmem,
        out_shape=jax.ShapeDtypeStruct((len(arrs),) + arrs[0].shape, arrs[0].dtype),
        compiler_params=pltpu.CompilerParams(vmem_limit_bytes=8 * 2**20),
        cost_estimate=pl.CostEstimate(flops=2**16, bytes_accessed=2**12, transcendentals=0),
        name="pack_pieces",
    )(*arrs)


def quark_kernel(masks, n_op, n_got, n_tau, n_h, *refs):
    got_refs = refs[:n_got]
    tau_refs = refs[n_got : n_got + n_tau]
    out_ref, left_ref = refs[n_got + n_tau :]
    my_space, my_op = lax.axis_index("space"), lax.axis_index("op")
    _, n_pair, _, own, n_b = out_ref.shape
    row = lax.broadcasted_iota(jnp.int32, (n_b, 2 * n_b), 0)
    col = lax.broadcasted_iota(jnp.int32, (n_b, 2 * n_b), 1)
    even = (col == 2 * row).astype(jnp.bfloat16)
    odd = (col == 2 * row + 1).astype(jnp.bfloat16)
    total = got_refs[0][...]
    for ref in got_refs[1:]:
        total = total + ref[...].astype(jnp.float32)
    swap = []
    for hel in range(n_h):
        start = hel * 2 * own
        swap += [-total[start + own : start + 2 * own], total[start : start + own]]
    left = jnp.dot(total.astype(jnp.bfloat16), even, preferred_element_type=jnp.float32)
    left += jnp.dot(
        jnp.concatenate(swap, 0).astype(jnp.bfloat16), odd, preferred_element_type=jnp.float32
    )
    left_ref[...] = left.astype(jnp.bfloat16)
    tau = []
    for ref in tau_refs:
        tau += [ref.at[which] for which in range(ref.shape[0])] if len(ref.shape) == 3 else [ref]
    depth = tau[0].shape[0]
    whole = depth == 2 * n_b
    if not whole:
        out_ref[...] = jnp.zeros_like(out_ref)
    for which, (mask, mask_op) in enumerate(masks):
        first = ((my_space ^ mask) * n_op + (my_op ^ mask_op)) * depth
        pair = first // (2 * n_b)
        if whole:
            lhs = left_ref[...]
        else:
            lhs = left_ref[:, pl.ds(pl.multiple_of(first - pair * 2 * n_b, depth), depth)]
        res = jnp.dot(lhs, tau[which][...], preferred_element_type=jnp.float32)
        for hel in range(n_h):
            for part in range(2):
                start = (hel * 2 + part) * own
                if whole:
                    out_ref[hel, pair, part] = res[start : start + own]
                else:
                    out_ref[hel, pair, part] += res[start : start + own]


def phase_kernel(n_op, n_x, planes, *refs):
    mom_refs = refs[:n_op]
    num_refs = refs[n_op : 2 * n_op]
    den_ref, out_ref = refs[2 * n_op :]
    my_space, my_op = lax.axis_index("space"), lax.axis_index("op")
    _, n_h, _, _, _, width = out_ref.shape
    n_mom = mom_refs[0].shape[0]
    moms = [(op, k) for op in range(n_op) for k in range(n_mom)]
    scale = 1.0 / math.sqrt(3.0 * n_x * LY * LZ)
    shape = (planes * len(moms), width)
    row = lax.broadcasted_iota(jnp.int32, shape, 0)
    lane = lax.broadcasted_iota(jnp.int32, shape, 1)
    yy = lane // LZ
    zz = lane & (LZ - 1)

    def spread(values):
        res = jnp.full(shape, values[0], jnp.int32)
        for which in range(1, len(values)):
            res = jnp.where(row == which, values[which], res)
        return res

    comps = [[mom_refs[op][k, axis] for _ in range(planes) for op, k in moms] for axis in range(3)]
    mom_x, mom_y, mom_z = [spread(comp) for comp in comps]
    pos_x = my_space * planes + row // len(moms)
    steps = ((0, 0, 0), (1, 0, 0), (0, 1, 0), (0, 0, 1))
    waves = []
    for step_x, step_y, step_z in steps:
        turn_x = lax.rem(mom_x * (pos_x + step_x), n_x).astype(jnp.float32) * (1.0 / n_x)
        turn_y = ((mom_y * (yy + step_y)) & (LY - 1)).astype(jnp.float32) * (1.0 / LY)
        turn_z = ((mom_z * (zz + step_z)) & (LZ - 1)).astype(jnp.float32) * (1.0 / LZ)
        turn = turn_x + turn_y + turn_z
        theta = (2.0 * math.pi) * (turn - jnp.floor(turn))
        waves.append((jnp.cos(theta), jnp.sin(theta)))
    for hel in range(n_h):
        which_h = my_op * n_h + hel
        den = jnp.full((1, width), den_ref[which_h], jnp.int32).astype(jnp.float32)
        for direc in range(NDIR):
            wts = []
            for op, k in moms:
                num = num_refs[op][direc, k, which_h]
                wts.append(jnp.full((1, width), num, jnp.int32).astype(jnp.float32) / den * scale)
            for kind, wave in ((0, waves[0]), (1, waves[1 + direc])):
                for plane in range(planes):
                    start = plane * len(moms)
                    real = sum(wt * wave[0][start + at : start + at + 1] for at, wt in enumerate(wts))
                    imag = sum(wt * wave[1][start + at : start + at + 1] for at, wt in enumerate(wts))
                    out_ref[kind, hel, direc, 0, plane : plane + 1, :] = -real if kind else real
                    out_ref[kind, hel, direc, 1, plane : plane + 1, :] = -imag


def shards(eigvecs, links, momenta, coef_num, coef_den, peram):
    n_space = lax.axis_size("space")
    n_op = lax.axis_size("op")
    n_tm = lax.axis_size("tm")
    _, _, n_b, _, planes, width = eigvecs.shape
    n_x = planes * n_space
    own = n_b // n_space
    n_h = coef_num.shape[0] // n_op
    my_op = lax.axis_index("op")
    my_space = lax.axis_index("space")

    nums = jnp.transpose(coef_num, (2, 1, 0))
    both = [(momenta, nums)]
    both += [(across(momenta, "op", mask), across(nums, "op", mask)) for mask in range(1, n_op)]

    group = n_space * n_op
    depth = n_b * SPINS // group
    first = (my_space * n_op + my_op) * depth
    piece = lax.dynamic_slice(
        peram.reshape(n_b, SPINS, 2, n_b), (first % n_b, first // n_b, 0, 0), (depth, 1, 2, n_b)
    ).reshape(depth * 2, n_b)

    moved = lax.optimization_barrier(jnp.transpose(eigvecs[0], (3, 0, 2, 1, 4)))
    moved, piece, both = lax.optimization_barrier((moved, piece, both))
    own_piece = from_behind(piece, "tm", n_tm - 1)
    vecs = [moved[plane] for plane in range(planes)]
    upper = from_behind(vecs[0], "space", -1)

    smem = pl.BlockSpec(memory_space=pltpu.SMEM)
    vmem = pl.BlockSpec(memory_space=pltpu.VMEM)
    phi = pl.pallas_call(
        functools.partial(phase_kernel, n_op, n_x, planes),
        in_specs=[smem] * (2 * n_op + 1),
        out_specs=vmem,
        out_shape=jax.ShapeDtypeStruct((2, n_h, NDIR, 2, planes, width), jnp.float32),
        compiler_params=pltpu.CompilerParams(vmem_limit_bytes=4 * 2**20),
        name="phases",
    )(*[mom for mom, _ in both], *[num for _, num in both], coef_den)

    dims = [("op", 1 << bit) for bit in range(n_op.bit_length() - 1)]
    dims += [("space", 1 << bit) for bit in range(1, n_space.bit_length() - 1)]
    load = [0] * len(dims)

    def stage(held, size):
        for group_dims in itertools.combinations(range(len(dims)), size):
            dim = min(group_dims, key=lambda at: load[at])
            load[dim] += 1
            before = held[tuple(at for at in group_dims if at != dim)]
            held[group_dims] = across(before, *dims[dim])

    def hold(held, other):
        arrs, other = lax.optimization_barrier((list(held.values()), other))
        return dict(zip(held.keys(), arrs)), other

    link = links[0]
    last = planes - 1
    partial = None
    for plane in range(planes):
        partial = plane_call(plane, (1, 2), vecs[plane], None, link, phi, partial)
    held, partial = hold({(): own_piece}, partial)
    stage(held, 1)
    for plane in range(last):
        partial = plane_call(plane, (0,), vecs[plane], vecs[plane + 1], link, phi, partial)
    held, partial = hold(held, partial)
    stage(held, 2)
    keep, give = plane_call(last, (0,), vecs[last], upper, link, phi, partial, n_space)
    swapped = across(give, "space", 1)
    held, keep = hold(held, keep)
    for size in range(3, len(dims) + 1):
        stage(held, size)
    early = [key for key in held if len(key) < 3]
    late = [key for key in held if len(key) >= 3]
    packed = pack_call([held[key] for key in early])
    merged = merge_call(keep, swapped)
    got = [merged[0]] + [across(arr, "space", 2 * mask) for mask, arr in enumerate(merged[1:], 1)]
    last_held, got = hold({key: held[key] for key in late}, got)
    held.update(last_held)
    tau = [held[key] for key in early + late]
    tau += [across(packed, "space", 1)] + [across(held[key], "space", 1) for key in late]
    masks = []
    for flip in range(2):
        for group_dims in early + late:
            mask = {"space": flip, "op": 0}
            for at in group_dims:
                mask[dims[at][0]] ^= dims[at][1]
            masks.append((mask["space"], mask["op"]))

    lines = pl.pallas_call(
        functools.partial(quark_kernel, masks, n_op, len(got), len(tau), n_h),
        in_specs=[vmem] * (len(got) + len(tau)),
        out_specs=vmem,
        out_shape=jax.ShapeDtypeStruct((n_h, SPINS, 2, own, n_b), jnp.float32),
        scratch_shapes=[
            pltpu.VMEM((n_h * 2 * own, 2 * n_b), jnp.bfloat16),
        ],
        compiler_params=pltpu.CompilerParams(vmem_limit_bytes=VMEM_BYTES),
        cost_estimate=pl.CostEstimate(
            flops=2 * SPINS * n_h * 2 * own * 2 * n_b * n_b, bytes_accessed=7 * 2**20, transcendentals=0
        ),
        name="quark_products",
    )(*got, *tau)
    return lines.reshape(1, n_h, 4, 4, 2, own, n_b)


def solution(mesh):
    return jax.shard_map(
        shards,
        mesh=mesh,
        in_specs=(
            P("tm", None, None, None, "space", None),
            P("tm", None, None, None, None, "space", None),
            P("op", None),
            P(None, "op", None),
            P(),
            P("tm", None, None, None, None, None),
        ),
        out_specs=P("tm", "op", None, None, None, "space", None),
        check_vma=False,
    )
```

```python
import functools
import itertools
import math

import jax
import jax.numpy as jnp
from jax import lax
from jax.experimental import pallas as pl
from jax.experimental.pallas import tpu as pltpu
from jax.sharding import PartitionSpec as P

LY = 32
LZ = 8
NDIR = 3
SPINS = 16
ROWS = 16
HALF = 128
BLOCK = 32
VMEM_BYTES = 20 * 2**20


def from_behind(value, axis, steps):
    count = lax.axis_size(axis)
    pairs = [(source, (source + steps) % count) for source in range(count)]
    return lax.ppermute(value, axis, pairs)


def across(value, axis, mask):
    pairs = [(source, source ^ mask) for source in range(lax.axis_size(axis))]
    return lax.ppermute(value, axis, pairs)


def dot_nt(left, right):
    return lax.dot_general(
        left, right, (((1,), (1,)), ((), ())), preferred_element_type=jnp.float32
    )


def shift_y(arr):
    return pltpu.roll(arr, arr.shape[1] - LZ, 1)


def shift_z(arr):
    width = arr.shape[1]
    lane = lax.broadcasted_iota(jnp.int32, arr.shape, 1)
    near = pltpu.roll(arr, width - 1, 1)
    far = pltpu.roll(arr, LZ - 1, 1)
    return jnp.where((lane & (LZ - 1)) == LZ - 1, far, near)


def weighted_links(u_ref, phi_ref, shifted, dirs, plane, n_h, store):
    width = u_ref.shape[-1]
    for half in range(width // HALF):
        lanes = pl.ds(half * HALF, HALF)
        for col in range(3):
            acc = {}
            for slot, direc in enumerate(dirs):
                f_r = None
                f_i = None
                for col_two in range(3):
                    u_r = u_ref[direc, col, col_two, 0, pl.ds(plane, 1), lanes]
                    u_i = u_ref[direc, col, col_two, 1, pl.ds(plane, 1), lanes]
                    v_r = shifted[slot, 0, col_two, :, lanes]
                    v_i = shifted[slot, 1, col_two, :, lanes]
                    term_r = u_r * v_r - u_i * v_i
                    term_i = u_r * v_i + u_i * v_r
                    f_r = term_r if f_r is None else f_r + term_r
                    f_i = term_i if f_i is None else f_i + term_i
                for kind in range(2):
                    for hel in range(n_h):
                        p_r = phi_ref[kind, hel, direc, 0, pl.ds(plane, 1), lanes]
                        p_i = phi_ref[kind, hel, direc, 1, pl.ds(plane, 1), lanes]
                        g_r = p_r * f_r - p_i * f_i
                        g_i = p_r * f_i + p_i * f_r
                        if (kind, hel) in acc:
                            old_r, old_i = acc[kind, hel]
                            g_r, g_i = old_r + g_r, old_i + g_i
                        acc[kind, hel] = (g_r, g_i)
            for (kind, hel), both in acc.items():
                store(kind, hel, col, half, both)


def plane_kernel(plane, dirs, has_part, n_out, *refs):
    refs = list(refs)
    v_ref = refs.pop(0)
    next_ref = refs.pop(0) if 0 in dirs else None
    u_ref, phi_ref = refs.pop(0), refs.pop(0)
    part_ref = refs.pop(0) if has_part else None
    keep_ref = refs.pop(0) if n_out else None
    give_ref = refs.pop(0) if n_out else None
    sum_ref, mat_ref, one_ref, two_ref, sh_ref = refs
    n_h = phi_ref.shape[1]
    _, _, n_b, width = v_ref.shape
    bufs = (one_ref, two_ref)
    last = n_b // BLOCK - 1

    for col in range(3):
        mat_ref[:, pl.ds(col * width, width)] = v_ref[:, col].reshape(2 * n_b, width)

    def fill(which, buf):
        for sub in range(BLOCK // ROWS):
            rows = pl.ds(pl.multiple_of(which * BLOCK + sub * ROWS, ROWS), ROWS)
            shifted = sh_ref.at[buf, sub]
            for slot, direc in enumerate(dirs):
                for part in range(2):
                    for col in range(3):
                        source = next_ref if direc == 0 else v_ref
                        field = source[part, col, rows, :].astype(jnp.float32)
                        if direc == 1:
                            field = shift_y(field)
                        elif direc == 2:
                            field = shift_z(field)
                        shifted[slot, part, col] = field

            def store(kind, hel, col, half, both, sub=sub):
                for part in range(2):
                    row = ((kind * n_h + hel) * 2 + part) * BLOCK + sub * ROWS
                    lanes = pl.ds(col * width + half * HALF, HALF)
                    bufs[buf][pl.ds(row, ROWS), lanes] = both[part].astype(jnp.bfloat16)

            weighted_links(u_ref, phi_ref, shifted, dirs, plane, n_h, store)

    def contract(which, buf):
        rows = pl.ds(pl.multiple_of(which * BLOCK, BLOCK), BLOCK)
        prod = dot_nt(bufs[buf][...], mat_ref[...])
        for kind in range(2):
            for hel in range(n_h):
                row = (kind * n_h + hel) * 2 * BLOCK
                re_row, im_row = prod[row : row + BLOCK], prod[row + BLOCK : row + 2 * BLOCK]
                real = re_row[:, :n_b] + im_row[:, n_b:]
                if kind:
                    imag = re_row[:, n_b:] - im_row[:, :n_b]
                else:
                    imag = im_row[:, :n_b] - re_row[:, n_b:]
                for part, total in enumerate((real, imag)):
                    if has_part:
                        total = total + part_ref[kind, hel, part, rows, :]
                    sum_ref[kind, hel, part, rows, :] = total

    fill(0, 0)

    def pair(step, carry):
        fill(2 * step + 1, 1)
        contract(2 * step, 0)
        fill(2 * step + 2, 0)
        contract(2 * step + 1, 1)
        return carry

    lax.fori_loop(0, last // 2, pair, 0)
    fill(last, 1)
    contract(last - 1, 0)
    contract(last, 1)

    if n_out:
        core = lax.axis_index("space") & 1
        for hel in range(n_h):
            for part in range(2):
                total = jnp.transpose(sum_ref[0, hel, part]) + sum_ref[1, hel, part]
                halves = total.reshape(n_out // 2, 2, n_b // n_out, n_b)
                keep_ref[:, hel, part] = jnp.where(core == 0, halves[:, 0], halves[:, 1])
                give = jnp.where(core == 0, halves[:, 1], halves[:, 0])
                give_ref[:, hel, part] = give.astype(jnp.bfloat16)


def plane_call(plane, dirs, vec, ahead, link, phi, part=None, n_out=0):
    n_h = phi.shape[1]
    _, _, n_b, width = vec.shape
    vmem = pl.BlockSpec(memory_space=pltpu.VMEM)
    args = [vec] + ([ahead] if 0 in dirs else []) + [link, phi]
    args += [part] if part is not None else []
    specs = [vmem] * len(args)
    sums = (2, n_h, 2, n_b, n_b)
    scratch = [
        pltpu.VMEM((2 * n_b, 3 * width), jnp.bfloat16),
        pltpu.VMEM((4 * n_h * BLOCK, 3 * width), jnp.bfloat16),
        pltpu.VMEM((4 * n_h * BLOCK, 3 * width), jnp.bfloat16),
        pltpu.VMEM((2, BLOCK // ROWS, len(dirs), 2, 3, ROWS, width), jnp.float32),
    ]
    if n_out:
        scratch.insert(0, pltpu.VMEM(sums, jnp.float32))
        blocks = (n_out // 2, n_h, 2, n_b // n_out, n_b)
        out_shape = [
            jax.ShapeDtypeStruct(blocks, jnp.float32),
            jax.ShapeDtypeStruct(blocks, jnp.bfloat16),
        ]
        out_specs = [vmem, vmem]
    else:
        out_shape = jax.ShapeDtypeStruct(sums, jnp.float32)
        out_specs = vmem
    return pl.pallas_call(
        functools.partial(plane_kernel, plane, dirs, part is not None, n_out),
        in_specs=specs,
        out_specs=out_specs,
        out_shape=out_shape,
        scratch_shapes=scratch,
        compiler_params=pltpu.CompilerParams(vmem_limit_bytes=VMEM_BYTES),
        cost_estimate=pl.CostEstimate(
            flops=(16 + 8 * len(dirs)) * n_h * n_b * n_b * 3 * width,
            bytes_accessed=2**22,
            transcendentals=0,
        ),
        name="plane%d_%s" % (plane, "".join(str(direc) for direc in dirs)),
    )(*args)


def merge_kernel(keep_ref, got_ref, own_ref, *out_refs):
    chip = lax.axis_index("space") >> 1
    shape = own_ref.shape
    own_ref[...] = (keep_ref[chip] + got_ref[chip].astype(jnp.float32)).reshape(shape)
    for mask, out_ref in enumerate(out_refs, 1):
        total = keep_ref[chip ^ mask] + got_ref[chip ^ mask].astype(jnp.float32)
        out_ref[...] = total.reshape(shape).astype(jnp.bfloat16)


def merge_call(keep, got):
    chips, n_h, _, own, n_b = keep.shape
    shape = (n_h * 2 * own, n_b)
    vmem = pl.BlockSpec(memory_space=pltpu.VMEM)
    return pl.pallas_call(
        merge_kernel,
        in_specs=[vmem, vmem],
        out_specs=[vmem] * chips,
        out_shape=[jax.ShapeDtypeStruct(shape, jnp.float32)]
        + [jax.ShapeDtypeStruct(shape, jnp.bfloat16)] * (chips - 1),
        compiler_params=pltpu.CompilerParams(vmem_limit_bytes=8 * 2**20),
        cost_estimate=pl.CostEstimate(flops=2**16, bytes_accessed=2**12, transcendentals=0),
        name="merge_cores",
    )(keep, got)


def pack_kernel(*refs):
    for which, ref in enumerate(refs[:-1]):
        refs[-1][which] = ref[...]


def pack_call(arrs):
    vmem = pl.BlockSpec(memory_space=pltpu.VMEM)
    return pl.pallas_call(
        pack_kernel,
        in_specs=[vmem] * len(arrs),
        out_specs=vmem,
        out_shape=jax.ShapeDtypeStruct((len(arrs),) + arrs[0].shape, arrs[0].dtype),
        compiler_params=pltpu.CompilerParams(vmem_limit_bytes=8 * 2**20),
        cost_estimate=pl.CostEstimate(flops=2**16, bytes_accessed=2**12, transcendentals=0),
        name="pack_pieces",
    )(*arrs)


def quark_kernel(masks, n_op, n_got, n_tau, n_h, *refs):
    got_refs = refs[:n_got]
    tau_refs = refs[n_got : n_got + n_tau]
    out_ref, left_ref = refs[n_got + n_tau :]
    my_space, my_op = lax.axis_index("space"), lax.axis_index("op")
    _, n_pair, _, own, n_b = out_ref.shape
    row = lax.broadcasted_iota(jnp.int32, (n_b, 2 * n_b), 0)
    col = lax.broadcasted_iota(jnp.int32, (n_b, 2 * n_b), 1)
    even = (col == 2 * row).astype(jnp.bfloat16)
    odd = (col == 2 * row + 1).astype(jnp.bfloat16)
    total = got_refs[0][...]
    for ref in got_refs[1:]:
        total = total + ref[...].astype(jnp.float32)
    swap = []
    for hel in range(n_h):
        start = hel * 2 * own
        swap += [-total[start + own : start + 2 * own], total[start : start + own]]
    left = jnp.dot(total.astype(jnp.bfloat16), even, preferred_element_type=jnp.float32)
    left += jnp.dot(
        jnp.concatenate(swap, 0).astype(jnp.bfloat16), odd, preferred_element_type=jnp.float32
    )
    left_ref[...] = left.astype(jnp.bfloat16)
    tau = []
    for ref in tau_refs:
        tau += [ref.at[which] for which in range(ref.shape[0])] if len(ref.shape) == 3 else [ref]
    depth = tau[0].shape[0]
    whole = depth == 2 * n_b
    if not whole:
        out_ref[...] = jnp.zeros_like(out_ref)
    for which, (mask, mask_op) in enumerate(masks):
        first = ((my_space ^ mask) * n_op + (my_op ^ mask_op)) * depth
        pair = first // (2 * n_b)
        if whole:
            lhs = left_ref[...]
        else:
            lhs = left_ref[:, pl.ds(pl.multiple_of(first - pair * 2 * n_b, depth), depth)]
        res = jnp.dot(lhs, tau[which][...], preferred_element_type=jnp.float32)
        for hel in range(n_h):
            for part in range(2):
                start = (hel * 2 + part) * own
                if whole:
                    out_ref[hel, pair, part] = res[start : start + own]
                else:
                    out_ref[hel, pair, part] += res[start : start + own]


def phase_kernel(n_op, n_x, planes, *refs):
    mom_refs = refs[:n_op]
    num_refs = refs[n_op : 2 * n_op]
    den_ref, out_ref = refs[2 * n_op :]
    my_space, my_op = lax.axis_index("space"), lax.axis_index("op")
    _, n_h, _, _, _, width = out_ref.shape
    n_mom = mom_refs[0].shape[0]
    moms = [(op, k) for op in range(n_op) for k in range(n_mom)]
    scale = 1.0 / math.sqrt(3.0 * n_x * LY * LZ)
    shape = (planes * len(moms), width)
    row = lax.broadcasted_iota(jnp.int32, shape, 0)
    lane = lax.broadcasted_iota(jnp.int32, shape, 1)
    yy = lane // LZ
    zz = lane & (LZ - 1)

    def spread(values):
        res = jnp.full(shape, values[0], jnp.int32)
        for which in range(1, len(values)):
            res = jnp.where(row == which, values[which], res)
        return res

    comps = [[mom_refs[op][k, axis] for _ in range(planes) for op, k in moms] for axis in range(3)]
    mom_x, mom_y, mom_z = [spread(comp) for comp in comps]
    pos_x = my_space * planes + row // len(moms)
    steps = ((0, 0, 0), (1, 0, 0), (0, 1, 0), (0, 0, 1))
    waves = []
    for step_x, step_y, step_z in steps:
        turn_x = lax.rem(mom_x * (pos_x + step_x), n_x).astype(jnp.float32) * (1.0 / n_x)
        turn_y = ((mom_y * (yy + step_y)) & (LY - 1)).astype(jnp.float32) * (1.0 / LY)
        turn_z = ((mom_z * (zz + step_z)) & (LZ - 1)).astype(jnp.float32) * (1.0 / LZ)
        turn = turn_x + turn_y + turn_z
        theta = (2.0 * math.pi) * (turn - jnp.floor(turn))
        waves.append((jnp.cos(theta), jnp.sin(theta)))
    for hel in range(n_h):
        which_h = my_op * n_h + hel
        den = jnp.full((1, width), den_ref[which_h], jnp.int32).astype(jnp.float32)
        for direc in range(NDIR):
            wts = []
            for op, k in moms:
                num = num_refs[op][direc, k, which_h]
                wts.append(jnp.full((1, width), num, jnp.int32).astype(jnp.float32) / den * scale)
            for kind, wave in ((0, waves[0]), (1, waves[1 + direc])):
                for plane in range(planes):
                    start = plane * len(moms)
                    real = sum(wt * wave[0][start + at : start + at + 1] for at, wt in enumerate(wts))
                    imag = sum(wt * wave[1][start + at : start + at + 1] for at, wt in enumerate(wts))
                    out_ref[kind, hel, direc, 0, plane : plane + 1, :] = -real if kind else real
                    out_ref[kind, hel, direc, 1, plane : plane + 1, :] = -imag


def shards(eigvecs, links, momenta, coef_num, coef_den, peram):
    n_space = lax.axis_size("space")
    n_op = lax.axis_size("op")
    n_tm = lax.axis_size("tm")
    _, _, n_b, _, planes, width = eigvecs.shape
    n_x = planes * n_space
    own = n_b // n_space
    n_h = coef_num.shape[0] // n_op
    my_op = lax.axis_index("op")
    my_space = lax.axis_index("space")

    nums = jnp.transpose(coef_num, (2, 1, 0))
    both = [(momenta, nums)]
    both += [(across(momenta, "op", mask), across(nums, "op", mask)) for mask in range(1, n_op)]

    group = n_space * n_op
    depth = n_b * SPINS // group
    first = (my_space * n_op + my_op) * depth
    piece = lax.dynamic_slice(
        peram.reshape(n_b, SPINS, 2, n_b), (first % n_b, first // n_b, 0, 0), (depth, 1, 2, n_b)
    ).reshape(depth * 2, n_b)

    moved = lax.optimization_barrier(jnp.transpose(eigvecs[0], (3, 0, 2, 1, 4)))
    own_piece = from_behind(piece, "tm", n_tm - 1)
    vecs = [moved[plane] for plane in range(planes)]
    upper = from_behind(vecs[0], "space", -1)

    smem = pl.BlockSpec(memory_space=pltpu.SMEM)
    vmem = pl.BlockSpec(memory_space=pltpu.VMEM)
    phi = pl.pallas_call(
        functools.partial(phase_kernel, n_op, n_x, planes),
        in_specs=[smem] * (2 * n_op + 1),
        out_specs=vmem,
        out_shape=jax.ShapeDtypeStruct((2, n_h, NDIR, 2, planes, width), jnp.float32),
        compiler_params=pltpu.CompilerParams(vmem_limit_bytes=4 * 2**20),
        name="phases",
    )(*[mom for mom, _ in both], *[num for _, num in both], coef_den)

    dims = [("op", 1 << bit) for bit in range(n_op.bit_length() - 1)]
    dims += [("space", 1 << bit) for bit in range(1, n_space.bit_length() - 1)]
    load = [0] * len(dims)

    def stage(held, size):
        for group_dims in itertools.combinations(range(len(dims)), size):
            dim = min(group_dims, key=lambda at: load[at])
            load[dim] += 1
            before = held[tuple(at for at in group_dims if at != dim)]
            held[group_dims] = across(before, *dims[dim])

    def hold(held, other):
        arrs, other = lax.optimization_barrier((list(held.values()), other))
        return dict(zip(held.keys(), arrs)), other

    link = links[0]
    last = planes - 1
    partial = None
    for plane in range(planes):
        partial = plane_call(plane, (1, 2), vecs[plane], None, link, phi, partial)
    held, partial = hold({(): own_piece}, partial)
    stage(held, 1)
    for plane in range(last):
        partial = plane_call(plane, (0,), vecs[plane], vecs[plane + 1], link, phi, partial)
    held, partial = hold(held, partial)
    stage(held, 2)
    keep, give = plane_call(last, (0,), vecs[last], upper, link, phi, partial, n_space)
    swapped = across(give, "space", 1)
    held, keep = hold(held, keep)
    for size in range(3, len(dims) + 1):
        stage(held, size)
    early = [key for key in held if len(key) < 3]
    late = [key for key in held if len(key) >= 3]
    early_held, swapped = hold({key: held[key] for key in early}, swapped)
    packed = pack_call([early_held[key] for key in early])
    merged = merge_call(keep, swapped)
    got = [merged[0]] + [across(arr, "space", 2 * mask) for mask, arr in enumerate(merged[1:], 1)]
    last_held, got = hold({key: held[key] for key in late}, got)
    held.update(last_held)
    tau = [held[key] for key in early + late]
    tau += [across(packed, "space", 1)] + [across(held[key], "space", 1) for key in late]
    masks = []
    for flip in range(2):
        for group_dims in early + late:
            mask = {"space": flip, "op": 0}
            for at in group_dims:
                mask[dims[at][0]] ^= dims[at][1]
            masks.append((mask["space"], mask["op"]))

    lines = pl.pallas_call(
        functools.partial(quark_kernel, masks, n_op, len(got), len(tau), n_h),
        in_specs=[vmem] * (len(got) + len(tau)),
        out_specs=vmem,
        out_shape=jax.ShapeDtypeStruct((n_h, SPINS, 2, own, n_b), jnp.float32),
        scratch_shapes=[
            pltpu.VMEM((n_h * 2 * own, 2 * n_b), jnp.bfloat16),
        ],
        compiler_params=pltpu.CompilerParams(vmem_limit_bytes=VMEM_BYTES),
        cost_estimate=pl.CostEstimate(
            flops=2 * SPINS * n_h * 2 * own * 2 * n_b * n_b, bytes_accessed=7 * 2**20, transcendentals=0
        ),
        name="quark_products",
    )(*got, *tau)
    return lines.reshape(1, n_h, 4, 4, 2, own, n_b)


def solution(mesh):
    return jax.shard_map(
        shards,
        mesh=mesh,
        in_specs=(
            P("tm", None, None, None, "space", None),
            P("tm", None, None, None, None, "space", None),
            P("op", None),
            P(None, "op", None),
            P(),
            P("tm", None, None, None, None, None),
        ),
        out_specs=P("tm", "op", None, None, None, "space", None),
        check_vma=False,
    )
```

```python
import functools
import itertools
import math

import jax
import jax.numpy as jnp
from jax import lax
from jax.experimental import pallas as pl
from jax.experimental.pallas import tpu as pltpu
from jax.sharding import PartitionSpec as P

LY = 32
LZ = 8
NDIR = 3
SPINS = 16
ROWS = 16
HALF = 128
BLOCK = 32
VMEM_BYTES = 20 * 2**20


def from_behind(value, axis, steps):
    count = lax.axis_size(axis)
    pairs = [(source, (source + steps) % count) for source in range(count)]
    return lax.ppermute(value, axis, pairs)


def across(value, axis, mask):
    pairs = [(source, source ^ mask) for source in range(lax.axis_size(axis))]
    return lax.ppermute(value, axis, pairs)


def diagonal(value, n_space, n_op):
    pairs = []
    for space in range(n_space):
        for oper in range(n_op):
            target = (space ^ (n_space - 2)) * n_op + (oper ^ (n_op - 1))
            pairs.append((space * n_op + oper, target))
    return lax.ppermute(value, ("space", "op"), pairs)


def dot_nt(left, right):
    return lax.dot_general(
        left, right, (((1,), (1,)), ((), ())), preferred_element_type=jnp.float32
    )


def shift_y(arr):
    return pltpu.roll(arr, arr.shape[1] - LZ, 1)


def shift_z(arr):
    width = arr.shape[1]
    lane = lax.broadcasted_iota(jnp.int32, arr.shape, 1)
    near = pltpu.roll(arr, width - 1, 1)
    far = pltpu.roll(arr, LZ - 1, 1)
    return jnp.where((lane & (LZ - 1)) == LZ - 1, far, near)


def weighted_links(u_ref, phi_ref, shifted, dirs, plane, n_h, store):
    width = u_ref.shape[-1]
    for half in range(width // HALF):
        lanes = pl.ds(half * HALF, HALF)
        for col in range(3):
            acc = {}
            for slot, direc in enumerate(dirs):
                f_r = None
                f_i = None
                for col_two in range(3):
                    u_r = u_ref[direc, col, col_two, 0, pl.ds(plane, 1), lanes]
                    u_i = u_ref[direc, col, col_two, 1, pl.ds(plane, 1), lanes]
                    v_r = shifted[slot, 0, col_two, :, lanes]
                    v_i = shifted[slot, 1, col_two, :, lanes]
                    term_r = u_r * v_r - u_i * v_i
                    term_i = u_r * v_i + u_i * v_r
                    f_r = term_r if f_r is None else f_r + term_r
                    f_i = term_i if f_i is None else f_i + term_i
                for kind in range(2):
                    for hel in range(n_h):
                        p_r = phi_ref[kind, hel, direc, 0, pl.ds(plane, 1), lanes]
                        p_i = phi_ref[kind, hel, direc, 1, pl.ds(plane, 1), lanes]
                        g_r = p_r * f_r - p_i * f_i
                        g_i = p_r * f_i + p_i * f_r
                        if (kind, hel) in acc:
                            old_r, old_i = acc[kind, hel]
                            g_r, g_i = old_r + g_r, old_i + g_i
                        acc[kind, hel] = (g_r, g_i)
            for (kind, hel), both in acc.items():
                store(kind, hel, col, half, both)


def plane_kernel(plane, dirs, has_part, n_out, *refs):
    refs = list(refs)
    v_ref = refs.pop(0)
    next_ref = refs.pop(0) if 0 in dirs else None
    u_ref, phi_ref = refs.pop(0), refs.pop(0)
    part_ref = refs.pop(0) if has_part else None
    keep_ref = refs.pop(0) if n_out else None
    give_ref = refs.pop(0) if n_out else None
    sum_ref, mat_ref, one_ref, two_ref, sh_ref = refs
    n_h = phi_ref.shape[1]
    _, _, n_b, width = v_ref.shape
    bufs = (one_ref, two_ref)
    last = n_b // BLOCK - 1

    for col in range(3):
        mat_ref[:, pl.ds(col * width, width)] = v_ref[:, col].reshape(2 * n_b, width)

    def fill(which, buf):
        for sub in range(BLOCK // ROWS):
            rows = pl.ds(pl.multiple_of(which * BLOCK + sub * ROWS, ROWS), ROWS)
            shifted = sh_ref.at[buf, sub]
            for slot, direc in enumerate(dirs):
                for part in range(2):
                    for col in range(3):
                        source = next_ref if direc == 0 else v_ref
                        field = source[part, col, rows, :].astype(jnp.float32)
                        if direc == 1:
                            field = shift_y(field)
                        elif direc == 2:
                            field = shift_z(field)
                        shifted[slot, part, col] = field

            def store(kind, hel, col, half, both, sub=sub):
                for part in range(2):
                    row = ((kind * n_h + hel) * 2 + part) * BLOCK + sub * ROWS
                    lanes = pl.ds(col * width + half * HALF, HALF)
                    bufs[buf][pl.ds(row, ROWS), lanes] = both[part].astype(jnp.bfloat16)

            weighted_links(u_ref, phi_ref, shifted, dirs, plane, n_h, store)

    def contract(which, buf):
        rows = pl.ds(pl.multiple_of(which * BLOCK, BLOCK), BLOCK)
        prod = dot_nt(bufs[buf][...], mat_ref[...])
        for kind in range(2):
            for hel in range(n_h):
                row = (kind * n_h + hel) * 2 * BLOCK
                re_row, im_row = prod[row : row + BLOCK], prod[row + BLOCK : row + 2 * BLOCK]
                real = re_row[:, :n_b] + im_row[:, n_b:]
                if kind:
                    imag = re_row[:, n_b:] - im_row[:, :n_b]
                else:
                    imag = im_row[:, :n_b] - re_row[:, n_b:]
                for part, total in enumerate((real, imag)):
                    if has_part:
                        total = total + part_ref[kind, hel, part, rows, :]
                    sum_ref[kind, hel, part, rows, :] = total

    fill(0, 0)

    def pair(step, carry):
        fill(2 * step + 1, 1)
        contract(2 * step, 0)
        fill(2 * step + 2, 0)
        contract(2 * step + 1, 1)
        return carry

    lax.fori_loop(0, last // 2, pair, 0)
    fill(last, 1)
    contract(last - 1, 0)
    contract(last, 1)

    if n_out:
        core = lax.axis_index("space") & 1
        for hel in range(n_h):
            for part in range(2):
                total = jnp.transpose(sum_ref[0, hel, part]) + sum_ref[1, hel, part]
                halves = total.reshape(n_out // 2, 2, n_b // n_out, n_b)
                keep_ref[:, hel, part] = jnp.where(core == 0, halves[:, 0], halves[:, 1])
                give = jnp.where(core == 0, halves[:, 1], halves[:, 0])
                give_ref[:, hel, part] = give.astype(jnp.bfloat16)


def plane_call(plane, dirs, vec, ahead, link, phi, part=None, n_out=0):
    n_h = phi.shape[1]
    _, _, n_b, width = vec.shape
    vmem = pl.BlockSpec(memory_space=pltpu.VMEM)
    args = [vec] + ([ahead] if 0 in dirs else []) + [link, phi]
    args += [part] if part is not None else []
    specs = [vmem] * len(args)
    sums = (2, n_h, 2, n_b, n_b)
    scratch = [
        pltpu.VMEM((2 * n_b, 3 * width), jnp.bfloat16),
        pltpu.VMEM((4 * n_h * BLOCK, 3 * width), jnp.bfloat16),
        pltpu.VMEM((4 * n_h * BLOCK, 3 * width), jnp.bfloat16),
        pltpu.VMEM((2, BLOCK // ROWS, len(dirs), 2, 3, ROWS, width), jnp.float32),
    ]
    if n_out:
        scratch.insert(0, pltpu.VMEM(sums, jnp.float32))
        blocks = (n_out // 2, n_h, 2, n_b // n_out, n_b)
        out_shape = [
            jax.ShapeDtypeStruct(blocks, jnp.float32),
            jax.ShapeDtypeStruct(blocks, jnp.bfloat16),
        ]
        out_specs = [vmem, vmem]
    else:
        out_shape = jax.ShapeDtypeStruct(sums, jnp.float32)
        out_specs = vmem
    return pl.pallas_call(
        functools.partial(plane_kernel, plane, dirs, part is not None, n_out),
        in_specs=specs,
        out_specs=out_specs,
        out_shape=out_shape,
        scratch_shapes=scratch,
        compiler_params=pltpu.CompilerParams(vmem_limit_bytes=VMEM_BYTES),
        cost_estimate=pl.CostEstimate(
            flops=2**34,
            bytes_accessed=2**28,
            transcendentals=0,
        ),
        name="plane%d_%s" % (plane, "".join(str(direc) for direc in dirs)),
    )(*args)


def merge_kernel(keep_ref, got_ref, own_ref, *out_refs):
    chip = lax.axis_index("space") >> 1
    shape = own_ref.shape
    own_ref[...] = (keep_ref[chip] + got_ref[chip].astype(jnp.float32)).reshape(shape)
    for mask, out_ref in enumerate(out_refs, 1):
        total = keep_ref[chip ^ mask] + got_ref[chip ^ mask].astype(jnp.float32)
        out_ref[...] = total.reshape(shape).astype(jnp.bfloat16)


def merge_call(keep, got):
    chips, n_h, _, own, n_b = keep.shape
    shape = (n_h * 2 * own, n_b)
    vmem = pl.BlockSpec(memory_space=pltpu.VMEM)
    return pl.pallas_call(
        merge_kernel,
        in_specs=[vmem, vmem],
        out_specs=[vmem] * chips,
        out_shape=[jax.ShapeDtypeStruct(shape, jnp.float32)]
        + [jax.ShapeDtypeStruct(shape, jnp.bfloat16)] * (chips - 1),
        compiler_params=pltpu.CompilerParams(vmem_limit_bytes=8 * 2**20),
        cost_estimate=pl.CostEstimate(flops=2**16, bytes_accessed=2**12, transcendentals=0),
        name="merge_cores",
    )(keep, got)


def pack_kernel(*refs):
    for which, ref in enumerate(refs[:-1]):
        refs[-1][which] = ref[...]


def pack_call(arrs):
    vmem = pl.BlockSpec(memory_space=pltpu.VMEM)
    return pl.pallas_call(
        pack_kernel,
        in_specs=[vmem] * len(arrs),
        out_specs=vmem,
        out_shape=jax.ShapeDtypeStruct((len(arrs),) + arrs[0].shape, arrs[0].dtype),
        compiler_params=pltpu.CompilerParams(vmem_limit_bytes=8 * 2**20),
        cost_estimate=pl.CostEstimate(flops=2**16, bytes_accessed=2**12, transcendentals=0),
        name="pack_pieces",
    )(*arrs)


def quark_kernel(masks, n_op, n_got, n_tau, n_h, *refs):
    got_refs = refs[:n_got]
    tau_refs = refs[n_got : n_got + n_tau]
    out_ref, left_ref = refs[n_got + n_tau :]
    my_space, my_op = lax.axis_index("space"), lax.axis_index("op")
    _, n_pair, _, own, n_b = out_ref.shape
    row = lax.broadcasted_iota(jnp.int32, (n_b, 2 * n_b), 0)
    col = lax.broadcasted_iota(jnp.int32, (n_b, 2 * n_b), 1)
    even = (col == 2 * row).astype(jnp.bfloat16)
    odd = (col == 2 * row + 1).astype(jnp.bfloat16)
    total = got_refs[0][...]
    for ref in got_refs[1:]:
        total = total + ref[...].astype(jnp.float32)
    swap = []
    for hel in range(n_h):
        start = hel * 2 * own
        swap += [-total[start + own : start + 2 * own], total[start : start + own]]
    left = jnp.dot(total.astype(jnp.bfloat16), even, preferred_element_type=jnp.float32)
    left += jnp.dot(
        jnp.concatenate(swap, 0).astype(jnp.bfloat16), odd, preferred_element_type=jnp.float32
    )
    left_ref[...] = left.astype(jnp.bfloat16)
    tau = []
    for ref in tau_refs:
        tau += [ref.at[which] for which in range(ref.shape[0])] if len(ref.shape) == 3 else [ref]
    depth = tau[0].shape[0]
    whole = depth == 2 * n_b
    if not whole:
        out_ref[...] = jnp.zeros_like(out_ref)
    for which, (mask, mask_op) in enumerate(masks):
        first = ((my_space ^ mask) * n_op + (my_op ^ mask_op)) * depth
        pair = first // (2 * n_b)
        if whole:
            lhs = left_ref[...]
        else:
            lhs = left_ref[:, pl.ds(pl.multiple_of(first - pair * 2 * n_b, depth), depth)]
        res = jnp.dot(lhs, tau[which][...], preferred_element_type=jnp.float32)
        for hel in range(n_h):
            for part in range(2):
                start = (hel * 2 + part) * own
                if whole:
                    out_ref[hel, pair, part] = res[start : start + own]
                else:
                    out_ref[hel, pair, part] += res[start : start + own]


def phase_kernel(n_op, n_x, planes, *refs):
    mom_refs = refs[:n_op]
    num_refs = refs[n_op : 2 * n_op]
    den_ref, out_ref = refs[2 * n_op :]
    my_space, my_op = lax.axis_index("space"), lax.axis_index("op")
    _, n_h, _, _, _, width = out_ref.shape
    n_mom = mom_refs[0].shape[0]
    moms = [(op, k) for op in range(n_op) for k in range(n_mom)]
    scale = 1.0 / math.sqrt(3.0 * n_x * LY * LZ)
    shape = (planes * len(moms), width)
    row = lax.broadcasted_iota(jnp.int32, shape, 0)
    lane = lax.broadcasted_iota(jnp.int32, shape, 1)
    yy = lane // LZ
    zz = lane & (LZ - 1)

    def spread(values):
        res = jnp.full(shape, values[0], jnp.int32)
        for which in range(1, len(values)):
            res = jnp.where(row == which, values[which], res)
        return res

    comps = [[mom_refs[op][k, axis] for _ in range(planes) for op, k in moms] for axis in range(3)]
    mom_x, mom_y, mom_z = [spread(comp) for comp in comps]
    pos_x = my_space * planes + row // len(moms)
    steps = ((0, 0, 0), (1, 0, 0), (0, 1, 0), (0, 0, 1))
    waves = []
    for step_x, step_y, step_z in steps:
        turn_x = lax.rem(mom_x * (pos_x + step_x), n_x).astype(jnp.float32) * (1.0 / n_x)
        turn_y = ((mom_y * (yy + step_y)) & (LY - 1)).astype(jnp.float32) * (1.0 / LY)
        turn_z = ((mom_z * (zz + step_z)) & (LZ - 1)).astype(jnp.float32) * (1.0 / LZ)
        turn = turn_x + turn_y + turn_z
        theta = (2.0 * math.pi) * (turn - jnp.floor(turn))
        waves.append((jnp.cos(theta), jnp.sin(theta)))
    for hel in range(n_h):
        which_h = my_op * n_h + hel
        den = jnp.full((1, width), den_ref[which_h], jnp.int32).astype(jnp.float32)
        for direc in range(NDIR):
            wts = []
            for op, k in moms:
                num = num_refs[op][direc, k, which_h]
                wts.append(jnp.full((1, width), num, jnp.int32).astype(jnp.float32) / den * scale)
            for kind, wave in ((0, waves[0]), (1, waves[1 + direc])):
                for plane in range(planes):
                    start = plane * len(moms)
                    real = sum(wt * wave[0][start + at : start + at + 1] for at, wt in enumerate(wts))
                    imag = sum(wt * wave[1][start + at : start + at + 1] for at, wt in enumerate(wts))
                    out_ref[kind, hel, direc, 0, plane : plane + 1, :] = -real if kind else real
                    out_ref[kind, hel, direc, 1, plane : plane + 1, :] = -imag


def shards(eigvecs, links, momenta, coef_num, coef_den, peram):
    n_space = lax.axis_size("space")
    n_op = lax.axis_size("op")
    n_tm = lax.axis_size("tm")
    _, _, n_b, _, planes, width = eigvecs.shape
    n_x = planes * n_space
    own = n_b // n_space
    n_h = coef_num.shape[0] // n_op
    my_op = lax.axis_index("op")
    my_space = lax.axis_index("space")

    nums = jnp.transpose(coef_num, (2, 1, 0))
    both = [(momenta, nums)]
    both += [(across(momenta, "op", mask), across(nums, "op", mask)) for mask in range(1, n_op)]

    group = n_space * n_op
    depth = n_b * SPINS // group
    first = (my_space * n_op + my_op) * depth
    piece = lax.dynamic_slice(
        peram.reshape(n_b, SPINS, 2, n_b), (first % n_b, first // n_b, 0, 0), (depth, 1, 2, n_b)
    ).reshape(depth * 2, n_b)

    moved = lax.optimization_barrier(jnp.transpose(eigvecs[0], (3, 0, 2, 1, 4)))
    own_piece = from_behind(piece, "tm", n_tm - 1)
    vecs = [moved[plane] for plane in range(planes)]
    upper = from_behind(vecs[0], "space", -1)

    smem = pl.BlockSpec(memory_space=pltpu.SMEM)
    vmem = pl.BlockSpec(memory_space=pltpu.VMEM)
    phi = pl.pallas_call(
        functools.partial(phase_kernel, n_op, n_x, planes),
        in_specs=[smem] * (2 * n_op + 1),
        out_specs=vmem,
        out_shape=jax.ShapeDtypeStruct((2, n_h, NDIR, 2, planes, width), jnp.float32),
        compiler_params=pltpu.CompilerParams(vmem_limit_bytes=4 * 2**20),
        name="phases",
    )(*[mom for mom, _ in both], *[num for _, num in both], coef_den)

    dims = [("op", 1 << bit) for bit in range(n_op.bit_length() - 1)]
    dims += [("space", 1 << bit) for bit in range(1, n_space.bit_length() - 1)]
    load = [0] * len(dims)

    def stage(held, size):
        for group_dims in itertools.combinations(range(len(dims)), size):
            dim = min(group_dims, key=lambda at: load[at])
            load[dim] += 1
            before = held[tuple(at for at in group_dims if at != dim)]
            held[group_dims] = across(before, *dims[dim])

    def hold(held, other):
        arrs, other = lax.optimization_barrier((list(held.values()), other))
        return dict(zip(held.keys(), arrs)), other

    link = links[0]
    last = planes - 1
    corner = tuple(range(len(dims)))
    partial = plane_call(last, (1, 2), vecs[last], None, link, phi)
    held, partial = hold({(): own_piece}, partial)
    stage(held, 1)
    if len(dims) > 2:
        far = diagonal(held[()], n_space, n_op)
    for plane in range(last):
        partial = plane_call(plane, (1, 2, 0), vecs[plane], vecs[plane + 1], link, phi, partial)
    held, partial = hold(held, partial)
    early = list(held)
    flipped = [across(pack_call([held[key] for key in early]), "space", 1)]
    for size in range(2, max(3, len(dims))):
        stage(held, size)
    if len(dims) > 2:
        held[corner] = far
    late = [key for key in held if key not in early]
    keep, give = plane_call(last, (0,), vecs[last], upper, link, phi, partial, n_space)
    swapped = across(give, "space", 1)
    merged = merge_call(keep, swapped)
    after, swapped = hold({key: held[key] for key in late}, swapped)
    held.update(after)
    flipped.append(across(pack_call([held[key] for key in late]), "space", 1))
    got = [merged[0]] + [across(arr, "space", 2 * mask) for mask, arr in enumerate(merged[1:], 1)]
    tau = [held[key] for key in early + late] + flipped
    masks = []
    for flip in range(2):
        for group_dims in early + late:
            mask = {"space": flip, "op": 0}
            for at in group_dims:
                mask[dims[at][0]] ^= dims[at][1]
            masks.append((mask["space"], mask["op"]))

    lines = pl.pallas_call(
        functools.partial(quark_kernel, masks, n_op, len(got), len(tau), n_h),
        in_specs=[vmem] * (len(got) + len(tau)),
        out_specs=vmem,
        out_shape=jax.ShapeDtypeStruct((n_h, SPINS, 2, own, n_b), jnp.float32),
        scratch_shapes=[
            pltpu.VMEM((n_h * 2 * own, 2 * n_b), jnp.bfloat16),
        ],
        compiler_params=pltpu.CompilerParams(vmem_limit_bytes=VMEM_BYTES),
        cost_estimate=pl.CostEstimate(
            flops=2 * SPINS * n_h * 2 * own * 2 * n_b * n_b, bytes_accessed=7 * 2**20, transcendentals=0
        ),
        name="quark_products",
    )(*got, *tau)
    return lines.reshape(1, n_h, 4, 4, 2, own, n_b)


def solution(mesh):
    return jax.shard_map(
        shards,
        mesh=mesh,
        in_specs=(
            P("tm", None, None, None, "space", None),
            P("tm", None, None, None, None, "space", None),
            P("op", None),
            P(None, "op", None),
            P(),
            P("tm", None, None, None, None, None),
        ),
        out_specs=P("tm", "op", None, None, None, "space", None),
        check_vma=False,
    )
```

```python
import functools
import itertools
import math

import jax
import jax.numpy as jnp
from jax import lax
from jax.experimental import pallas as pl
from jax.experimental.pallas import tpu as pltpu
from jax.sharding import PartitionSpec as P

LY = 32
LZ = 8
NDIR = 3
SPINS = 16
ROWS = 16
HALF = 128
BLOCK = 32
VMEM_BYTES = 20 * 2**20


def from_behind(value, axis, steps):
    count = lax.axis_size(axis)
    pairs = [(source, (source + steps) % count) for source in range(count)]
    return lax.ppermute(value, axis, pairs)


def across(value, axis, mask):
    pairs = [(source, source ^ mask) for source in range(lax.axis_size(axis))]
    return lax.ppermute(value, axis, pairs)


def diagonal(value, n_space, n_op):
    pairs = []
    for space in range(n_space):
        for oper in range(n_op):
            target = (space ^ (n_space - 2)) * n_op + (oper ^ (n_op - 1))
            pairs.append((space * n_op + oper, target))
    return lax.ppermute(value, ("space", "op"), pairs)


def dot_nt(left, right):
    return lax.dot_general(
        left, right, (((1,), (1,)), ((), ())), preferred_element_type=jnp.float32
    )


def shift_y(arr):
    return pltpu.roll(arr, arr.shape[1] - LZ, 1)


def shift_z(arr):
    width = arr.shape[1]
    lane = lax.broadcasted_iota(jnp.int32, arr.shape, 1)
    near = pltpu.roll(arr, width - 1, 1)
    far = pltpu.roll(arr, LZ - 1, 1)
    return jnp.where((lane & (LZ - 1)) == LZ - 1, far, near)


def weighted_links(u_ref, phi_ref, shifted, dirs, plane, n_h, store):
    width = u_ref.shape[-1]
    for half in range(width // HALF):
        lanes = pl.ds(half * HALF, HALF)
        for col in range(3):
            acc = {}
            for slot, direc in enumerate(dirs):
                f_r = None
                f_i = None
                for col_two in range(3):
                    u_r = u_ref[direc, col, col_two, 0, pl.ds(plane, 1), lanes]
                    u_i = u_ref[direc, col, col_two, 1, pl.ds(plane, 1), lanes]
                    v_r = shifted[slot, 0, col_two, :, lanes]
                    v_i = shifted[slot, 1, col_two, :, lanes]
                    term_r = u_r * v_r - u_i * v_i
                    term_i = u_r * v_i + u_i * v_r
                    f_r = term_r if f_r is None else f_r + term_r
                    f_i = term_i if f_i is None else f_i + term_i
                for kind in range(2):
                    for hel in range(n_h):
                        p_r = phi_ref[kind, hel, direc, 0, pl.ds(plane, 1), lanes]
                        p_i = phi_ref[kind, hel, direc, 1, pl.ds(plane, 1), lanes]
                        g_r = p_r * f_r - p_i * f_i
                        g_i = p_r * f_i + p_i * f_r
                        if (kind, hel) in acc:
                            old_r, old_i = acc[kind, hel]
                            g_r, g_i = old_r + g_r, old_i + g_i
                        acc[kind, hel] = (g_r, g_i)
            for (kind, hel), both in acc.items():
                store(kind, hel, col, half, both)


def plane_kernel(plane, dirs, has_part, n_out, *refs):
    refs = list(refs)
    v_ref = refs.pop(0)
    next_ref = refs.pop(0) if 0 in dirs else None
    u_ref, phi_ref = refs.pop(0), refs.pop(0)
    part_ref = refs.pop(0) if has_part else None
    keep_ref = refs.pop(0) if n_out else None
    give_ref = refs.pop(0) if n_out else None
    sum_ref, mat_ref, one_ref, two_ref, sh_ref = refs
    n_h = phi_ref.shape[1]
    _, _, n_b, width = v_ref.shape
    bufs = (one_ref, two_ref)
    last = n_b // BLOCK - 1

    for col in range(3):
        mat_ref[:, pl.ds(col * width, width)] = v_ref[:, col].reshape(2 * n_b, width)

    def fill(which, buf):
        for sub in range(BLOCK // ROWS):
            rows = pl.ds(pl.multiple_of(which * BLOCK + sub * ROWS, ROWS), ROWS)
            shifted = sh_ref.at[buf, sub]
            for slot, direc in enumerate(dirs):
                for part in range(2):
                    for col in range(3):
                        source = next_ref if direc == 0 else v_ref
                        field = source[part, col, rows, :].astype(jnp.float32)
                        if direc == 1:
                            field = shift_y(field)
                        elif direc == 2:
                            field = shift_z(field)
                        shifted[slot, part, col] = field

            def store(kind, hel, col, half, both, sub=sub):
                for part in range(2):
                    row = ((kind * n_h + hel) * 2 + part) * BLOCK + sub * ROWS
                    lanes = pl.ds(col * width + half * HALF, HALF)
                    bufs[buf][pl.ds(row, ROWS), lanes] = both[part].astype(jnp.bfloat16)

            weighted_links(u_ref, phi_ref, shifted, dirs, plane, n_h, store)

    def contract(which, buf):
        rows = pl.ds(pl.multiple_of(which * BLOCK, BLOCK), BLOCK)
        prod = dot_nt(bufs[buf][...], mat_ref[...])
        for kind in range(2):
            for hel in range(n_h):
                row = (kind * n_h + hel) * 2 * BLOCK
                re_row, im_row = prod[row : row + BLOCK], prod[row + BLOCK : row + 2 * BLOCK]
                real = re_row[:, :n_b] + im_row[:, n_b:]
                if kind:
                    imag = re_row[:, n_b:] - im_row[:, :n_b]
                else:
                    imag = im_row[:, :n_b] - re_row[:, n_b:]
                for part, total in enumerate((real, imag)):
                    if has_part:
                        total = total + part_ref[kind, hel, part, rows, :]
                    sum_ref[kind, hel, part, rows, :] = total

    fill(0, 0)

    def pair(step, carry):
        fill(2 * step + 1, 1)
        contract(2 * step, 0)
        fill(2 * step + 2, 0)
        contract(2 * step + 1, 1)
        return carry

    lax.fori_loop(0, last // 2, pair, 0)
    fill(last, 1)
    contract(last - 1, 0)
    contract(last, 1)

    if n_out:
        core = lax.axis_index("space") & 1
        for hel in range(n_h):
            for part in range(2):
                total = jnp.transpose(sum_ref[0, hel, part]) + sum_ref[1, hel, part]
                halves = total.reshape(n_out // 2, 2, n_b // n_out, n_b)
                keep_ref[:, hel, part] = jnp.where(core == 0, halves[:, 0], halves[:, 1])
                give = jnp.where(core == 0, halves[:, 1], halves[:, 0])
                give_ref[:, hel, part] = give.astype(jnp.bfloat16)


def plane_call(plane, dirs, vec, ahead, link, phi, part=None, n_out=0):
    n_h = phi.shape[1]
    _, _, n_b, width = vec.shape
    vmem = pl.BlockSpec(memory_space=pltpu.VMEM)
    args = [vec] + ([ahead] if 0 in dirs else []) + [link, phi]
    args += [part] if part is not None else []
    specs = [vmem] * len(args)
    sums = (2, n_h, 2, n_b, n_b)
    scratch = [
        pltpu.VMEM((2 * n_b, 3 * width), jnp.bfloat16),
        pltpu.VMEM((4 * n_h * BLOCK, 3 * width), jnp.bfloat16),
        pltpu.VMEM((4 * n_h * BLOCK, 3 * width), jnp.bfloat16),
        pltpu.VMEM((2, BLOCK // ROWS, len(dirs), 2, 3, ROWS, width), jnp.float32),
    ]
    if n_out:
        scratch.insert(0, pltpu.VMEM(sums, jnp.float32))
        blocks = (n_out // 2, n_h, 2, n_b // n_out, n_b)
        out_shape = [
            jax.ShapeDtypeStruct(blocks, jnp.float32),
            jax.ShapeDtypeStruct(blocks, jnp.bfloat16),
        ]
        out_specs = [vmem, vmem]
    else:
        out_shape = jax.ShapeDtypeStruct(sums, jnp.float32)
        out_specs = vmem
    return pl.pallas_call(
        functools.partial(plane_kernel, plane, dirs, part is not None, n_out),
        in_specs=specs,
        out_specs=out_specs,
        out_shape=out_shape,
        scratch_shapes=scratch,
        compiler_params=pltpu.CompilerParams(vmem_limit_bytes=VMEM_BYTES),
        cost_estimate=pl.CostEstimate(
            flops=2**34,
            bytes_accessed=2**28,
            transcendentals=0,
        ),
        name="plane%d_%s" % (plane, "".join(str(direc) for direc in dirs)),
    )(*args)


def merge_kernel(keep_ref, got_ref, own_ref, *out_refs):
    chip = lax.axis_index("space") >> 1
    shape = own_ref.shape
    own_ref[...] = (keep_ref[chip] + got_ref[chip].astype(jnp.float32)).reshape(shape)
    for mask, out_ref in enumerate(out_refs, 1):
        total = keep_ref[chip ^ mask] + got_ref[chip ^ mask].astype(jnp.float32)
        out_ref[...] = total.reshape(shape).astype(jnp.bfloat16)


def merge_call(keep, got):
    chips, n_h, _, own, n_b = keep.shape
    shape = (n_h * 2 * own, n_b)
    vmem = pl.BlockSpec(memory_space=pltpu.VMEM)
    return pl.pallas_call(
        merge_kernel,
        in_specs=[vmem, vmem],
        out_specs=[vmem] * chips,
        out_shape=[jax.ShapeDtypeStruct(shape, jnp.float32)]
        + [jax.ShapeDtypeStruct(shape, jnp.bfloat16)] * (chips - 1),
        compiler_params=pltpu.CompilerParams(vmem_limit_bytes=8 * 2**20),
        cost_estimate=pl.CostEstimate(flops=2**16, bytes_accessed=2**12, transcendentals=0),
        name="merge_cores",
    )(keep, got)


def pack_kernel(*refs):
    for which, ref in enumerate(refs[:-1]):
        refs[-1][which] = ref[...]


def pack_call(arrs):
    vmem = pl.BlockSpec(memory_space=pltpu.VMEM)
    return pl.pallas_call(
        pack_kernel,
        in_specs=[vmem] * len(arrs),
        out_specs=vmem,
        out_shape=jax.ShapeDtypeStruct((len(arrs),) + arrs[0].shape, arrs[0].dtype),
        compiler_params=pltpu.CompilerParams(vmem_limit_bytes=8 * 2**20),
        cost_estimate=pl.CostEstimate(flops=2**16, bytes_accessed=2**12, transcendentals=0),
        name="pack_pieces",
    )(*arrs)


def quark_kernel(masks, n_op, n_got, n_tau, n_h, *refs):
    got_refs = refs[:n_got]
    tau_refs = refs[n_got : n_got + n_tau]
    out_ref, left_ref = refs[n_got + n_tau :]
    my_space, my_op = lax.axis_index("space"), lax.axis_index("op")
    _, n_pair, _, own, n_b = out_ref.shape
    row = lax.broadcasted_iota(jnp.int32, (n_b, 2 * n_b), 0)
    col = lax.broadcasted_iota(jnp.int32, (n_b, 2 * n_b), 1)
    even = (col == 2 * row).astype(jnp.bfloat16)
    odd = (col == 2 * row + 1).astype(jnp.bfloat16)
    total = got_refs[0][...]
    for ref in got_refs[1:]:
        total = total + ref[...].astype(jnp.float32)
    swap = []
    for hel in range(n_h):
        start = hel * 2 * own
        swap += [-total[start + own : start + 2 * own], total[start : start + own]]
    left = jnp.dot(total.astype(jnp.bfloat16), even, preferred_element_type=jnp.float32)
    left += jnp.dot(
        jnp.concatenate(swap, 0).astype(jnp.bfloat16), odd, preferred_element_type=jnp.float32
    )
    left_ref[...] = left.astype(jnp.bfloat16)
    tau = []
    for ref in tau_refs:
        tau += [ref.at[which] for which in range(ref.shape[0])] if len(ref.shape) == 3 else [ref]
    depth = tau[0].shape[0]
    whole = depth == 2 * n_b
    if not whole:
        out_ref[...] = jnp.zeros_like(out_ref)
    for which, (mask, mask_op) in enumerate(masks):
        first = ((my_space ^ mask) * n_op + (my_op ^ mask_op)) * depth
        pair = first // (2 * n_b)
        if whole:
            lhs = left_ref[...]
        else:
            lhs = left_ref[:, pl.ds(pl.multiple_of(first - pair * 2 * n_b, depth), depth)]
        res = jnp.dot(lhs, tau[which][...], preferred_element_type=jnp.float32)
        for hel in range(n_h):
            for part in range(2):
                start = (hel * 2 + part) * own
                if whole:
                    out_ref[hel, pair, part] = res[start : start + own]
                else:
                    out_ref[hel, pair, part] += res[start : start + own]


def phase_kernel(n_op, n_x, planes, *refs):
    mom_refs = refs[:n_op]
    num_refs = refs[n_op : 2 * n_op]
    den_ref, out_ref = refs[2 * n_op :]
    my_space, my_op = lax.axis_index("space"), lax.axis_index("op")
    _, n_h, _, _, _, width = out_ref.shape
    n_mom = mom_refs[0].shape[0]
    moms = [(op, k) for op in range(n_op) for k in range(n_mom)]
    scale = 1.0 / math.sqrt(3.0 * n_x * LY * LZ)
    shape = (planes * len(moms), width)
    row = lax.broadcasted_iota(jnp.int32, shape, 0)
    lane = lax.broadcasted_iota(jnp.int32, shape, 1)
    yy = lane // LZ
    zz = lane & (LZ - 1)

    def spread(values):
        res = jnp.full(shape, values[0], jnp.int32)
        for which in range(1, len(values)):
            res = jnp.where(row == which, values[which], res)
        return res

    comps = [[mom_refs[op][k, axis] for _ in range(planes) for op, k in moms] for axis in range(3)]
    mom_x, mom_y, mom_z = [spread(comp) for comp in comps]
    pos_x = my_space * planes + row // len(moms)
    steps = ((0, 0, 0), (1, 0, 0), (0, 1, 0), (0, 0, 1))
    waves = []
    for step_x, step_y, step_z in steps:
        turn_x = lax.rem(mom_x * (pos_x + step_x), n_x).astype(jnp.float32) * (1.0 / n_x)
        turn_y = ((mom_y * (yy + step_y)) & (LY - 1)).astype(jnp.float32) * (1.0 / LY)
        turn_z = ((mom_z * (zz + step_z)) & (LZ - 1)).astype(jnp.float32) * (1.0 / LZ)
        turn = turn_x + turn_y + turn_z
        theta = (2.0 * math.pi) * (turn - jnp.floor(turn))
        waves.append((jnp.cos(theta), jnp.sin(theta)))
    for hel in range(n_h):
        which_h = my_op * n_h + hel
        den = jnp.full((1, width), den_ref[which_h], jnp.int32).astype(jnp.float32)
        for direc in range(NDIR):
            wts = []
            for op, k in moms:
                num = num_refs[op][direc, k, which_h]
                wts.append(jnp.full((1, width), num, jnp.int32).astype(jnp.float32) / den * scale)
            for kind, wave in ((0, waves[0]), (1, waves[1 + direc])):
                for plane in range(planes):
                    start = plane * len(moms)
                    real = sum(wt * wave[0][start + at : start + at + 1] for at, wt in enumerate(wts))
                    imag = sum(wt * wave[1][start + at : start + at + 1] for at, wt in enumerate(wts))
                    out_ref[kind, hel, direc, 0, plane : plane + 1, :] = -real if kind else real
                    out_ref[kind, hel, direc, 1, plane : plane + 1, :] = -imag


def shards(eigvecs, links, momenta, coef_num, coef_den, peram):
    n_space = lax.axis_size("space")
    n_op = lax.axis_size("op")
    n_tm = lax.axis_size("tm")
    _, _, n_b, _, planes, width = eigvecs.shape
    n_x = planes * n_space
    own = n_b // n_space
    n_h = coef_num.shape[0] // n_op
    my_op = lax.axis_index("op")
    my_space = lax.axis_index("space")

    nums = jnp.transpose(coef_num, (2, 1, 0))
    both = [(momenta, nums)]
    both += [(across(momenta, "op", mask), across(nums, "op", mask)) for mask in range(1, n_op)]

    group = n_space * n_op
    depth = n_b * SPINS // group
    first = (my_space * n_op + my_op) * depth
    piece = lax.dynamic_slice(
        peram.reshape(n_b, SPINS, 2, n_b), (first % n_b, first // n_b, 0, 0), (depth, 1, 2, n_b)
    ).reshape(depth * 2, n_b)

    moved = lax.optimization_barrier(jnp.transpose(eigvecs[0], (3, 0, 2, 1, 4)))
    own_piece = from_behind(piece, "tm", n_tm - 1)
    vecs = [moved[plane] for plane in range(planes)]
    upper = from_behind(vecs[0], "space", -1)

    smem = pl.BlockSpec(memory_space=pltpu.SMEM)
    vmem = pl.BlockSpec(memory_space=pltpu.VMEM)
    phi = pl.pallas_call(
        functools.partial(phase_kernel, n_op, n_x, planes),
        in_specs=[smem] * (2 * n_op + 1),
        out_specs=vmem,
        out_shape=jax.ShapeDtypeStruct((2, n_h, NDIR, 2, planes, width), jnp.float32),
        compiler_params=pltpu.CompilerParams(vmem_limit_bytes=4 * 2**20),
        name="phases",
    )(*[mom for mom, _ in both], *[num for _, num in both], coef_den)

    dims = [("op", 1 << bit) for bit in range(n_op.bit_length() - 1)]
    dims += [("space", 1 << bit) for bit in range(1, n_space.bit_length() - 1)]
    load = [0] * len(dims)

    def stage(held, size):
        for group_dims in itertools.combinations(range(len(dims)), size):
            dim = min(group_dims, key=lambda at: load[at])
            load[dim] += 1
            before = held[tuple(at for at in group_dims if at != dim)]
            held[group_dims] = across(before, *dims[dim])

    def hold(held, other):
        arrs, other = lax.optimization_barrier((list(held.values()), other))
        return dict(zip(held.keys(), arrs)), other

    link = links[0]
    last = planes - 1
    corner = tuple(range(len(dims)))
    partial = plane_call(last, (1, 2), vecs[last], None, link, phi)
    held, partial = hold({(): own_piece}, partial)
    stage(held, 1)
    if len(dims) > 2:
        far = diagonal(held[()], n_space, n_op)
    for plane in range(last):
        partial = plane_call(plane, (1, 2, 0), vecs[plane], vecs[plane + 1], link, phi, partial)
    keep, give = plane_call(last, (0,), vecs[last], upper, link, phi, partial, n_space)
    swapped = across(give, "space", 1)
    early = list(held)
    if len(dims) > 2:
        held[corner] = far
    held, keep = hold(held, keep)
    flipped = [across(pack_call([held[key] for key in early]), "space", 1)]
    for size in range(2, len(dims) if len(dims) > 2 else 3):
        stage(held, size)
    late = [key for key in held if key not in early]
    merged = merge_call(keep, swapped)
    got = [merged[0]] + [across(arr, "space", 2 * mask) for mask, arr in enumerate(merged[1:], 1)]
    after, got = hold({key: held[key] for key in late}, got)
    held.update(after)
    flipped.append(across(pack_call([held[key] for key in late]), "space", 1))
    tau = [held[key] for key in early + late] + flipped
    masks = []
    for flip in range(2):
        for group_dims in early + late:
            mask = {"space": flip, "op": 0}
            for at in group_dims:
                mask[dims[at][0]] ^= dims[at][1]
            masks.append((mask["space"], mask["op"]))

    lines = pl.pallas_call(
        functools.partial(quark_kernel, masks, n_op, len(got), len(tau), n_h),
        in_specs=[vmem] * (len(got) + len(tau)),
        out_specs=vmem,
        out_shape=jax.ShapeDtypeStruct((n_h, SPINS, 2, own, n_b), jnp.float32),
        scratch_shapes=[
            pltpu.VMEM((n_h * 2 * own, 2 * n_b), jnp.bfloat16),
        ],
        compiler_params=pltpu.CompilerParams(vmem_limit_bytes=VMEM_BYTES),
        cost_estimate=pl.CostEstimate(
            flops=2 * SPINS * n_h * 2 * own * 2 * n_b * n_b, bytes_accessed=7 * 2**20, transcendentals=0
        ),
        name="quark_products",
    )(*got, *tau)
    return lines.reshape(1, n_h, 4, 4, 2, own, n_b)


def solution(mesh):
    return jax.shard_map(
        shards,
        mesh=mesh,
        in_specs=(
            P("tm", None, None, None, "space", None),
            P("tm", None, None, None, None, "space", None),
            P("op", None),
            P(None, "op", None),
            P(),
            P("tm", None, None, None, None, None),
        ),
        out_specs=P("tm", "op", None, None, None, "space", None),
        check_vma=False,
    )
```

```python
import functools
import itertools
import math

import jax
import jax.numpy as jnp
from jax import lax
from jax.experimental import pallas as pl
from jax.experimental.pallas import tpu as pltpu
from jax.sharding import PartitionSpec as P

LY = 32
LZ = 8
NDIR = 3
SPINS = 16
ROWS = 16
HALF = 128
BLOCK = 32
VMEM_BYTES = 20 * 2**20


def from_behind(value, axis, steps):
    count = lax.axis_size(axis)
    pairs = [(source, (source + steps) % count) for source in range(count)]
    return lax.ppermute(value, axis, pairs)


def across(value, axis, mask):
    pairs = [(source, source ^ mask) for source in range(lax.axis_size(axis))]
    return lax.ppermute(value, axis, pairs)


def diagonal(value, n_space, n_op):
    pairs = []
    for space in range(n_space):
        for oper in range(n_op):
            target = (space ^ (n_space - 2)) * n_op + (oper ^ (n_op - 1))
            pairs.append((space * n_op + oper, target))
    return lax.ppermute(value, ("space", "op"), pairs)


def dot_nt(left, right):
    return lax.dot_general(
        left, right, (((1,), (1,)), ((), ())), preferred_element_type=jnp.float32
    )


def shift_y(arr):
    return pltpu.roll(arr, arr.shape[1] - LZ, 1)


def shift_z(arr):
    width = arr.shape[1]
    lane = lax.broadcasted_iota(jnp.int32, arr.shape, 1)
    near = pltpu.roll(arr, width - 1, 1)
    far = pltpu.roll(arr, LZ - 1, 1)
    return jnp.where((lane & (LZ - 1)) == LZ - 1, far, near)


def weighted_links(u_ref, phi_ref, shifted, dirs, plane, n_h, store):
    width = u_ref.shape[-1]
    for half in range(width // HALF):
        lanes = pl.ds(half * HALF, HALF)
        for col in range(3):
            acc = {}
            for slot, direc in enumerate(dirs):
                f_r = None
                f_i = None
                for col_two in range(3):
                    u_r = u_ref[direc, col, col_two, 0, pl.ds(plane, 1), lanes]
                    u_i = u_ref[direc, col, col_two, 1, pl.ds(plane, 1), lanes]
                    v_r = shifted[slot, 0, col_two, :, lanes]
                    v_i = shifted[slot, 1, col_two, :, lanes]
                    term_r = u_r * v_r - u_i * v_i
                    term_i = u_r * v_i + u_i * v_r
                    f_r = term_r if f_r is None else f_r + term_r
                    f_i = term_i if f_i is None else f_i + term_i
                for kind in range(2):
                    for hel in range(n_h):
                        p_r = phi_ref[kind, hel, direc, 0, pl.ds(plane, 1), lanes]
                        p_i = phi_ref[kind, hel, direc, 1, pl.ds(plane, 1), lanes]
                        g_r = p_r * f_r - p_i * f_i
                        g_i = p_r * f_i + p_i * f_r
                        if (kind, hel) in acc:
                            old_r, old_i = acc[kind, hel]
                            g_r, g_i = old_r + g_r, old_i + g_i
                        acc[kind, hel] = (g_r, g_i)
            for (kind, hel), both in acc.items():
                store(kind, hel, col, half, both)


def plane_kernel(plane, dirs, has_part, n_out, *refs):
    refs = list(refs)
    v_ref = refs.pop(0)
    next_ref = refs.pop(0) if 0 in dirs else None
    u_ref, phi_ref = refs.pop(0), refs.pop(0)
    part_ref = refs.pop(0) if has_part else None
    keep_ref = refs.pop(0) if n_out else None
    give_ref = refs.pop(0) if n_out else None
    sum_ref, mat_ref, one_ref, two_ref, sh_ref = refs
    n_h = phi_ref.shape[1]
    _, _, n_b, width = v_ref.shape
    bufs = (one_ref, two_ref)
    last = n_b // BLOCK - 1

    for col in range(3):
        mat_ref[:, pl.ds(col * width, width)] = v_ref[:, col].reshape(2 * n_b, width)

    def fill(which, buf):
        for sub in range(BLOCK // ROWS):
            rows = pl.ds(pl.multiple_of(which * BLOCK + sub * ROWS, ROWS), ROWS)
            shifted = sh_ref.at[buf, sub]
            for slot, direc in enumerate(dirs):
                for part in range(2):
                    for col in range(3):
                        source = next_ref if direc == 0 else v_ref
                        field = source[part, col, rows, :].astype(jnp.float32)
                        if direc == 1:
                            field = shift_y(field)
                        elif direc == 2:
                            field = shift_z(field)
                        shifted[slot, part, col] = field

            def store(kind, hel, col, half, both, sub=sub):
                for part in range(2):
                    row = ((kind * n_h + hel) * 2 + part) * BLOCK + sub * ROWS
                    lanes = pl.ds(col * width + half * HALF, HALF)
                    bufs[buf][pl.ds(row, ROWS), lanes] = both[part].astype(jnp.bfloat16)

            weighted_links(u_ref, phi_ref, shifted, dirs, plane, n_h, store)

    def contract(which, buf):
        rows = pl.ds(pl.multiple_of(which * BLOCK, BLOCK), BLOCK)
        prod = dot_nt(bufs[buf][...], mat_ref[...])
        for kind in range(2):
            for hel in range(n_h):
                row = (kind * n_h + hel) * 2 * BLOCK
                re_row, im_row = prod[row : row + BLOCK], prod[row + BLOCK : row + 2 * BLOCK]
                real = re_row[:, :n_b] + im_row[:, n_b:]
                if kind:
                    imag = re_row[:, n_b:] - im_row[:, :n_b]
                else:
                    imag = im_row[:, :n_b] - re_row[:, n_b:]
                for part, total in enumerate((real, imag)):
                    if has_part:
                        total = total + part_ref[kind, hel, part, rows, :]
                    sum_ref[kind, hel, part, rows, :] = total

    fill(0, 0)

    def pair(step, carry):
        fill(2 * step + 1, 1)
        contract(2 * step, 0)
        fill(2 * step + 2, 0)
        contract(2 * step + 1, 1)
        return carry

    lax.fori_loop(0, last // 2, pair, 0)
    fill(last, 1)
    contract(last - 1, 0)
    contract(last, 1)

    if n_out:
        core = lax.axis_index("space") & 1
        for hel in range(n_h):
            for part in range(2):
                total = jnp.transpose(sum_ref[0, hel, part]) + sum_ref[1, hel, part]
                halves = total.reshape(n_out // 2, 2, n_b // n_out, n_b)
                keep_ref[:, hel, part] = jnp.where(core == 0, halves[:, 0], halves[:, 1])
                give = jnp.where(core == 0, halves[:, 1], halves[:, 0])
                give_ref[:, hel, part] = give.astype(jnp.bfloat16)


def plane_call(plane, dirs, vec, ahead, link, phi, part=None, n_out=0):
    n_h = phi.shape[1]
    _, _, n_b, width = vec.shape
    vmem = pl.BlockSpec(memory_space=pltpu.VMEM)
    args = [vec] + ([ahead] if 0 in dirs else []) + [link, phi]
    args += [part] if part is not None else []
    specs = [vmem] * len(args)
    sums = (2, n_h, 2, n_b, n_b)
    scratch = [
        pltpu.VMEM((2 * n_b, 3 * width), jnp.bfloat16),
        pltpu.VMEM((4 * n_h * BLOCK, 3 * width), jnp.bfloat16),
        pltpu.VMEM((4 * n_h * BLOCK, 3 * width), jnp.bfloat16),
        pltpu.VMEM((2, BLOCK // ROWS, len(dirs), 2, 3, ROWS, width), jnp.float32),
    ]
    if n_out:
        scratch.insert(0, pltpu.VMEM(sums, jnp.float32))
        blocks = (n_out // 2, n_h, 2, n_b // n_out, n_b)
        out_shape = [
            jax.ShapeDtypeStruct(blocks, jnp.float32),
            jax.ShapeDtypeStruct(blocks, jnp.bfloat16),
        ]
        out_specs = [vmem, vmem]
    else:
        out_shape = jax.ShapeDtypeStruct(sums, jnp.float32)
        out_specs = vmem
    return pl.pallas_call(
        functools.partial(plane_kernel, plane, dirs, part is not None, n_out),
        in_specs=specs,
        out_specs=out_specs,
        out_shape=out_shape,
        scratch_shapes=scratch,
        compiler_params=pltpu.CompilerParams(vmem_limit_bytes=VMEM_BYTES),
        cost_estimate=pl.CostEstimate(
            flops=2**34,
            bytes_accessed=2**28,
            transcendentals=0,
        ),
        name="plane%d_%s" % (plane, "".join(str(direc) for direc in dirs)),
    )(*args)


def merge_kernel(bit, keep_ref, got_ref, next_ref, give_ref):
    mine = (lax.axis_index("space") >> bit) & 1
    total = keep_ref[...] + got_ref[...].astype(jnp.float32)
    halves = total.reshape((total.shape[0] // 2, 2) + total.shape[1:])
    next_ref[...] = jnp.where(mine == 0, halves[:, 0], halves[:, 1])
    give_ref[...] = jnp.where(mine == 0, halves[:, 1], halves[:, 0]).astype(jnp.bfloat16)


def merge_call(keep, got, bit):
    shape = (keep.shape[0] // 2,) + keep.shape[1:]
    vmem = pl.BlockSpec(memory_space=pltpu.VMEM)
    return pl.pallas_call(
        functools.partial(merge_kernel, bit),
        in_specs=[vmem, vmem],
        out_specs=[vmem, vmem],
        out_shape=[jax.ShapeDtypeStruct(shape, jnp.float32), jax.ShapeDtypeStruct(shape, jnp.bfloat16)],
        compiler_params=pltpu.CompilerParams(vmem_limit_bytes=8 * 2**20),
        cost_estimate=pl.CostEstimate(flops=2**16, bytes_accessed=2**12, transcendentals=0),
        name="merge_bit%d" % bit,
    )(keep, got)


def pack_kernel(*refs):
    for which, ref in enumerate(refs[:-1]):
        refs[-1][which] = ref[...]


def pack_call(arrs):
    vmem = pl.BlockSpec(memory_space=pltpu.VMEM)
    return pl.pallas_call(
        pack_kernel,
        in_specs=[vmem] * len(arrs),
        out_specs=vmem,
        out_shape=jax.ShapeDtypeStruct((len(arrs),) + arrs[0].shape, arrs[0].dtype),
        compiler_params=pltpu.CompilerParams(vmem_limit_bytes=8 * 2**20),
        cost_estimate=pl.CostEstimate(flops=2**16, bytes_accessed=2**12, transcendentals=0),
        name="pack_pieces",
    )(*arrs)


def quark_kernel(masks, n_op, n_got, n_tau, n_h, *refs):
    got_refs = refs[:n_got]
    tau_refs = refs[n_got : n_got + n_tau]
    out_ref, left_ref = refs[n_got + n_tau :]
    my_space, my_op = lax.axis_index("space"), lax.axis_index("op")
    _, n_pair, _, own, n_b = out_ref.shape
    row = lax.broadcasted_iota(jnp.int32, (n_b, 2 * n_b), 0)
    col = lax.broadcasted_iota(jnp.int32, (n_b, 2 * n_b), 1)
    even = (col == 2 * row).astype(jnp.bfloat16)
    odd = (col == 2 * row + 1).astype(jnp.bfloat16)
    total = got_refs[0][0] + got_refs[1][0].astype(jnp.float32)
    total = total.reshape(n_h * 2 * own, n_b)
    swap = []
    for hel in range(n_h):
        start = hel * 2 * own
        swap += [-total[start + own : start + 2 * own], total[start : start + own]]
    left = jnp.dot(total.astype(jnp.bfloat16), even, preferred_element_type=jnp.float32)
    left += jnp.dot(
        jnp.concatenate(swap, 0).astype(jnp.bfloat16), odd, preferred_element_type=jnp.float32
    )
    left_ref[...] = left.astype(jnp.bfloat16)
    tau = []
    for ref in tau_refs:
        tau += [ref.at[which] for which in range(ref.shape[0])] if len(ref.shape) == 3 else [ref]
    depth = tau[0].shape[0]
    whole = depth == 2 * n_b
    if not whole:
        out_ref[...] = jnp.zeros_like(out_ref)
    for which, (mask, mask_op) in enumerate(masks):
        first = ((my_space ^ mask) * n_op + (my_op ^ mask_op)) * depth
        pair = first // (2 * n_b)
        if whole:
            lhs = left_ref[...]
        else:
            lhs = left_ref[:, pl.ds(pl.multiple_of(first - pair * 2 * n_b, depth), depth)]
        res = jnp.dot(lhs, tau[which][...], preferred_element_type=jnp.float32)
        for hel in range(n_h):
            for part in range(2):
                start = (hel * 2 + part) * own
                if whole:
                    out_ref[hel, pair, part] = res[start : start + own]
                else:
                    out_ref[hel, pair, part] += res[start : start + own]


def phase_kernel(n_op, n_x, planes, *refs):
    mom_refs = refs[:n_op]
    num_refs = refs[n_op : 2 * n_op]
    den_ref, out_ref = refs[2 * n_op :]
    my_space, my_op = lax.axis_index("space"), lax.axis_index("op")
    _, n_h, _, _, _, width = out_ref.shape
    n_mom = mom_refs[0].shape[0]
    moms = [(op, k) for op in range(n_op) for k in range(n_mom)]
    scale = 1.0 / math.sqrt(3.0 * n_x * LY * LZ)
    shape = (planes * len(moms), width)
    row = lax.broadcasted_iota(jnp.int32, shape, 0)
    lane = lax.broadcasted_iota(jnp.int32, shape, 1)
    yy = lane // LZ
    zz = lane & (LZ - 1)

    def spread(values):
        res = jnp.full(shape, values[0], jnp.int32)
        for which in range(1, len(values)):
            res = jnp.where(row == which, values[which], res)
        return res

    comps = [[mom_refs[op][k, axis] for _ in range(planes) for op, k in moms] for axis in range(3)]
    mom_x, mom_y, mom_z = [spread(comp) for comp in comps]
    pos_x = my_space * planes + row // len(moms)
    steps = ((0, 0, 0), (1, 0, 0), (0, 1, 0), (0, 0, 1))
    waves = []
    for step_x, step_y, step_z in steps:
        turn_x = lax.rem(mom_x * (pos_x + step_x), n_x).astype(jnp.float32) * (1.0 / n_x)
        turn_y = ((mom_y * (yy + step_y)) & (LY - 1)).astype(jnp.float32) * (1.0 / LY)
        turn_z = ((mom_z * (zz + step_z)) & (LZ - 1)).astype(jnp.float32) * (1.0 / LZ)
        turn = turn_x + turn_y + turn_z
        theta = (2.0 * math.pi) * (turn - jnp.floor(turn))
        waves.append((jnp.cos(theta), jnp.sin(theta)))
    for hel in range(n_h):
        which_h = my_op * n_h + hel
        den = jnp.full((1, width), den_ref[which_h], jnp.int32).astype(jnp.float32)
        for direc in range(NDIR):
            wts = []
            for op, k in moms:
                num = num_refs[op][direc, k, which_h]
                wts.append(jnp.full((1, width), num, jnp.int32).astype(jnp.float32) / den * scale)
            for kind, wave in ((0, waves[0]), (1, waves[1 + direc])):
                for plane in range(planes):
                    start = plane * len(moms)
                    real = sum(wt * wave[0][start + at : start + at + 1] for at, wt in enumerate(wts))
                    imag = sum(wt * wave[1][start + at : start + at + 1] for at, wt in enumerate(wts))
                    out_ref[kind, hel, direc, 0, plane : plane + 1, :] = -real if kind else real
                    out_ref[kind, hel, direc, 1, plane : plane + 1, :] = -imag


def shards(eigvecs, links, momenta, coef_num, coef_den, peram):
    n_space = lax.axis_size("space")
    n_op = lax.axis_size("op")
    n_tm = lax.axis_size("tm")
    _, _, n_b, _, planes, width = eigvecs.shape
    n_x = planes * n_space
    own = n_b // n_space
    n_h = coef_num.shape[0] // n_op
    my_op = lax.axis_index("op")
    my_space = lax.axis_index("space")

    nums = jnp.transpose(coef_num, (2, 1, 0))
    both = [(momenta, nums)]
    both += [(across(momenta, "op", mask), across(nums, "op", mask)) for mask in range(1, n_op)]

    group = n_space * n_op
    depth = n_b * SPINS // group
    first = (my_space * n_op + my_op) * depth
    piece = lax.dynamic_slice(
        peram.reshape(n_b, SPINS, 2, n_b), (first % n_b, first // n_b, 0, 0), (depth, 1, 2, n_b)
    ).reshape(depth * 2, n_b)

    moved = lax.optimization_barrier(jnp.transpose(eigvecs[0], (3, 0, 2, 1, 4)))
    own_piece = from_behind(piece, "tm", n_tm - 1)
    vecs = [moved[plane] for plane in range(planes)]
    upper = from_behind(vecs[0], "space", -1)

    smem = pl.BlockSpec(memory_space=pltpu.SMEM)
    vmem = pl.BlockSpec(memory_space=pltpu.VMEM)
    phi = pl.pallas_call(
        functools.partial(phase_kernel, n_op, n_x, planes),
        in_specs=[smem] * (2 * n_op + 1),
        out_specs=vmem,
        out_shape=jax.ShapeDtypeStruct((2, n_h, NDIR, 2, planes, width), jnp.float32),
        compiler_params=pltpu.CompilerParams(vmem_limit_bytes=4 * 2**20),
        name="phases",
    )(*[mom for mom, _ in both], *[num for _, num in both], coef_den)

    dims = [("op", 1 << bit) for bit in range(n_op.bit_length() - 1)]
    dims += [("space", 1 << bit) for bit in range(1, n_space.bit_length() - 1)]
    load = [0] * len(dims)

    def stage(held, size):
        for group_dims in itertools.combinations(range(len(dims)), size):
            dim = min(group_dims, key=lambda at: load[at])
            load[dim] += 1
            before = held[tuple(at for at in group_dims if at != dim)]
            held[group_dims] = across(before, *dims[dim])

    def hold(held, other):
        arrs, other = lax.optimization_barrier((list(held.values()), other))
        return dict(zip(held.keys(), arrs)), other

    link = links[0]
    last = planes - 1
    corner = tuple(range(len(dims)))
    partial = plane_call(last, (1, 2), vecs[last], None, link, phi)
    held, partial = hold({(): own_piece}, partial)
    stage(held, 1)
    if len(dims) > 2:
        far = diagonal(held[()], n_space, n_op)
    for plane in range(last):
        partial = plane_call(plane, (1, 2, 0), vecs[plane], vecs[plane + 1], link, phi, partial)
    keep, give = plane_call(last, (0,), vecs[last], upper, link, phi, partial, n_space)
    swapped = across(give, "space", 1)
    early = list(held)
    if len(dims) > 2:
        held[corner] = far
    held, keep = hold(held, keep)
    flipped = [across(pack_call([held[key] for key in early]), "space", 1)]
    for size in range(2, len(dims) if len(dims) > 2 else 3):
        stage(held, size)
    late = [key for key in held if key not in early]
    for bit in range(1, n_space.bit_length() - 1):
        keep, give = merge_call(keep, swapped, bit)
        if bit == n_space.bit_length() - 2:
            after, give = hold({key: held[key] for key in late}, give)
            held.update(after)
        swapped = across(give, "space", 1 << bit)
    got = [keep, swapped]
    flipped.append(across(pack_call([held[key] for key in late]), "space", 1))
    tau = [held[key] for key in early + late] + flipped
    masks = []
    for flip in range(2):
        for group_dims in early + late:
            mask = {"space": flip, "op": 0}
            for at in group_dims:
                mask[dims[at][0]] ^= dims[at][1]
            masks.append((mask["space"], mask["op"]))

    lines = pl.pallas_call(
        functools.partial(quark_kernel, masks, n_op, len(got), len(tau), n_h),
        in_specs=[vmem] * (len(got) + len(tau)),
        out_specs=vmem,
        out_shape=jax.ShapeDtypeStruct((n_h, SPINS, 2, own, n_b), jnp.float32),
        scratch_shapes=[
            pltpu.VMEM((n_h * 2 * own, 2 * n_b), jnp.bfloat16),
        ],
        compiler_params=pltpu.CompilerParams(vmem_limit_bytes=VMEM_BYTES),
        cost_estimate=pl.CostEstimate(
            flops=2 * SPINS * n_h * 2 * own * 2 * n_b * n_b, bytes_accessed=7 * 2**20, transcendentals=0
        ),
        name="quark_products",
    )(*got, *tau)
    return lines.reshape(1, n_h, 4, 4, 2, own, n_b)


def solution(mesh):
    return jax.shard_map(
        shards,
        mesh=mesh,
        in_specs=(
            P("tm", None, None, None, "space", None),
            P("tm", None, None, None, None, "space", None),
            P("op", None),
            P(None, "op", None),
            P(),
            P("tm", None, None, None, None, None),
        ),
        out_specs=P("tm", "op", None, None, None, "space", None),
        check_vma=False,
    )
```

```python
import functools
import itertools
import math

import jax
import jax.numpy as jnp
from jax import lax
from jax.experimental import pallas as pl
from jax.experimental.pallas import tpu as pltpu
from jax.sharding import PartitionSpec as P

LY = 32
LZ = 8
NDIR = 3
SPINS = 16
ROWS = 16
HALF = 128
BLOCK = 32
VMEM_BYTES = 20 * 2**20


def from_behind(value, axis, steps):
    count = lax.axis_size(axis)
    pairs = [(source, (source + steps) % count) for source in range(count)]
    return lax.ppermute(value, axis, pairs)


def across(value, axis, mask):
    pairs = [(source, source ^ mask) for source in range(lax.axis_size(axis))]
    return lax.ppermute(value, axis, pairs)


def diagonal(value, n_space, n_op):
    pairs = []
    for space in range(n_space):
        for oper in range(n_op):
            target = (space ^ (n_space - 2)) * n_op + (oper ^ (n_op - 1))
            pairs.append((space * n_op + oper, target))
    return lax.ppermute(value, ("space", "op"), pairs)


def dot_nt(left, right):
    return lax.dot_general(
        left, right, (((1,), (1,)), ((), ())), preferred_element_type=jnp.float32
    )


def shift_y(arr):
    return pltpu.roll(arr, arr.shape[1] - LZ, 1)


def shift_z(arr):
    width = arr.shape[1]
    lane = lax.broadcasted_iota(jnp.int32, arr.shape, 1)
    near = pltpu.roll(arr, width - 1, 1)
    far = pltpu.roll(arr, LZ - 1, 1)
    return jnp.where((lane & (LZ - 1)) == LZ - 1, far, near)


def weighted_links(u_ref, phi_ref, shifted, dirs, plane, n_h, store):
    width = u_ref.shape[-1]
    for half in range(width // HALF):
        lanes = pl.ds(half * HALF, HALF)
        for col in range(3):
            acc = {}
            for slot, direc in enumerate(dirs):
                f_r = None
                f_i = None
                for col_two in range(3):
                    u_r = u_ref[direc, col, col_two, 0, pl.ds(plane, 1), lanes]
                    u_i = u_ref[direc, col, col_two, 1, pl.ds(plane, 1), lanes]
                    v_r = shifted[slot, 0, col_two, :, lanes]
                    v_i = shifted[slot, 1, col_two, :, lanes]
                    term_r = u_r * v_r - u_i * v_i
                    term_i = u_r * v_i + u_i * v_r
                    f_r = term_r if f_r is None else f_r + term_r
                    f_i = term_i if f_i is None else f_i + term_i
                for kind in range(2):
                    for hel in range(n_h):
                        p_r = phi_ref[kind, hel, direc, 0, pl.ds(plane, 1), lanes]
                        p_i = phi_ref[kind, hel, direc, 1, pl.ds(plane, 1), lanes]
                        g_r = p_r * f_r - p_i * f_i
                        g_i = p_r * f_i + p_i * f_r
                        if (kind, hel) in acc:
                            old_r, old_i = acc[kind, hel]
                            g_r, g_i = old_r + g_r, old_i + g_i
                        acc[kind, hel] = (g_r, g_i)
            for (kind, hel), both in acc.items():
                store(kind, hel, col, half, both)


def plane_kernel(plane, dirs, has_part, n_out, *refs):
    refs = list(refs)
    v_ref = refs.pop(0)
    next_ref = refs.pop(0) if 0 in dirs else None
    u_ref, phi_ref = refs.pop(0), refs.pop(0)
    part_ref = refs.pop(0) if has_part else None
    keep_ref = refs.pop(0) if n_out else None
    give_ref = refs.pop(0) if n_out else None
    sum_ref, mat_ref, one_ref, two_ref, sh_ref = refs
    n_h = phi_ref.shape[1]
    _, _, n_b, width = v_ref.shape
    bufs = (one_ref, two_ref)
    last = n_b // BLOCK - 1

    for col in range(3):
        mat_ref[:, pl.ds(col * width, width)] = v_ref[:, col].reshape(2 * n_b, width)

    def fill(which, buf):
        for sub in range(BLOCK // ROWS):
            rows = pl.ds(pl.multiple_of(which * BLOCK + sub * ROWS, ROWS), ROWS)
            shifted = sh_ref.at[buf, sub]
            for slot, direc in enumerate(dirs):
                for part in range(2):
                    for col in range(3):
                        source = next_ref if direc == 0 else v_ref
                        field = source[part, col, rows, :].astype(jnp.float32)
                        if direc == 1:
                            field = shift_y(field)
                        elif direc == 2:
                            field = shift_z(field)
                        shifted[slot, part, col] = field

            def store(kind, hel, col, half, both, sub=sub):
                for part in range(2):
                    row = ((kind * n_h + hel) * 2 + part) * BLOCK + sub * ROWS
                    lanes = pl.ds(col * width + half * HALF, HALF)
                    bufs[buf][pl.ds(row, ROWS), lanes] = both[part].astype(jnp.bfloat16)

            weighted_links(u_ref, phi_ref, shifted, dirs, plane, n_h, store)

    def contract(which, buf):
        rows = pl.ds(pl.multiple_of(which * BLOCK, BLOCK), BLOCK)
        prod = dot_nt(bufs[buf][...], mat_ref[...])
        for kind in range(2):
            for hel in range(n_h):
                row = (kind * n_h + hel) * 2 * BLOCK
                re_row, im_row = prod[row : row + BLOCK], prod[row + BLOCK : row + 2 * BLOCK]
                real = re_row[:, :n_b] + im_row[:, n_b:]
                if kind:
                    imag = re_row[:, n_b:] - im_row[:, :n_b]
                else:
                    imag = im_row[:, :n_b] - re_row[:, n_b:]
                for part, total in enumerate((real, imag)):
                    if has_part:
                        total = total + part_ref[kind, hel, part, rows, :]
                    sum_ref[kind, hel, part, rows, :] = total

    fill(0, 0)

    def pair(step, carry):
        fill(2 * step + 1, 1)
        contract(2 * step, 0)
        fill(2 * step + 2, 0)
        contract(2 * step + 1, 1)
        return carry

    lax.fori_loop(0, last // 2, pair, 0)
    fill(last, 1)
    contract(last - 1, 0)
    contract(last, 1)

    if n_out:
        core = lax.axis_index("space") & 1
        for hel in range(n_h):
            for part in range(2):
                total = jnp.transpose(sum_ref[0, hel, part]) + sum_ref[1, hel, part]
                halves = total.reshape(n_out // 2, 2, n_b // n_out, n_b)
                keep_ref[:, hel, part] = jnp.where(core == 0, halves[:, 0], halves[:, 1])
                give = jnp.where(core == 0, halves[:, 1], halves[:, 0])
                give_ref[:, hel, part] = give.astype(jnp.bfloat16)


def plane_call(plane, dirs, vec, ahead, link, phi, part=None, n_out=0):
    n_h = phi.shape[1]
    _, _, n_b, width = vec.shape
    vmem = pl.BlockSpec(memory_space=pltpu.VMEM)
    args = [vec] + ([ahead] if 0 in dirs else []) + [link, phi]
    args += [part] if part is not None else []
    specs = [vmem] * len(args)
    sums = (2, n_h, 2, n_b, n_b)
    scratch = [
        pltpu.VMEM((2 * n_b, 3 * width), jnp.bfloat16),
        pltpu.VMEM((4 * n_h * BLOCK, 3 * width), jnp.bfloat16),
        pltpu.VMEM((4 * n_h * BLOCK, 3 * width), jnp.bfloat16),
        pltpu.VMEM((2, BLOCK // ROWS, len(dirs), 2, 3, ROWS, width), jnp.float32),
    ]
    if n_out:
        scratch.insert(0, pltpu.VMEM(sums, jnp.float32))
        blocks = (n_out // 2, n_h, 2, n_b // n_out, n_b)
        out_shape = [
            jax.ShapeDtypeStruct(blocks, jnp.float32),
            jax.ShapeDtypeStruct(blocks, jnp.bfloat16),
        ]
        out_specs = [vmem, vmem]
    else:
        out_shape = jax.ShapeDtypeStruct(sums, jnp.float32)
        out_specs = vmem
    return pl.pallas_call(
        functools.partial(plane_kernel, plane, dirs, part is not None, n_out),
        in_specs=specs,
        out_specs=out_specs,
        out_shape=out_shape,
        scratch_shapes=scratch,
        compiler_params=pltpu.CompilerParams(vmem_limit_bytes=VMEM_BYTES),
        cost_estimate=pl.CostEstimate(
            flops=2**34,
            bytes_accessed=2**28,
            transcendentals=0,
        ),
        name="plane%d_%s" % (plane, "".join(str(direc) for direc in dirs)),
    )(*args)


def merge_kernel(keep_ref, got_ref, own_ref, *out_refs):
    chip = lax.axis_index("space") >> 1
    shape = own_ref.shape
    own_ref[...] = (keep_ref[chip] + got_ref[chip].astype(jnp.float32)).reshape(shape)
    for mask, out_ref in enumerate(out_refs, 1):
        total = keep_ref[chip ^ mask] + got_ref[chip ^ mask].astype(jnp.float32)
        out_ref[...] = total.reshape(shape).astype(jnp.bfloat16)


def merge_call(keep, got):
    chips, n_h, _, own, n_b = keep.shape
    shape = (n_h * 2 * own, n_b)
    vmem = pl.BlockSpec(memory_space=pltpu.VMEM)
    return pl.pallas_call(
        merge_kernel,
        in_specs=[vmem, vmem],
        out_specs=[vmem] * chips,
        out_shape=[jax.ShapeDtypeStruct(shape, jnp.float32)]
        + [jax.ShapeDtypeStruct(shape, jnp.bfloat16)] * (chips - 1),
        compiler_params=pltpu.CompilerParams(vmem_limit_bytes=8 * 2**20),
        cost_estimate=pl.CostEstimate(flops=2**16, bytes_accessed=2**12, transcendentals=0),
        name="merge_cores",
    )(keep, got)


def pack_kernel(*refs):
    for which, ref in enumerate(refs[:-1]):
        refs[-1][which] = ref[...]


def pack_call(arrs):
    vmem = pl.BlockSpec(memory_space=pltpu.VMEM)
    return pl.pallas_call(
        pack_kernel,
        in_specs=[vmem] * len(arrs),
        out_specs=vmem,
        out_shape=jax.ShapeDtypeStruct((len(arrs),) + arrs[0].shape, arrs[0].dtype),
        compiler_params=pltpu.CompilerParams(vmem_limit_bytes=8 * 2**20),
        cost_estimate=pl.CostEstimate(flops=2**16, bytes_accessed=2**12, transcendentals=0),
        name="pack_pieces",
    )(*arrs)


def quark_kernel(masks, n_op, n_got, n_tau, n_h, *refs):
    got_refs = refs[:n_got]
    tau_refs = refs[n_got : n_got + n_tau]
    out_ref, left_ref = refs[n_got + n_tau :]
    my_space, my_op = lax.axis_index("space"), lax.axis_index("op")
    _, n_pair, _, own, n_b = out_ref.shape
    row = lax.broadcasted_iota(jnp.int32, (n_b, 2 * n_b), 0)
    col = lax.broadcasted_iota(jnp.int32, (n_b, 2 * n_b), 1)
    even = (col == 2 * row).astype(jnp.bfloat16)
    odd = (col == 2 * row + 1).astype(jnp.bfloat16)
    total = got_refs[0][...]
    for ref in got_refs[1:]:
        total = total + ref[...].astype(jnp.float32)
    swap = []
    for hel in range(n_h):
        start = hel * 2 * own
        swap += [-total[start + own : start + 2 * own], total[start : start + own]]
    left = jnp.dot(total.astype(jnp.bfloat16), even, preferred_element_type=jnp.float32)
    left += jnp.dot(
        jnp.concatenate(swap, 0).astype(jnp.bfloat16), odd, preferred_element_type=jnp.float32
    )
    left_ref[...] = left.astype(jnp.bfloat16)
    tau = []
    for ref in tau_refs:
        tau += [ref.at[which] for which in range(ref.shape[0])] if len(ref.shape) == 3 else [ref]
    depth = tau[0].shape[0]
    whole = depth == 2 * n_b
    if not whole:
        out_ref[...] = jnp.zeros_like(out_ref)
    for which, (mask, mask_op) in enumerate(masks):
        first = ((my_space ^ mask) * n_op + (my_op ^ mask_op)) * depth
        pair = first // (2 * n_b)
        if whole:
            lhs = left_ref[...]
        else:
            lhs = left_ref[:, pl.ds(pl.multiple_of(first - pair * 2 * n_b, depth), depth)]
        res = jnp.dot(lhs, tau[which][...], preferred_element_type=jnp.float32)
        for hel in range(n_h):
            for part in range(2):
                start = (hel * 2 + part) * own
                if whole:
                    out_ref[hel, pair, part] = res[start : start + own]
                else:
                    out_ref[hel, pair, part] += res[start : start + own]


def phase_kernel(n_op, n_x, planes, *refs):
    mom_refs = refs[:n_op]
    num_refs = refs[n_op : 2 * n_op]
    den_ref, out_ref = refs[2 * n_op :]
    my_space, my_op = lax.axis_index("space"), lax.axis_index("op")
    _, n_h, _, _, _, width = out_ref.shape
    n_mom = mom_refs[0].shape[0]
    moms = [(op, k) for op in range(n_op) for k in range(n_mom)]
    scale = 1.0 / math.sqrt(3.0 * n_x * LY * LZ)
    shape = (planes * len(moms), width)
    row = lax.broadcasted_iota(jnp.int32, shape, 0)
    lane = lax.broadcasted_iota(jnp.int32, shape, 1)
    yy = lane // LZ
    zz = lane & (LZ - 1)

    def spread(values):
        res = jnp.full(shape, values[0], jnp.int32)
        for which in range(1, len(values)):
            res = jnp.where(row == which, values[which], res)
        return res

    comps = [[mom_refs[op][k, axis] for _ in range(planes) for op, k in moms] for axis in range(3)]
    mom_x, mom_y, mom_z = [spread(comp) for comp in comps]
    pos_x = my_space * planes + row // len(moms)
    steps = ((0, 0, 0), (1, 0, 0), (0, 1, 0), (0, 0, 1))
    waves = []
    for step_x, step_y, step_z in steps:
        turn_x = lax.rem(mom_x * (pos_x + step_x), n_x).astype(jnp.float32) * (1.0 / n_x)
        turn_y = ((mom_y * (yy + step_y)) & (LY - 1)).astype(jnp.float32) * (1.0 / LY)
        turn_z = ((mom_z * (zz + step_z)) & (LZ - 1)).astype(jnp.float32) * (1.0 / LZ)
        turn = turn_x + turn_y + turn_z
        theta = (2.0 * math.pi) * (turn - jnp.floor(turn))
        waves.append((jnp.cos(theta), jnp.sin(theta)))
    for hel in range(n_h):
        which_h = my_op * n_h + hel
        den = jnp.full((1, width), den_ref[which_h], jnp.int32).astype(jnp.float32)
        for direc in range(NDIR):
            wts = []
            for op, k in moms:
                num = num_refs[op][direc, k, which_h]
                wts.append(jnp.full((1, width), num, jnp.int32).astype(jnp.float32) / den * scale)
            for kind, wave in ((0, waves[0]), (1, waves[1 + direc])):
                for plane in range(planes):
                    start = plane * len(moms)
                    real = sum(wt * wave[0][start + at : start + at + 1] for at, wt in enumerate(wts))
                    imag = sum(wt * wave[1][start + at : start + at + 1] for at, wt in enumerate(wts))
                    out_ref[kind, hel, direc, 0, plane : plane + 1, :] = -real if kind else real
                    out_ref[kind, hel, direc, 1, plane : plane + 1, :] = -imag


def shards(eigvecs, links, momenta, coef_num, coef_den, peram):
    n_space = lax.axis_size("space")
    n_op = lax.axis_size("op")
    n_tm = lax.axis_size("tm")
    _, _, n_b, _, planes, width = eigvecs.shape
    n_x = planes * n_space
    own = n_b // n_space
    n_h = coef_num.shape[0] // n_op
    my_op = lax.axis_index("op")
    my_space = lax.axis_index("space")

    nums = jnp.transpose(coef_num, (2, 1, 0))
    both = [(momenta, nums)]
    both += [(across(momenta, "op", mask), across(nums, "op", mask)) for mask in range(1, n_op)]

    group = n_space * n_op
    depth = n_b * SPINS // group
    first = (my_space * n_op + my_op) * depth
    piece = lax.dynamic_slice(
        peram.reshape(n_b, SPINS, 2, n_b), (first % n_b, first // n_b, 0, 0), (depth, 1, 2, n_b)
    ).reshape(depth * 2, n_b)

    moved = lax.optimization_barrier(jnp.transpose(eigvecs[0], (3, 0, 2, 1, 4)))
    own_piece = from_behind(piece, "tm", n_tm - 1)
    vecs = [moved[plane] for plane in range(planes)]
    upper = from_behind(vecs[0], "space", -1)

    smem = pl.BlockSpec(memory_space=pltpu.SMEM)
    vmem = pl.BlockSpec(memory_space=pltpu.VMEM)
    phi = pl.pallas_call(
        functools.partial(phase_kernel, n_op, n_x, planes),
        in_specs=[smem] * (2 * n_op + 1),
        out_specs=vmem,
        out_shape=jax.ShapeDtypeStruct((2, n_h, NDIR, 2, planes, width), jnp.float32),
        compiler_params=pltpu.CompilerParams(vmem_limit_bytes=4 * 2**20),
        name="phases",
    )(*[mom for mom, _ in both], *[num for _, num in both], coef_den)

    dims = [("op", 1 << bit) for bit in range(n_op.bit_length() - 1)]
    dims += [("space", 1 << bit) for bit in range(1, n_space.bit_length() - 1)]
    load = [0] * len(dims)

    def stage(held, size):
        for group_dims in itertools.combinations(range(len(dims)), size):
            dim = min(group_dims, key=lambda at: load[at])
            load[dim] += 1
            before = held[tuple(at for at in group_dims if at != dim)]
            held[group_dims] = across(before, *dims[dim])

    def hold(held, other):
        arrs, other = lax.optimization_barrier((list(held.values()), other))
        return dict(zip(held.keys(), arrs)), other

    link = links[0]
    last = planes - 1
    corner = tuple(range(len(dims)))
    partial = None
    for plane in range(last):
        partial = plane_call(plane, (1, 2, 0), vecs[plane], vecs[plane + 1], link, phi, partial)
    held, partial = hold({(): own_piece}, partial)
    stage(held, 1)
    if len(dims) > 2:
        far = diagonal(held[()], n_space, n_op)
    partial = plane_call(last, (1, 2), vecs[last], None, link, phi, partial)
    keep, give = plane_call(last, (0,), vecs[last], upper, link, phi, partial, n_space)
    swapped = across(give, "space", 1)
    if len(dims) > 2:
        held[corner] = far
    early = list(held)
    held, keep = hold(held, keep)
    for size in range(2, len(dims) if len(dims) > 2 else 3):
        stage(held, size)
    late = [key for key in held if key not in early]
    ready, swapped = hold({key: held[key] for key in early}, swapped)
    flipped = [across(pack_call(list(ready.values())), "space", 1)]
    merged = merge_call(keep, swapped)
    flipped, merged = lax.optimization_barrier((flipped, merged))
    got = [across(merged[mask], "space", 2 * mask) for mask in range(n_space // 2 - 1, 0, -1)]
    after, got = hold({key: held[key] for key in late}, got)
    held.update(after)
    got.insert(0, merged[0])
    flipped.append(across(pack_call([held[key] for key in late]), "space", 1))
    tau = [held[key] for key in early + late] + flipped
    masks = []
    for flip in range(2):
        for group_dims in early + late:
            mask = {"space": flip, "op": 0}
            for at in group_dims:
                mask[dims[at][0]] ^= dims[at][1]
            masks.append((mask["space"], mask["op"]))

    lines = pl.pallas_call(
        functools.partial(quark_kernel, masks, n_op, len(got), len(tau), n_h),
        in_specs=[vmem] * (len(got) + len(tau)),
        out_specs=vmem,
        out_shape=jax.ShapeDtypeStruct((n_h, SPINS, 2, own, n_b), jnp.float32),
        scratch_shapes=[
            pltpu.VMEM((n_h * 2 * own, 2 * n_b), jnp.bfloat16),
        ],
        compiler_params=pltpu.CompilerParams(vmem_limit_bytes=VMEM_BYTES),
        cost_estimate=pl.CostEstimate(
            flops=2 * SPINS * n_h * 2 * own * 2 * n_b * n_b, bytes_accessed=7 * 2**20, transcendentals=0
        ),
        name="quark_products",
    )(*got, *tau)
    return lines.reshape(1, n_h, 4, 4, 2, own, n_b)


def solution(mesh):
    return jax.shard_map(
        shards,
        mesh=mesh,
        in_specs=(
            P("tm", None, None, None, "space", None),
            P("tm", None, None, None, None, "space", None),
            P("op", None),
            P(None, "op", None),
            P(),
            P("tm", None, None, None, None, None),
        ),
        out_specs=P("tm", "op", None, None, None, "space", None),
        check_vma=False,
    )
```

```python
import functools
import itertools
import math

import jax
import jax.numpy as jnp
from jax import lax
from jax.experimental import pallas as pl
from jax.experimental.pallas import tpu as pltpu
from jax.sharding import PartitionSpec as P

LY = 32
LZ = 8
NDIR = 3
SPINS = 16
ROWS = 16
HALF = 128
BLOCK = 32
VMEM_BYTES = 20 * 2**20


def from_behind(value, axis, steps):
    count = lax.axis_size(axis)
    pairs = [(source, (source + steps) % count) for source in range(count)]
    return lax.ppermute(value, axis, pairs)


def across(value, axis, mask):
    pairs = [(source, source ^ mask) for source in range(lax.axis_size(axis))]
    return lax.ppermute(value, axis, pairs)


def diagonal(value, n_space, n_op):
    pairs = []
    for space in range(n_space):
        for oper in range(n_op):
            target = (space ^ (n_space - 2)) * n_op + (oper ^ (n_op - 1))
            pairs.append((space * n_op + oper, target))
    return lax.ppermute(value, ("space", "op"), pairs)


def dot_nt(left, right):
    return lax.dot_general(
        left, right, (((1,), (1,)), ((), ())), preferred_element_type=jnp.float32
    )


def shift_y(arr):
    return pltpu.roll(arr, arr.shape[1] - LZ, 1)


def shift_z(arr):
    width = arr.shape[1]
    lane = lax.broadcasted_iota(jnp.int32, arr.shape, 1)
    near = pltpu.roll(arr, width - 1, 1)
    far = pltpu.roll(arr, LZ - 1, 1)
    return jnp.where((lane & (LZ - 1)) == LZ - 1, far, near)


def weighted_links(u_ref, phi_ref, shifted, dirs, plane, n_h, store):
    width = u_ref.shape[-1]
    for half in range(width // HALF):
        lanes = pl.ds(half * HALF, HALF)
        for col in range(3):
            acc = {}
            for slot, direc in enumerate(dirs):
                f_r = None
                f_i = None
                for col_two in range(3):
                    u_r = u_ref[direc, col, col_two, 0, pl.ds(plane, 1), lanes]
                    u_i = u_ref[direc, col, col_two, 1, pl.ds(plane, 1), lanes]
                    v_r = shifted[slot, 0, col_two, :, lanes]
                    v_i = shifted[slot, 1, col_two, :, lanes]
                    term_r = u_r * v_r - u_i * v_i
                    term_i = u_r * v_i + u_i * v_r
                    f_r = term_r if f_r is None else f_r + term_r
                    f_i = term_i if f_i is None else f_i + term_i
                for kind in range(2):
                    for hel in range(n_h):
                        p_r = phi_ref[kind, hel, direc, 0, pl.ds(plane, 1), lanes]
                        p_i = phi_ref[kind, hel, direc, 1, pl.ds(plane, 1), lanes]
                        g_r = p_r * f_r - p_i * f_i
                        g_i = p_r * f_i + p_i * f_r
                        if (kind, hel) in acc:
                            old_r, old_i = acc[kind, hel]
                            g_r, g_i = old_r + g_r, old_i + g_i
                        acc[kind, hel] = (g_r, g_i)
            for (kind, hel), both in acc.items():
                store(kind, hel, col, half, both)


def plane_kernel(plane, dirs, has_part, n_out, *refs):
    refs = list(refs)
    v_ref = refs.pop(0)
    next_ref = refs.pop(0) if 0 in dirs else None
    u_ref, phi_ref = refs.pop(0), refs.pop(0)
    part_ref = refs.pop(0) if has_part else None
    keep_ref = refs.pop(0) if n_out else None
    give_ref = refs.pop(0) if n_out else None
    sum_ref, mat_ref, one_ref, two_ref, sh_ref = refs
    n_h = phi_ref.shape[1]
    _, _, n_b, width = v_ref.shape
    bufs = (one_ref, two_ref)
    last = n_b // BLOCK - 1

    for col in range(3):
        mat_ref[:, pl.ds(col * width, width)] = v_ref[:, col].reshape(2 * n_b, width)

    def fill(which, buf):
        for sub in range(BLOCK // ROWS):
            rows = pl.ds(pl.multiple_of(which * BLOCK + sub * ROWS, ROWS), ROWS)
            shifted = sh_ref.at[buf, sub]
            for slot, direc in enumerate(dirs):
                for part in range(2):
                    for col in range(3):
                        source = next_ref if direc == 0 else v_ref
                        field = source[part, col, rows, :].astype(jnp.float32)
                        if direc == 1:
                            field = shift_y(field)
                        elif direc == 2:
                            field = shift_z(field)
                        shifted[slot, part, col] = field

            def store(kind, hel, col, half, both, sub=sub):
                for part in range(2):
                    row = ((kind * n_h + hel) * 2 + part) * BLOCK + sub * ROWS
                    lanes = pl.ds(col * width + half * HALF, HALF)
                    bufs[buf][pl.ds(row, ROWS), lanes] = both[part].astype(jnp.bfloat16)

            weighted_links(u_ref, phi_ref, shifted, dirs, plane, n_h, store)

    def contract(which, buf):
        rows = pl.ds(pl.multiple_of(which * BLOCK, BLOCK), BLOCK)
        prod = dot_nt(bufs[buf][...], mat_ref[...])
        for kind in range(2):
            for hel in range(n_h):
                row = (kind * n_h + hel) * 2 * BLOCK
                re_row, im_row = prod[row : row + BLOCK], prod[row + BLOCK : row + 2 * BLOCK]
                real = re_row[:, :n_b] + im_row[:, n_b:]
                if kind:
                    imag = re_row[:, n_b:] - im_row[:, :n_b]
                else:
                    imag = im_row[:, :n_b] - re_row[:, n_b:]
                for part, total in enumerate((real, imag)):
                    if has_part:
                        total = total + part_ref[kind, hel, part, rows, :]
                    sum_ref[kind, hel, part, rows, :] = total

    fill(0, 0)

    def pair(step, carry):
        fill(2 * step + 1, 1)
        contract(2 * step, 0)
        fill(2 * step + 2, 0)
        contract(2 * step + 1, 1)
        return carry

    lax.fori_loop(0, last // 2, pair, 0)
    fill(last, 1)
    contract(last - 1, 0)
    contract(last, 1)

    if n_out:
        core = lax.axis_index("space") & 1
        for hel in range(n_h):
            for part in range(2):
                total = jnp.transpose(sum_ref[0, hel, part]) + sum_ref[1, hel, part]
                halves = total.reshape(n_out // 2, 2, n_b // n_out, n_b)
                keep_ref[:, hel, part] = jnp.where(core == 0, halves[:, 0], halves[:, 1])
                give = jnp.where(core == 0, halves[:, 1], halves[:, 0])
                give_ref[:, hel, part] = give.astype(jnp.bfloat16)


def plane_call(plane, dirs, vec, ahead, link, phi, part=None, n_out=0):
    n_h = phi.shape[1]
    _, _, n_b, width = vec.shape
    vmem = pl.BlockSpec(memory_space=pltpu.VMEM)
    args = [vec] + ([ahead] if 0 in dirs else []) + [link, phi]
    args += [part] if part is not None else []
    specs = [vmem] * len(args)
    sums = (2, n_h, 2, n_b, n_b)
    scratch = [
        pltpu.VMEM((2 * n_b, 3 * width), jnp.bfloat16),
        pltpu.VMEM((4 * n_h * BLOCK, 3 * width), jnp.bfloat16),
        pltpu.VMEM((4 * n_h * BLOCK, 3 * width), jnp.bfloat16),
        pltpu.VMEM((2, BLOCK // ROWS, len(dirs), 2, 3, ROWS, width), jnp.float32),
    ]
    if n_out:
        scratch.insert(0, pltpu.VMEM(sums, jnp.float32))
        blocks = (n_out // 2, n_h, 2, n_b // n_out, n_b)
        out_shape = [
            jax.ShapeDtypeStruct(blocks, jnp.float32),
            jax.ShapeDtypeStruct(blocks, jnp.bfloat16),
        ]
        out_specs = [vmem, vmem]
    else:
        out_shape = jax.ShapeDtypeStruct(sums, jnp.float32)
        out_specs = vmem
    return pl.pallas_call(
        functools.partial(plane_kernel, plane, dirs, part is not None, n_out),
        in_specs=specs,
        out_specs=out_specs,
        out_shape=out_shape,
        scratch_shapes=scratch,
        compiler_params=pltpu.CompilerParams(vmem_limit_bytes=VMEM_BYTES),
        cost_estimate=pl.CostEstimate(
            flops=2**34,
            bytes_accessed=2**28,
            transcendentals=0,
        ),
        name="plane%d_%s" % (plane, "".join(str(direc) for direc in dirs)),
    )(*args)


def merge_kernel(keep_ref, got_ref, own_ref, *out_refs):
    chip = lax.axis_index("space") >> 1
    shape = own_ref.shape
    own_ref[...] = (keep_ref[chip] + got_ref[chip].astype(jnp.float32)).reshape(shape)
    for mask, out_ref in enumerate(out_refs, 1):
        total = keep_ref[chip ^ mask] + got_ref[chip ^ mask].astype(jnp.float32)
        out_ref[...] = total.reshape(shape).astype(jnp.bfloat16)


def merge_call(keep, got):
    chips, n_h, _, own, n_b = keep.shape
    shape = (n_h * 2 * own, n_b)
    vmem = pl.BlockSpec(memory_space=pltpu.VMEM)
    return pl.pallas_call(
        merge_kernel,
        in_specs=[vmem, vmem],
        out_specs=[vmem] * chips,
        out_shape=[jax.ShapeDtypeStruct(shape, jnp.float32)]
        + [jax.ShapeDtypeStruct(shape, jnp.bfloat16)] * (chips - 1),
        compiler_params=pltpu.CompilerParams(vmem_limit_bytes=8 * 2**20),
        cost_estimate=pl.CostEstimate(flops=2**16, bytes_accessed=2**12, transcendentals=0),
        name="merge_cores",
    )(keep, got)


def pack_kernel(*refs):
    for which, ref in enumerate(refs[:-1]):
        refs[-1][which] = ref[...]


def pack_call(arrs):
    vmem = pl.BlockSpec(memory_space=pltpu.VMEM)
    return pl.pallas_call(
        pack_kernel,
        in_specs=[vmem] * len(arrs),
        out_specs=vmem,
        out_shape=jax.ShapeDtypeStruct((len(arrs),) + arrs[0].shape, arrs[0].dtype),
        compiler_params=pltpu.CompilerParams(vmem_limit_bytes=8 * 2**20),
        cost_estimate=pl.CostEstimate(flops=2**16, bytes_accessed=2**12, transcendentals=0),
        name="pack_pieces",
    )(*arrs)


def left_kernel(n_h, *refs):
    got_refs, left_ref = refs[:-1], refs[-1]
    rows, n_b = got_refs[0].shape
    own = rows // (2 * n_h)
    row = lax.broadcasted_iota(jnp.int32, (n_b, 2 * n_b), 0)
    col = lax.broadcasted_iota(jnp.int32, (n_b, 2 * n_b), 1)
    even = (col == 2 * row).astype(jnp.bfloat16)
    odd = (col == 2 * row + 1).astype(jnp.bfloat16)
    total = got_refs[0][...]
    for ref in got_refs[1:]:
        total = total + ref[...].astype(jnp.float32)
    swap = []
    for hel in range(n_h):
        start = hel * 2 * own
        swap += [-total[start + own : start + 2 * own], total[start : start + own]]
    left = jnp.dot(total.astype(jnp.bfloat16), even, preferred_element_type=jnp.float32)
    left += jnp.dot(
        jnp.concatenate(swap, 0).astype(jnp.bfloat16), odd, preferred_element_type=jnp.float32
    )
    left_ref[...] = left.astype(jnp.bfloat16)


def left_call(got, n_h):
    rows, n_b = got[0].shape
    vmem = pl.BlockSpec(memory_space=pltpu.VMEM)
    return pl.pallas_call(
        functools.partial(left_kernel, n_h),
        in_specs=[vmem] * len(got),
        out_specs=vmem,
        out_shape=jax.ShapeDtypeStruct((rows, 2 * n_b), jnp.bfloat16),
        compiler_params=pltpu.CompilerParams(vmem_limit_bytes=8 * 2**20),
        cost_estimate=pl.CostEstimate(flops=2**34, bytes_accessed=2**24, transcendentals=0),
        name="left_operand",
    )(*got)


def quark_kernel(masks, n_op, left_ref, *refs):
    tau_refs, out_ref = refs[:-1], refs[-1]
    my_space, my_op = lax.axis_index("space"), lax.axis_index("op")
    n_h, n_pair, _, own, n_b = out_ref.shape
    tau = []
    for ref in tau_refs:
        tau += [ref.at[which] for which in range(ref.shape[0])] if len(ref.shape) == 3 else [ref]
    depth = tau[0].shape[0]
    whole = depth == 2 * n_b
    if not whole:
        out_ref[...] = jnp.zeros_like(out_ref)
    for which, (mask, mask_op) in enumerate(masks):
        first = ((my_space ^ mask) * n_op + (my_op ^ mask_op)) * depth
        pair = first // (2 * n_b)
        if whole:
            lhs = left_ref[...]
        else:
            lhs = left_ref[:, pl.ds(pl.multiple_of(first - pair * 2 * n_b, depth), depth)]
        res = jnp.dot(lhs, tau[which][...], preferred_element_type=jnp.float32)
        for hel in range(n_h):
            for part in range(2):
                start = (hel * 2 + part) * own
                if whole:
                    out_ref[hel, pair, part] = res[start : start + own]
                else:
                    out_ref[hel, pair, part] += res[start : start + own]


def phase_kernel(n_op, n_x, planes, *refs):
    mom_refs = refs[:n_op]
    num_refs = refs[n_op : 2 * n_op]
    den_ref, out_ref = refs[2 * n_op :]
    my_space, my_op = lax.axis_index("space"), lax.axis_index("op")
    _, n_h, _, _, _, width = out_ref.shape
    n_mom = mom_refs[0].shape[0]
    moms = [(op, k) for op in range(n_op) for k in range(n_mom)]
    scale = 1.0 / math.sqrt(3.0 * n_x * LY * LZ)
    shape = (planes * len(moms), width)
    row = lax.broadcasted_iota(jnp.int32, shape, 0)
    lane = lax.broadcasted_iota(jnp.int32, shape, 1)
    yy = lane // LZ
    zz = lane & (LZ - 1)

    def spread(values):
        res = jnp.full(shape, values[0], jnp.int32)
        for which in range(1, len(values)):
            res = jnp.where(row == which, values[which], res)
        return res

    comps = [[mom_refs[op][k, axis] for _ in range(planes) for op, k in moms] for axis in range(3)]
    mom_x, mom_y, mom_z = [spread(comp) for comp in comps]
    pos_x = my_space * planes + row // len(moms)
    steps = ((0, 0, 0), (1, 0, 0), (0, 1, 0), (0, 0, 1))
    waves = []
    for step_x, step_y, step_z in steps:
        turn_x = lax.rem(mom_x * (pos_x + step_x), n_x).astype(jnp.float32) * (1.0 / n_x)
        turn_y = ((mom_y * (yy + step_y)) & (LY - 1)).astype(jnp.float32) * (1.0 / LY)
        turn_z = ((mom_z * (zz + step_z)) & (LZ - 1)).astype(jnp.float32) * (1.0 / LZ)
        turn = turn_x + turn_y + turn_z
        theta = (2.0 * math.pi) * (turn - jnp.floor(turn))
        waves.append((jnp.cos(theta), jnp.sin(theta)))
    for hel in range(n_h):
        which_h = my_op * n_h + hel
        den = jnp.full((1, width), den_ref[which_h], jnp.int32).astype(jnp.float32)
        for direc in range(NDIR):
            wts = []
            for op, k in moms:
                num = num_refs[op][direc, k, which_h]
                wts.append(jnp.full((1, width), num, jnp.int32).astype(jnp.float32) / den * scale)
            for kind, wave in ((0, waves[0]), (1, waves[1 + direc])):
                for plane in range(planes):
                    start = plane * len(moms)
                    real = sum(wt * wave[0][start + at : start + at + 1] for at, wt in enumerate(wts))
                    imag = sum(wt * wave[1][start + at : start + at + 1] for at, wt in enumerate(wts))
                    out_ref[kind, hel, direc, 0, plane : plane + 1, :] = -real if kind else real
                    out_ref[kind, hel, direc, 1, plane : plane + 1, :] = -imag


def shards(eigvecs, links, momenta, coef_num, coef_den, peram):
    n_space = lax.axis_size("space")
    n_op = lax.axis_size("op")
    n_tm = lax.axis_size("tm")
    _, _, n_b, _, planes, width = eigvecs.shape
    n_x = planes * n_space
    own = n_b // n_space
    n_h = coef_num.shape[0] // n_op
    my_op = lax.axis_index("op")
    my_space = lax.axis_index("space")

    nums = jnp.transpose(coef_num, (2, 1, 0))
    both = [(momenta, nums)]
    both += [(across(momenta, "op", mask), across(nums, "op", mask)) for mask in range(1, n_op)]

    group = n_space * n_op
    depth = n_b * SPINS // group
    first = (my_space * n_op + my_op) * depth
    piece = lax.dynamic_slice(
        peram.reshape(n_b, SPINS, 2, n_b), (first % n_b, first // n_b, 0, 0), (depth, 1, 2, n_b)
    ).reshape(depth * 2, n_b)

    moved = lax.optimization_barrier(jnp.transpose(eigvecs[0], (3, 0, 2, 1, 4)))
    own_piece = from_behind(piece, "tm", n_tm - 1)
    vecs = [moved[plane] for plane in range(planes)]
    upper = from_behind(vecs[0], "space", -1)

    smem = pl.BlockSpec(memory_space=pltpu.SMEM)
    vmem = pl.BlockSpec(memory_space=pltpu.VMEM)
    phi = pl.pallas_call(
        functools.partial(phase_kernel, n_op, n_x, planes),
        in_specs=[smem] * (2 * n_op + 1),
        out_specs=vmem,
        out_shape=jax.ShapeDtypeStruct((2, n_h, NDIR, 2, planes, width), jnp.float32),
        compiler_params=pltpu.CompilerParams(vmem_limit_bytes=4 * 2**20),
        name="phases",
    )(*[mom for mom, _ in both], *[num for _, num in both], coef_den)

    dims = [("op", 1 << bit) for bit in range(n_op.bit_length() - 1)]
    dims += [("space", 1 << bit) for bit in range(1, n_space.bit_length() - 1)]
    load = [0] * len(dims)

    def stage(held, size):
        for group_dims in itertools.combinations(range(len(dims)), size):
            dim = min(group_dims, key=lambda at: load[at])
            load[dim] += 1
            before = held[tuple(at for at in group_dims if at != dim)]
            held[group_dims] = across(before, *dims[dim])

    def hold(held, other):
        arrs, other = lax.optimization_barrier((list(held.values()), other))
        return dict(zip(held.keys(), arrs)), other

    link = links[0]
    last = planes - 1
    corner = tuple(range(len(dims)))
    partial = plane_call(last, (1, 2), vecs[last], None, link, phi)
    held, partial = hold({(): own_piece}, partial)
    stage(held, 1)
    if len(dims) > 2:
        far = diagonal(held[()], n_space, n_op)
    for plane in range(last):
        partial = plane_call(plane, (1, 2, 0), vecs[plane], vecs[plane + 1], link, phi, partial)
    keep, give = plane_call(last, (0,), vecs[last], upper, link, phi, partial, n_space)
    swapped = across(give, "space", 1)
    if len(dims) > 2:
        held[corner] = far
    early = list(held)
    held, keep = hold(held, keep)
    for size in range(2, len(dims) if len(dims) > 2 else 3):
        stage(held, size)
    late = [key for key in held if key not in early]
    ready, swapped = hold({key: held[key] for key in early}, swapped)
    flipped = [across(pack_call(list(ready.values())), "space", 1)]
    merged = merge_call(keep, swapped)
    flipped, merged = lax.optimization_barrier((flipped, merged))
    got = [across(merged[mask], "space", 2 * mask) for mask in range(n_space // 2 - 1, 0, -1)]
    got.insert(0, merged[0])
    flipped.append(across(pack_call([held[key] for key in late]), "space", 1))
    tau = [held[key] for key in early + late] + flipped
    masks = []
    for flip in range(2):
        for group_dims in early + late:
            mask = {"space": flip, "op": 0}
            for at in group_dims:
                mask[dims[at][0]] ^= dims[at][1]
            masks.append((mask["space"], mask["op"]))

    lines = pl.pallas_call(
        functools.partial(quark_kernel, masks, n_op),
        in_specs=[vmem] * (1 + len(tau)),
        out_specs=vmem,
        out_shape=jax.ShapeDtypeStruct((n_h, SPINS, 2, own, n_b), jnp.float32),
        compiler_params=pltpu.CompilerParams(vmem_limit_bytes=VMEM_BYTES),
        cost_estimate=pl.CostEstimate(
            flops=2 * SPINS * n_h * 2 * own * 2 * n_b * n_b, bytes_accessed=7 * 2**20, transcendentals=0
        ),
        name="quark_products",
    )(left_call(got, n_h), *tau)
    return lines.reshape(1, n_h, 4, 4, 2, own, n_b)


def solution(mesh):
    return jax.shard_map(
        shards,
        mesh=mesh,
        in_specs=(
            P("tm", None, None, None, "space", None),
            P("tm", None, None, None, None, "space", None),
            P("op", None),
            P(None, "op", None),
            P(),
            P("tm", None, None, None, None, None),
        ),
        out_specs=P("tm", "op", None, None, None, "space", None),
        check_vma=False,
    )
```

```python
import functools
import itertools
import math

import jax
import jax.numpy as jnp
from jax import lax
from jax.experimental import pallas as pl
from jax.experimental.pallas import tpu as pltpu
from jax.sharding import PartitionSpec as P

LY = 32
LZ = 8
NDIR = 3
SPINS = 16
ROWS = 16
HALF = 128
BLOCK = 32
VMEM_BYTES = 20 * 2**20


def from_behind(value, axis, steps):
    count = lax.axis_size(axis)
    pairs = [(source, (source + steps) % count) for source in range(count)]
    return lax.ppermute(value, axis, pairs)


def across(value, axis, mask):
    pairs = [(source, source ^ mask) for source in range(lax.axis_size(axis))]
    return lax.ppermute(value, axis, pairs)


def diagonal(value, n_space, n_op):
    pairs = []
    for space in range(n_space):
        for oper in range(n_op):
            target = (space ^ (n_space - 2)) * n_op + (oper ^ (n_op - 1))
            pairs.append((space * n_op + oper, target))
    return lax.ppermute(value, ("space", "op"), pairs)


def dot_nt(left, right):
    return lax.dot_general(
        left, right, (((1,), (1,)), ((), ())), preferred_element_type=jnp.float32
    )


def shift_y(arr):
    return pltpu.roll(arr, arr.shape[1] - LZ, 1)


def shift_z(arr):
    width = arr.shape[1]
    lane = lax.broadcasted_iota(jnp.int32, arr.shape, 1)
    near = pltpu.roll(arr, width - 1, 1)
    far = pltpu.roll(arr, LZ - 1, 1)
    return jnp.where((lane & (LZ - 1)) == LZ - 1, far, near)


def weighted_links(u_ref, phi_ref, shifted, dirs, plane, n_h, store):
    width = u_ref.shape[-1]
    for half in range(width // HALF):
        lanes = pl.ds(half * HALF, HALF)
        for col in range(3):
            acc = {}
            for slot, direc in enumerate(dirs):
                f_r = None
                f_i = None
                for col_two in range(3):
                    u_r = u_ref[direc, col, col_two, 0, pl.ds(plane, 1), lanes]
                    u_i = u_ref[direc, col, col_two, 1, pl.ds(plane, 1), lanes]
                    v_r = shifted[slot, 0, col_two, :, lanes]
                    v_i = shifted[slot, 1, col_two, :, lanes]
                    term_r = u_r * v_r - u_i * v_i
                    term_i = u_r * v_i + u_i * v_r
                    f_r = term_r if f_r is None else f_r + term_r
                    f_i = term_i if f_i is None else f_i + term_i
                for kind in range(2):
                    for hel in range(n_h):
                        p_r = phi_ref[kind, hel, direc, 0, pl.ds(plane, 1), lanes]
                        p_i = phi_ref[kind, hel, direc, 1, pl.ds(plane, 1), lanes]
                        g_r = p_r * f_r - p_i * f_i
                        g_i = p_r * f_i + p_i * f_r
                        if (kind, hel) in acc:
                            old_r, old_i = acc[kind, hel]
                            g_r, g_i = old_r + g_r, old_i + g_i
                        acc[kind, hel] = (g_r, g_i)
            for (kind, hel), both in acc.items():
                store(kind, hel, col, half, both)


def plane_kernel(plane, dirs, has_part, n_out, *refs):
    refs = list(refs)
    v_ref = refs.pop(0)
    next_ref = refs.pop(0) if 0 in dirs else None
    u_ref, phi_ref = refs.pop(0), refs.pop(0)
    part_ref = refs.pop(0) if has_part else None
    keep_ref = refs.pop(0) if n_out else None
    give_ref = refs.pop(0) if n_out else None
    sum_ref, mat_ref, one_ref, two_ref, sh_ref = refs
    n_h = phi_ref.shape[1]
    _, _, n_b, width = v_ref.shape
    bufs = (one_ref, two_ref)
    last = n_b // BLOCK - 1

    for col in range(3):
        mat_ref[:, pl.ds(col * width, width)] = v_ref[:, col].reshape(2 * n_b, width)

    def fill(which, buf):
        for sub in range(BLOCK // ROWS):
            rows = pl.ds(pl.multiple_of(which * BLOCK + sub * ROWS, ROWS), ROWS)
            shifted = sh_ref.at[buf, sub]
            for slot, direc in enumerate(dirs):
                for part in range(2):
                    for col in range(3):
                        source = next_ref if direc == 0 else v_ref
                        field = source[part, col, rows, :].astype(jnp.float32)
                        if direc == 1:
                            field = shift_y(field)
                        elif direc == 2:
                            field = shift_z(field)
                        shifted[slot, part, col] = field

            def store(kind, hel, col, half, both, sub=sub):
                for part in range(2):
                    row = ((kind * n_h + hel) * 2 + part) * BLOCK + sub * ROWS
                    lanes = pl.ds(col * width + half * HALF, HALF)
                    bufs[buf][pl.ds(row, ROWS), lanes] = both[part].astype(jnp.bfloat16)

            weighted_links(u_ref, phi_ref, shifted, dirs, plane, n_h, store)

    def contract(which, buf):
        rows = pl.ds(pl.multiple_of(which * BLOCK, BLOCK), BLOCK)
        prod = dot_nt(bufs[buf][...], mat_ref[...])
        for kind in range(2):
            for hel in range(n_h):
                row = (kind * n_h + hel) * 2 * BLOCK
                re_row, im_row = prod[row : row + BLOCK], prod[row + BLOCK : row + 2 * BLOCK]
                real = re_row[:, :n_b] + im_row[:, n_b:]
                if kind:
                    imag = re_row[:, n_b:] - im_row[:, :n_b]
                else:
                    imag = im_row[:, :n_b] - re_row[:, n_b:]
                for part, total in enumerate((real, imag)):
                    if has_part:
                        total = total + part_ref[kind, hel, part, rows, :]
                    sum_ref[kind, hel, part, rows, :] = total

    fill(0, 0)

    def pair(step, carry):
        fill(2 * step + 1, 1)
        contract(2 * step, 0)
        fill(2 * step + 2, 0)
        contract(2 * step + 1, 1)
        return carry

    lax.fori_loop(0, last // 2, pair, 0)
    fill(last, 1)
    contract(last - 1, 0)
    contract(last, 1)

    if n_out:
        core = lax.axis_index("space") & 1
        for hel in range(n_h):
            for part in range(2):
                total = jnp.transpose(sum_ref[0, hel, part]) + sum_ref[1, hel, part]
                halves = total.reshape(n_out // 2, 2, n_b // n_out, n_b)
                keep_ref[:, hel, part] = jnp.where(core == 0, halves[:, 0], halves[:, 1])
                give = jnp.where(core == 0, halves[:, 1], halves[:, 0])
                give_ref[:, hel, part] = give.astype(jnp.bfloat16)


def plane_call(plane, dirs, vec, ahead, link, phi, part=None, n_out=0):
    n_h = phi.shape[1]
    _, _, n_b, width = vec.shape
    vmem = pl.BlockSpec(memory_space=pltpu.VMEM)
    args = [vec] + ([ahead] if 0 in dirs else []) + [link, phi]
    args += [part] if part is not None else []
    specs = [vmem] * len(args)
    sums = (2, n_h, 2, n_b, n_b)
    scratch = [
        pltpu.VMEM((2 * n_b, 3 * width), jnp.bfloat16),
        pltpu.VMEM((4 * n_h * BLOCK, 3 * width), jnp.bfloat16),
        pltpu.VMEM((4 * n_h * BLOCK, 3 * width), jnp.bfloat16),
        pltpu.VMEM((2, BLOCK // ROWS, len(dirs), 2, 3, ROWS, width), jnp.float32),
    ]
    if n_out:
        scratch.insert(0, pltpu.VMEM(sums, jnp.float32))
        blocks = (n_out // 2, n_h, 2, n_b // n_out, n_b)
        out_shape = [
            jax.ShapeDtypeStruct(blocks, jnp.float32),
            jax.ShapeDtypeStruct(blocks, jnp.bfloat16),
        ]
        out_specs = [vmem, vmem]
    else:
        out_shape = jax.ShapeDtypeStruct(sums, jnp.float32)
        out_specs = vmem
    return pl.pallas_call(
        functools.partial(plane_kernel, plane, dirs, part is not None, n_out),
        in_specs=specs,
        out_specs=out_specs,
        out_shape=out_shape,
        scratch_shapes=scratch,
        compiler_params=pltpu.CompilerParams(vmem_limit_bytes=VMEM_BYTES),
        cost_estimate=pl.CostEstimate(
            flops=2**34,
            bytes_accessed=2**28,
            transcendentals=0,
        ),
        name="plane%d_%s" % (plane, "".join(str(direc) for direc in dirs)),
    )(*args)


def merge_kernel(keep_ref, got_ref, own_ref, *out_refs):
    chip = lax.axis_index("space") >> 1
    shape = own_ref.shape
    own_ref[...] = (keep_ref[chip] + got_ref[chip].astype(jnp.float32)).reshape(shape)
    for mask, out_ref in enumerate(out_refs, 1):
        total = keep_ref[chip ^ mask] + got_ref[chip ^ mask].astype(jnp.float32)
        out_ref[...] = total.reshape(shape).astype(jnp.bfloat16)


def merge_call(keep, got):
    chips, n_h, _, own, n_b = keep.shape
    shape = (n_h * 2 * own, n_b)
    vmem = pl.BlockSpec(memory_space=pltpu.VMEM)
    return pl.pallas_call(
        merge_kernel,
        in_specs=[vmem, vmem],
        out_specs=[vmem] * chips,
        out_shape=[jax.ShapeDtypeStruct(shape, jnp.float32)]
        + [jax.ShapeDtypeStruct(shape, jnp.bfloat16)] * (chips - 1),
        compiler_params=pltpu.CompilerParams(vmem_limit_bytes=8 * 2**20),
        cost_estimate=pl.CostEstimate(flops=2**16, bytes_accessed=2**12, transcendentals=0),
        name="merge_cores",
    )(keep, got)


def pack_kernel(*refs):
    for which, ref in enumerate(refs[:-1]):
        refs[-1][which] = ref[...]


def pack_call(arrs):
    vmem = pl.BlockSpec(memory_space=pltpu.VMEM)
    return pl.pallas_call(
        pack_kernel,
        in_specs=[vmem] * len(arrs),
        out_specs=vmem,
        out_shape=jax.ShapeDtypeStruct((len(arrs),) + arrs[0].shape, arrs[0].dtype),
        compiler_params=pltpu.CompilerParams(vmem_limit_bytes=8 * 2**20),
        cost_estimate=pl.CostEstimate(flops=2**16, bytes_accessed=2**12, transcendentals=0),
        name="pack_pieces",
    )(*arrs)


def left_kernel(n_h, *refs):
    got_refs, left_ref = refs[:-1], refs[-1]
    rows, n_b = got_refs[0].shape
    own = rows // (2 * n_h)
    row = lax.broadcasted_iota(jnp.int32, (n_b, 2 * n_b), 0)
    col = lax.broadcasted_iota(jnp.int32, (n_b, 2 * n_b), 1)
    even = (col == 2 * row).astype(jnp.bfloat16)
    odd = (col == 2 * row + 1).astype(jnp.bfloat16)
    total = got_refs[0][...]
    for ref in got_refs[1:]:
        total = total + ref[...].astype(jnp.float32)
    swap = []
    for hel in range(n_h):
        start = hel * 2 * own
        swap += [-total[start + own : start + 2 * own], total[start : start + own]]
    left = jnp.dot(total.astype(jnp.bfloat16), even, preferred_element_type=jnp.float32)
    left += jnp.dot(
        jnp.concatenate(swap, 0).astype(jnp.bfloat16), odd, preferred_element_type=jnp.float32
    )
    left_ref[...] = left.astype(jnp.bfloat16)


def left_call(got, n_h):
    rows, n_b = got[0].shape
    vmem = pl.BlockSpec(memory_space=pltpu.VMEM)
    return pl.pallas_call(
        functools.partial(left_kernel, n_h),
        in_specs=[vmem] * len(got),
        out_specs=vmem,
        out_shape=jax.ShapeDtypeStruct((rows, 2 * n_b), jnp.bfloat16),
        compiler_params=pltpu.CompilerParams(vmem_limit_bytes=8 * 2**20),
        cost_estimate=pl.CostEstimate(flops=2**34, bytes_accessed=2**24, transcendentals=0),
        name="left_operand",
    )(*got)


def quark_kernel(masks, n_op, left_ref, *refs):
    tau_refs, out_ref = refs[:-1], refs[-1]
    my_space, my_op = lax.axis_index("space"), lax.axis_index("op")
    n_h, n_pair, _, own, n_b = out_ref.shape
    tau = []
    for ref in tau_refs:
        tau += [ref.at[which] for which in range(ref.shape[0])] if len(ref.shape) == 3 else [ref]
    depth = tau[0].shape[0]
    whole = depth == 2 * n_b
    if not whole:
        out_ref[...] = jnp.zeros_like(out_ref)
    for which, (mask, mask_op) in enumerate(masks):
        first = ((my_space ^ mask) * n_op + (my_op ^ mask_op)) * depth
        pair = first // (2 * n_b)
        if whole:
            lhs = left_ref[...]
        else:
            lhs = left_ref[:, pl.ds(pl.multiple_of(first - pair * 2 * n_b, depth), depth)]
        res = jnp.dot(lhs, tau[which][...], preferred_element_type=jnp.float32)
        for hel in range(n_h):
            for part in range(2):
                start = (hel * 2 + part) * own
                if whole:
                    out_ref[hel, pair, part] = res[start : start + own]
                else:
                    out_ref[hel, pair, part] += res[start : start + own]


def phase_kernel(n_op, n_x, planes, *refs):
    mom_refs = refs[:n_op]
    num_refs = refs[n_op : 2 * n_op]
    den_ref, out_ref = refs[2 * n_op :]
    my_space, my_op = lax.axis_index("space"), lax.axis_index("op")
    _, n_h, _, _, _, width = out_ref.shape
    n_mom = mom_refs[0].shape[0]
    moms = [(op, k) for op in range(n_op) for k in range(n_mom)]
    scale = 1.0 / math.sqrt(3.0 * n_x * LY * LZ)
    shape = (planes * len(moms), width)
    row = lax.broadcasted_iota(jnp.int32, shape, 0)
    lane = lax.broadcasted_iota(jnp.int32, shape, 1)
    yy = lane // LZ
    zz = lane & (LZ - 1)

    def spread(values):
        res = jnp.full(shape, values[0], jnp.int32)
        for which in range(1, len(values)):
            res = jnp.where(row == which, values[which], res)
        return res

    comps = [[mom_refs[op][k, axis] for _ in range(planes) for op, k in moms] for axis in range(3)]
    mom_x, mom_y, mom_z = [spread(comp) for comp in comps]
    pos_x = my_space * planes + row // len(moms)
    steps = ((0, 0, 0), (1, 0, 0), (0, 1, 0), (0, 0, 1))
    waves = []
    for step_x, step_y, step_z in steps:
        turn_x = lax.rem(mom_x * (pos_x + step_x), n_x).astype(jnp.float32) * (1.0 / n_x)
        turn_y = ((mom_y * (yy + step_y)) & (LY - 1)).astype(jnp.float32) * (1.0 / LY)
        turn_z = ((mom_z * (zz + step_z)) & (LZ - 1)).astype(jnp.float32) * (1.0 / LZ)
        turn = turn_x + turn_y + turn_z
        theta = (2.0 * math.pi) * (turn - jnp.floor(turn))
        waves.append((jnp.cos(theta), jnp.sin(theta)))
    for hel in range(n_h):
        which_h = my_op * n_h + hel
        den = jnp.full((1, width), den_ref[which_h], jnp.int32).astype(jnp.float32)
        for direc in range(NDIR):
            wts = []
            for op, k in moms:
                num = num_refs[op][direc, k, which_h]
                wts.append(jnp.full((1, width), num, jnp.int32).astype(jnp.float32) / den * scale)
            for kind, wave in ((0, waves[0]), (1, waves[1 + direc])):
                for plane in range(planes):
                    start = plane * len(moms)
                    real = sum(wt * wave[0][start + at : start + at + 1] for at, wt in enumerate(wts))
                    imag = sum(wt * wave[1][start + at : start + at + 1] for at, wt in enumerate(wts))
                    out_ref[kind, hel, direc, 0, plane : plane + 1, :] = -real if kind else real
                    out_ref[kind, hel, direc, 1, plane : plane + 1, :] = -imag


def shards(eigvecs, links, momenta, coef_num, coef_den, peram):
    n_space = lax.axis_size("space")
    n_op = lax.axis_size("op")
    n_tm = lax.axis_size("tm")
    _, _, n_b, _, planes, width = eigvecs.shape
    n_x = planes * n_space
    own = n_b // n_space
    n_h = coef_num.shape[0] // n_op
    my_op = lax.axis_index("op")
    my_space = lax.axis_index("space")

    nums = jnp.transpose(coef_num, (2, 1, 0))
    both = [(momenta, nums)]
    both += [(across(momenta, "op", mask), across(nums, "op", mask)) for mask in range(1, n_op)]

    group = n_space * n_op
    depth = n_b * SPINS // group
    first = (my_space * n_op + my_op) * depth
    piece = lax.dynamic_slice(
        peram.reshape(n_b, SPINS, 2, n_b), (first % n_b, first // n_b, 0, 0), (depth, 1, 2, n_b)
    ).reshape(depth * 2, n_b)

    moved = lax.optimization_barrier(jnp.transpose(eigvecs[0], (3, 0, 2, 1, 4)))
    own_piece = from_behind(piece, "tm", n_tm - 1)
    vecs = [moved[plane] for plane in range(planes)]
    upper = from_behind(vecs[0], "space", -1)

    smem = pl.BlockSpec(memory_space=pltpu.SMEM)
    vmem = pl.BlockSpec(memory_space=pltpu.VMEM)
    phi = pl.pallas_call(
        functools.partial(phase_kernel, n_op, n_x, planes),
        in_specs=[smem] * (2 * n_op + 1),
        out_specs=vmem,
        out_shape=jax.ShapeDtypeStruct((2, n_h, NDIR, 2, planes, width), jnp.float32),
        compiler_params=pltpu.CompilerParams(vmem_limit_bytes=4 * 2**20),
        name="phases",
    )(*[mom for mom, _ in both], *[num for _, num in both], coef_den)

    dims = [("op", 1 << bit) for bit in range(n_op.bit_length() - 1)]
    dims += [("space", 1 << bit) for bit in range(1, n_space.bit_length() - 1)]
    load = [0] * len(dims)

    def stage(held, size):
        for group_dims in itertools.combinations(range(len(dims)), size):
            dim = min(group_dims, key=lambda at: load[at])
            load[dim] += 1
            before = held[tuple(at for at in group_dims if at != dim)]
            held[group_dims] = across(before, *dims[dim])

    def hold(held, other):
        arrs, other = lax.optimization_barrier((list(held.values()), other))
        return dict(zip(held.keys(), arrs)), other

    link = links[0]
    last = planes - 1
    corner = tuple(range(len(dims)))
    partial = plane_call(last, (1, 2), vecs[last], None, link, phi)
    held, partial = hold({(): own_piece}, partial)
    stage(held, 1)
    if len(dims) > 2:
        far = diagonal(held[()], n_space, n_op)
    for plane in range(last):
        partial = plane_call(plane, (1, 2, 0), vecs[plane], vecs[plane + 1], link, phi, partial)
    keep, give = plane_call(last, (0,), vecs[last], upper, link, phi, partial, n_space)
    swapped = across(give, "space", 1)
    if len(dims) > 2:
        held[corner] = far
    early = list(held)
    held, keep = hold(held, keep)
    for size in range(2, len(dims) if len(dims) > 2 else 3):
        stage(held, size)
    late = [key for key in held if key not in early]
    flipped = [across(pack_call([held[key] for key in early]), "space", 1)]
    merged = merge_call(keep, swapped)
    got = [across(merged[mask], "space", 2 * mask) for mask in range(n_space // 2 - 1, 0, -1)]
    got.insert(0, merged[0])
    flipped.append(across(pack_call([held[key] for key in late]), "space", 1))
    tau = [held[key] for key in early + late] + flipped
    masks = []
    for flip in range(2):
        for group_dims in early + late:
            mask = {"space": flip, "op": 0}
            for at in group_dims:
                mask[dims[at][0]] ^= dims[at][1]
            masks.append((mask["space"], mask["op"]))

    lines = pl.pallas_call(
        functools.partial(quark_kernel, masks, n_op),
        in_specs=[vmem] * (1 + len(tau)),
        out_specs=vmem,
        out_shape=jax.ShapeDtypeStruct((n_h, SPINS, 2, own, n_b), jnp.float32),
        compiler_params=pltpu.CompilerParams(vmem_limit_bytes=VMEM_BYTES),
        cost_estimate=pl.CostEstimate(
            flops=2 * SPINS * n_h * 2 * own * 2 * n_b * n_b, bytes_accessed=7 * 2**20, transcendentals=0
        ),
        name="quark_products",
    )(left_call(got, n_h), *tau)
    return lines.reshape(1, n_h, 4, 4, 2, own, n_b)


def solution(mesh):
    return jax.shard_map(
        shards,
        mesh=mesh,
        in_specs=(
            P("tm", None, None, None, "space", None),
            P("tm", None, None, None, None, "space", None),
            P("op", None),
            P(None, "op", None),
            P(),
            P("tm", None, None, None, None, None),
        ),
        out_specs=P("tm", "op", None, None, None, "space", None),
        check_vma=False,
    )
```

```python
import functools
import itertools
import math

import jax
import jax.numpy as jnp
from jax import lax
from jax.experimental import pallas as pl
from jax.experimental.pallas import tpu as pltpu
from jax.sharding import PartitionSpec as P

LY = 32
LZ = 8
NDIR = 3
SPINS = 16
ROWS = 16
HALF = 128
BLOCK = 32
VMEM_BYTES = 20 * 2**20


def from_behind(value, axis, steps):
    count = lax.axis_size(axis)
    pairs = [(source, (source + steps) % count) for source in range(count)]
    return lax.ppermute(value, axis, pairs)


def across(value, axis, mask):
    pairs = [(source, source ^ mask) for source in range(lax.axis_size(axis))]
    return lax.ppermute(value, axis, pairs)


def diagonal(value, n_space, n_op):
    pairs = []
    for space in range(n_space):
        for oper in range(n_op):
            target = (space ^ (n_space - 2)) * n_op + (oper ^ (n_op - 1))
            pairs.append((space * n_op + oper, target))
    return lax.ppermute(value, ("space", "op"), pairs)


def dot_nt(left, right):
    return lax.dot_general(
        left, right, (((1,), (1,)), ((), ())), preferred_element_type=jnp.float32
    )


def shift_y(arr):
    return pltpu.roll(arr, arr.shape[1] - LZ, 1)


def shift_z(arr):
    width = arr.shape[1]
    lane = lax.broadcasted_iota(jnp.int32, arr.shape, 1)
    near = pltpu.roll(arr, width - 1, 1)
    far = pltpu.roll(arr, LZ - 1, 1)
    return jnp.where((lane & (LZ - 1)) == LZ - 1, far, near)


def weighted_links(u_ref, phi_ref, shifted, dirs, plane, n_h, store):
    width = u_ref.shape[-1]
    for half in range(width // HALF):
        lanes = pl.ds(half * HALF, HALF)
        for col in range(3):
            acc = {}
            for slot, direc in enumerate(dirs):
                f_r = None
                f_i = None
                for col_two in range(3):
                    u_r = u_ref[direc, col, col_two, 0, pl.ds(plane, 1), lanes]
                    u_i = u_ref[direc, col, col_two, 1, pl.ds(plane, 1), lanes]
                    v_r = shifted[slot, 0, col_two, :, lanes]
                    v_i = shifted[slot, 1, col_two, :, lanes]
                    term_r = u_r * v_r - u_i * v_i
                    term_i = u_r * v_i + u_i * v_r
                    f_r = term_r if f_r is None else f_r + term_r
                    f_i = term_i if f_i is None else f_i + term_i
                for kind in range(2):
                    for hel in range(n_h):
                        p_r = phi_ref[kind, hel, direc, 0, pl.ds(plane, 1), lanes]
                        p_i = phi_ref[kind, hel, direc, 1, pl.ds(plane, 1), lanes]
                        g_r = p_r * f_r - p_i * f_i
                        g_i = p_r * f_i + p_i * f_r
                        if (kind, hel) in acc:
                            old_r, old_i = acc[kind, hel]
                            g_r, g_i = old_r + g_r, old_i + g_i
                        acc[kind, hel] = (g_r, g_i)
            for (kind, hel), both in acc.items():
                store(kind, hel, col, half, both)


def plane_kernel(plane, dirs, has_part, n_out, *refs):
    refs = list(refs)
    v_ref = refs.pop(0)
    next_ref = refs.pop(0) if 0 in dirs else None
    u_ref, phi_ref = refs.pop(0), refs.pop(0)
    part_ref = refs.pop(0) if has_part else None
    keep_ref = refs.pop(0) if n_out else None
    give_ref = refs.pop(0) if n_out else None
    sum_ref, mat_ref, one_ref, two_ref, sh_ref = refs
    n_h = phi_ref.shape[1]
    _, _, n_b, width = v_ref.shape
    bufs = (one_ref, two_ref)
    last = n_b // BLOCK - 1

    for col in range(3):
        mat_ref[:, pl.ds(col * width, width)] = v_ref[:, col].reshape(2 * n_b, width)

    def fill(which, buf):
        for sub in range(BLOCK // ROWS):
            rows = pl.ds(pl.multiple_of(which * BLOCK + sub * ROWS, ROWS), ROWS)
            shifted = sh_ref.at[buf, sub]
            for slot, direc in enumerate(dirs):
                for part in range(2):
                    for col in range(3):
                        source = next_ref if direc == 0 else v_ref
                        field = source[part, col, rows, :].astype(jnp.float32)
                        if direc == 1:
                            field = shift_y(field)
                        elif direc == 2:
                            field = shift_z(field)
                        shifted[slot, part, col] = field

            def store(kind, hel, col, half, both, sub=sub):
                for part in range(2):
                    row = ((kind * n_h + hel) * 2 + part) * BLOCK + sub * ROWS
                    lanes = pl.ds(col * width + half * HALF, HALF)
                    bufs[buf][pl.ds(row, ROWS), lanes] = both[part].astype(jnp.bfloat16)

            weighted_links(u_ref, phi_ref, shifted, dirs, plane, n_h, store)

    def contract(which, buf):
        rows = pl.ds(pl.multiple_of(which * BLOCK, BLOCK), BLOCK)
        prod = dot_nt(bufs[buf][...], mat_ref[...])
        for kind in range(2):
            for hel in range(n_h):
                row = (kind * n_h + hel) * 2 * BLOCK
                re_row, im_row = prod[row : row + BLOCK], prod[row + BLOCK : row + 2 * BLOCK]
                real = re_row[:, :n_b] + im_row[:, n_b:]
                if kind:
                    imag = re_row[:, n_b:] - im_row[:, :n_b]
                else:
                    imag = im_row[:, :n_b] - re_row[:, n_b:]
                for part, total in enumerate((real, imag)):
                    if has_part:
                        total = total + part_ref[kind, hel, part, rows, :]
                    sum_ref[kind, hel, part, rows, :] = total

    fill(0, 0)

    def pair(step, carry):
        fill(2 * step + 1, 1)
        contract(2 * step, 0)
        fill(2 * step + 2, 0)
        contract(2 * step + 1, 1)
        return carry

    lax.fori_loop(0, last // 2, pair, 0)
    fill(last, 1)
    contract(last - 1, 0)
    contract(last, 1)

    if n_out:
        core = lax.axis_index("space") & 1
        for hel in range(n_h):
            for part in range(2):
                total = jnp.transpose(sum_ref[0, hel, part]) + sum_ref[1, hel, part]
                halves = total.reshape(n_out // 2, 2, n_b // n_out, n_b)
                keep_ref[:, hel, part] = jnp.where(core == 0, halves[:, 0], halves[:, 1])
                give = jnp.where(core == 0, halves[:, 1], halves[:, 0])
                give_ref[:, hel, part] = give.astype(jnp.bfloat16)


def plane_call(plane, dirs, vec, ahead, link, phi, part=None, n_out=0):
    n_h = phi.shape[1]
    _, _, n_b, width = vec.shape
    vmem = pl.BlockSpec(memory_space=pltpu.VMEM)
    args = [vec] + ([ahead] if 0 in dirs else []) + [link, phi]
    args += [part] if part is not None else []
    specs = [vmem] * len(args)
    sums = (2, n_h, 2, n_b, n_b)
    scratch = [
        pltpu.VMEM((2 * n_b, 3 * width), jnp.bfloat16),
        pltpu.VMEM((4 * n_h * BLOCK, 3 * width), jnp.bfloat16),
        pltpu.VMEM((4 * n_h * BLOCK, 3 * width), jnp.bfloat16),
        pltpu.VMEM((2, BLOCK // ROWS, len(dirs), 2, 3, ROWS, width), jnp.float32),
    ]
    if n_out:
        scratch.insert(0, pltpu.VMEM(sums, jnp.float32))
        blocks = (n_out // 2, n_h, 2, n_b // n_out, n_b)
        out_shape = [
            jax.ShapeDtypeStruct(blocks, jnp.float32),
            jax.ShapeDtypeStruct(blocks, jnp.bfloat16),
        ]
        out_specs = [vmem, vmem]
    else:
        out_shape = jax.ShapeDtypeStruct(sums, jnp.float32)
        out_specs = vmem
    return pl.pallas_call(
        functools.partial(plane_kernel, plane, dirs, part is not None, n_out),
        in_specs=specs,
        out_specs=out_specs,
        out_shape=out_shape,
        scratch_shapes=scratch,
        compiler_params=pltpu.CompilerParams(vmem_limit_bytes=VMEM_BYTES),
        cost_estimate=pl.CostEstimate(
            flops=2**34,
            bytes_accessed=2**28,
            transcendentals=0,
        ),
        name="plane%d_%s" % (plane, "".join(str(direc) for direc in dirs)),
    )(*args)


def merge_kernel(keep_ref, got_ref, own_ref, *out_refs):
    chip = lax.axis_index("space") >> 1
    shape = own_ref.shape
    own_ref[...] = (keep_ref[chip] + got_ref[chip].astype(jnp.float32)).reshape(shape)
    for mask, out_ref in enumerate(out_refs, 1):
        total = keep_ref[chip ^ mask] + got_ref[chip ^ mask].astype(jnp.float32)
        out_ref[...] = total.reshape(shape).astype(jnp.bfloat16)


def merge_call(keep, got):
    chips, n_h, _, own, n_b = keep.shape
    shape = (n_h * 2 * own, n_b)
    vmem = pl.BlockSpec(memory_space=pltpu.VMEM)
    return pl.pallas_call(
        merge_kernel,
        in_specs=[vmem, vmem],
        out_specs=[vmem] * chips,
        out_shape=[jax.ShapeDtypeStruct(shape, jnp.float32)]
        + [jax.ShapeDtypeStruct(shape, jnp.bfloat16)] * (chips - 1),
        compiler_params=pltpu.CompilerParams(vmem_limit_bytes=8 * 2**20),
        cost_estimate=pl.CostEstimate(flops=2**16, bytes_accessed=2**12, transcendentals=0),
        name="merge_cores",
    )(keep, got)


def pack_kernel(*refs):
    for which, ref in enumerate(refs[:-1]):
        refs[-1][which] = ref[...]


def pack_call(arrs):
    vmem = pl.BlockSpec(memory_space=pltpu.VMEM)
    return pl.pallas_call(
        pack_kernel,
        in_specs=[vmem] * len(arrs),
        out_specs=vmem,
        out_shape=jax.ShapeDtypeStruct((len(arrs),) + arrs[0].shape, arrs[0].dtype),
        compiler_params=pltpu.CompilerParams(vmem_limit_bytes=8 * 2**20),
        cost_estimate=pl.CostEstimate(flops=2**16, bytes_accessed=2**12, transcendentals=0),
        name="pack_pieces",
    )(*arrs)


def left_kernel(n_h, *refs):
    got_refs, left_ref = refs[:-1], refs[-1]
    rows, n_b = got_refs[0].shape
    own = rows // (2 * n_h)
    row = lax.broadcasted_iota(jnp.int32, (n_b, 2 * n_b), 0)
    col = lax.broadcasted_iota(jnp.int32, (n_b, 2 * n_b), 1)
    even = (col == 2 * row).astype(jnp.bfloat16)
    odd = (col == 2 * row + 1).astype(jnp.bfloat16)
    total = got_refs[0][...]
    for ref in got_refs[1:]:
        total = total + ref[...].astype(jnp.float32)
    swap = []
    for hel in range(n_h):
        start = hel * 2 * own
        swap += [-total[start + own : start + 2 * own], total[start : start + own]]
    left = jnp.dot(total.astype(jnp.bfloat16), even, preferred_element_type=jnp.float32)
    left += jnp.dot(
        jnp.concatenate(swap, 0).astype(jnp.bfloat16), odd, preferred_element_type=jnp.float32
    )
    left_ref[...] = left.astype(jnp.bfloat16)


def left_call(got, n_h):
    rows, n_b = got[0].shape
    vmem = pl.BlockSpec(memory_space=pltpu.VMEM)
    return pl.pallas_call(
        functools.partial(left_kernel, n_h),
        in_specs=[vmem] * len(got),
        out_specs=vmem,
        out_shape=jax.ShapeDtypeStruct((rows, 2 * n_b), jnp.bfloat16),
        compiler_params=pltpu.CompilerParams(vmem_limit_bytes=8 * 2**20),
        cost_estimate=pl.CostEstimate(flops=2**34, bytes_accessed=2**24, transcendentals=0),
        name="left_operand",
    )(*got)


def quark_kernel(masks, n_op, left_ref, *refs):
    tau_refs, out_ref = refs[:-1], refs[-1]
    my_space, my_op = lax.axis_index("space"), lax.axis_index("op")
    n_h, n_pair, _, own, n_b = out_ref.shape
    tau = []
    for ref in tau_refs:
        tau += [ref.at[which] for which in range(ref.shape[0])] if len(ref.shape) == 3 else [ref]
    depth = tau[0].shape[0]
    whole = depth == 2 * n_b
    if not whole:
        out_ref[...] = jnp.zeros_like(out_ref)
    for which, (mask, mask_op) in enumerate(masks):
        first = ((my_space ^ mask) * n_op + (my_op ^ mask_op)) * depth
        pair = first // (2 * n_b)
        if whole:
            lhs = left_ref[...]
        else:
            lhs = left_ref[:, pl.ds(pl.multiple_of(first - pair * 2 * n_b, depth), depth)]
        res = jnp.dot(lhs, tau[which][...], preferred_element_type=jnp.float32)
        for hel in range(n_h):
            for part in range(2):
                start = (hel * 2 + part) * own
                if whole:
                    out_ref[hel, pair, part] = res[start : start + own]
                else:
                    out_ref[hel, pair, part] += res[start : start + own]


def phase_kernel(n_op, n_x, planes, *refs):
    mom_refs = refs[:n_op]
    num_refs = refs[n_op : 2 * n_op]
    den_ref, out_ref = refs[2 * n_op :]
    my_space, my_op = lax.axis_index("space"), lax.axis_index("op")
    _, n_h, _, _, _, width = out_ref.shape
    n_mom = mom_refs[0].shape[0]
    moms = [(op, k) for op in range(n_op) for k in range(n_mom)]
    scale = 1.0 / math.sqrt(3.0 * n_x * LY * LZ)
    shape = (planes * len(moms), width)
    row = lax.broadcasted_iota(jnp.int32, shape, 0)
    lane = lax.broadcasted_iota(jnp.int32, shape, 1)
    yy = lane // LZ
    zz = lane & (LZ - 1)

    def spread(values):
        res = jnp.full(shape, values[0], jnp.int32)
        for which in range(1, len(values)):
            res = jnp.where(row == which, values[which], res)
        return res

    comps = [[mom_refs[op][k, axis] for _ in range(planes) for op, k in moms] for axis in range(3)]
    mom_x, mom_y, mom_z = [spread(comp) for comp in comps]
    pos_x = my_space * planes + row // len(moms)
    steps = ((0, 0, 0), (1, 0, 0), (0, 1, 0), (0, 0, 1))
    waves = []
    for step_x, step_y, step_z in steps:
        turn_x = lax.rem(mom_x * (pos_x + step_x), n_x).astype(jnp.float32) * (1.0 / n_x)
        turn_y = ((mom_y * (yy + step_y)) & (LY - 1)).astype(jnp.float32) * (1.0 / LY)
        turn_z = ((mom_z * (zz + step_z)) & (LZ - 1)).astype(jnp.float32) * (1.0 / LZ)
        turn = turn_x + turn_y + turn_z
        theta = (2.0 * math.pi) * (turn - jnp.floor(turn))
        waves.append((jnp.cos(theta), jnp.sin(theta)))
    for hel in range(n_h):
        which_h = my_op * n_h + hel
        den = jnp.full((1, width), den_ref[which_h], jnp.int32).astype(jnp.float32)
        for direc in range(NDIR):
            wts = []
            for op, k in moms:
                num = num_refs[op][direc, k, which_h]
                wts.append(jnp.full((1, width), num, jnp.int32).astype(jnp.float32) / den * scale)
            for kind, wave in ((0, waves[0]), (1, waves[1 + direc])):
                for plane in range(planes):
                    start = plane * len(moms)
                    real = sum(wt * wave[0][start + at : start + at + 1] for at, wt in enumerate(wts))
                    imag = sum(wt * wave[1][start + at : start + at + 1] for at, wt in enumerate(wts))
                    out_ref[kind, hel, direc, 0, plane : plane + 1, :] = -real if kind else real
                    out_ref[kind, hel, direc, 1, plane : plane + 1, :] = -imag


def shards(eigvecs, links, momenta, coef_num, coef_den, peram):
    n_space = lax.axis_size("space")
    n_op = lax.axis_size("op")
    n_tm = lax.axis_size("tm")
    _, _, n_b, _, planes, width = eigvecs.shape
    n_x = planes * n_space
    own = n_b // n_space
    n_h = coef_num.shape[0] // n_op
    my_op = lax.axis_index("op")
    my_space = lax.axis_index("space")

    group = n_space * n_op
    depth = n_b * SPINS // group
    first = (my_space * n_op + my_op) * depth
    piece = lax.dynamic_slice(
        peram.reshape(n_b, SPINS, 2, n_b), (first % n_b, first // n_b, 0, 0), (depth, 1, 2, n_b)
    ).reshape(depth * 2, n_b)
    own_piece = from_behind(piece, "tm", n_tm - 1)

    momenta, coef_num, piece = lax.optimization_barrier((momenta, coef_num, piece))
    nums = jnp.transpose(coef_num, (2, 1, 0))
    both = [(momenta, nums)]
    both += [(across(momenta, "op", mask), across(nums, "op", mask)) for mask in range(1, n_op)]

    moved = lax.optimization_barrier(jnp.transpose(eigvecs[0], (3, 0, 2, 1, 4)))
    vecs = [moved[plane] for plane in range(planes)]
    upper = from_behind(vecs[0], "space", -1)

    smem = pl.BlockSpec(memory_space=pltpu.SMEM)
    vmem = pl.BlockSpec(memory_space=pltpu.VMEM)
    phi = pl.pallas_call(
        functools.partial(phase_kernel, n_op, n_x, planes),
        in_specs=[smem] * (2 * n_op + 1),
        out_specs=vmem,
        out_shape=jax.ShapeDtypeStruct((2, n_h, NDIR, 2, planes, width), jnp.float32),
        compiler_params=pltpu.CompilerParams(vmem_limit_bytes=4 * 2**20),
        name="phases",
    )(*[mom for mom, _ in both], *[num for _, num in both], coef_den)

    dims = [("op", 1 << bit) for bit in range(n_op.bit_length() - 1)]
    dims += [("space", 1 << bit) for bit in range(1, n_space.bit_length() - 1)]
    load = [0] * len(dims)

    def stage(held, size):
        for group_dims in itertools.combinations(range(len(dims)), size):
            dim = min(group_dims, key=lambda at: load[at])
            load[dim] += 1
            before = held[tuple(at for at in group_dims if at != dim)]
            held[group_dims] = across(before, *dims[dim])

    def hold(held, other):
        arrs, other = lax.optimization_barrier((list(held.values()), other))
        return dict(zip(held.keys(), arrs)), other

    link = links[0]
    last = planes - 1
    corner = tuple(range(len(dims)))
    partial = None
    for plane in range(last):
        partial = plane_call(plane, (1, 2, 0), vecs[plane], vecs[plane + 1], link, phi, partial)
    held, partial = hold({(): own_piece}, partial)
    stage(held, 1)
    if len(dims) > 2:
        far = diagonal(held[()], n_space, n_op)
    partial = plane_call(last, (1, 2), vecs[last], None, link, phi, partial)
    keep, give = plane_call(last, (0,), vecs[last], upper, link, phi, partial, n_space)
    swapped = across(give, "space", 1)
    if len(dims) > 2:
        held[corner] = far
    early = list(held)
    held, keep = hold(held, keep)
    for size in range(2, len(dims) if len(dims) > 2 else 3):
        stage(held, size)
    late = [key for key in held if key not in early]
    flipped = [across(pack_call([held[key] for key in early]), "space", 1)]
    merged = merge_call(keep, swapped)
    got = [across(merged[mask], "space", 2 * mask) for mask in range(n_space // 2 - 1, 0, -1)]
    got.insert(0, merged[0])
    flipped.append(across(pack_call([held[key] for key in late]), "space", 1))
    tau = [held[key] for key in early + late] + flipped
    masks = []
    for flip in range(2):
        for group_dims in early + late:
            mask = {"space": flip, "op": 0}
            for at in group_dims:
                mask[dims[at][0]] ^= dims[at][1]
            masks.append((mask["space"], mask["op"]))

    lines = pl.pallas_call(
        functools.partial(quark_kernel, masks, n_op),
        in_specs=[vmem] * (1 + len(tau)),
        out_specs=vmem,
        out_shape=jax.ShapeDtypeStruct((n_h, SPINS, 2, own, n_b), jnp.float32),
        compiler_params=pltpu.CompilerParams(vmem_limit_bytes=VMEM_BYTES),
        cost_estimate=pl.CostEstimate(
            flops=2 * SPINS * n_h * 2 * own * 2 * n_b * n_b, bytes_accessed=7 * 2**20, transcendentals=0
        ),
        name="quark_products",
    )(left_call(got, n_h), *tau)
    return lines.reshape(1, n_h, 4, 4, 2, own, n_b)


def solution(mesh):
    return jax.shard_map(
        shards,
        mesh=mesh,
        in_specs=(
            P("tm", None, None, None, "space", None),
            P("tm", None, None, None, None, "space", None),
            P("op", None),
            P(None, "op", None),
            P(),
            P("tm", None, None, None, None, None),
        ),
        out_specs=P("tm", "op", None, None, None, "space", None),
        check_vma=False,
    )
```
